512 devices in a mesh: tm: 32 (over x, y), rows: 16 (over z, core).
Axes of the slice: x: 4, y: 8, z: 8, core: 2. Of those that a mesh axis runs over, the one named last changes fastest.
Arguments:
- frames: bfloat16 [32, 128, 128, 128], P('tm', 'rows'), may hold values from -6 to 6
- kernel: bfloat16 [3, 3, 3, 128, 128], replicated, may hold values from -0.109375 to 0.109375
- cotangent: bfloat16 [32, 128, 128, 128], P('tm', 'rows'), may hold values from -6 to 6
Outputs:
- code: bfloat16 [32, 128, 128, 128], P('tm', 'rows')
- grad_frames: bfloat16 [32, 128, 128, 128], P('tm', 'rows')
- grad_kernel: float32 [3, 3, 3, 128, 128], replicated
The draws below stay inside these ranges and needn't reach their ends.
All inputs are finite; a program needn't handle non-finite values.
Results may differ from the reference program's by a relative error of at most 0.013.
Values may be sent and summed in bfloat16 or wider, within the bound.
No kernel may reach another device: no remote copies, remote signals or barrier semaphores. Data moves between devices by JAX's collectives and lax.ppermute only.
A program may use at most 64 MiB of HBM per device.

```python
import math
import jax
import jax.numpy as jnp
from jax import lax

C = 128
WCOL = 128
LEVELS = 3
NF = 32
NH = 128


def block_scale(key, shape, shards, low, high):
    factor_of, own = 1.0, jax.random.fold_in(key, 6)
    for axis_at, shards_of in shards:
        steps = jnp.exp(jax.random.uniform(jax.random.fold_in(own, axis_at), (shards_of,), jnp.float32, low / len(shards), high / len(shards)))
        factor_of = factor_of * jnp.repeat(steps, shape[axis_at] // shards_of).reshape([-1 if axis == axis_at else 1 for axis in range(len(shape))])
    return factor_of


def gaussian(stream_key, dims, scale, most, split=(), kind=jnp.bfloat16):
    level = block_scale(stream_key, dims, split, -0.22, 0.18) if split else 1.0
    values = jax.random.normal(stream_key, dims, jnp.float32) * scale * level
    return jnp.minimum(jnp.maximum(values, -most), most).astype(kind)


def setup_inputs(seed: int = 0) -> dict:
    arg_keys = jax.random.split(jax.random.key(seed), 4)
    return {
        "frames": gaussian(arg_keys[0], (NF, NH, WCOL, C), 1.0, 6.0, ((0, 32), (1, 16))),
        "kernel": gaussian(arg_keys[1], (3, 3, 3, C, C), (27 * C) ** -0.5, 0.109375),
        "cotangent": gaussian(arg_keys[2], (NF, NH, WCOL, C), 1.0, 6.0, ((0, 32), (1, 16))),
    }


band_weight = 0.75
root_half = 0.7071067811865476

def tap_offsets(tap_id):
    tap_id = tap_id.astype(jnp.int32)
    return (tap_id // 9, tap_id // 3 % 3, tap_id % 3)

def forward_conv(frames, kernel):
    padded = jnp.pad(frames.astype(jnp.float32), ((2, 0), (1, 1), (1, 1), (0, 0)))
    kernel_flat = kernel.astype(jnp.float32).reshape(27, C, C)
    anchor = jnp.int32(0)

    def add_tap(tap_id, running):
        frame_tap, row_tap, col_tap = tap_offsets(tap_id)
        window = lax.dynamic_slice(padded, (frame_tap, row_tap, col_tap, anchor), (NF, NH, WCOL, C))
        return running + jnp.einsum('fhwc,cd->fhwd', window, kernel_flat[tap_id], precision=lax.Precision.HIGHEST)
    return lax.fori_loop(0, 27, add_tap, jnp.zeros((NF, NH, WCOL, C), jnp.float32))

def transpose_conv(grads, kernel):
    padded = jnp.pad(grads.astype(jnp.float32), ((0, 2), (1, 1), (1, 1), (0, 0)))
    kernel_flat = kernel.astype(jnp.float32).reshape(27, C, C)
    anchor = jnp.int32(0)

    def add_tap(tap_id, running):
        frame_tap, row_tap, col_tap = tap_offsets(tap_id)
        window = lax.dynamic_slice(padded, (2 - frame_tap, 2 - row_tap, 2 - col_tap, anchor), (NF, NH, WCOL, C))
        return running + jnp.einsum('fhwd,cd->fhwc', window, kernel_flat[tap_id], precision=lax.Precision.HIGHEST)
    return lax.fori_loop(0, 27, add_tap, jnp.zeros((NF, NH, WCOL, C), jnp.float32))

def weight_grads(frames, grads):
    padded = jnp.pad(frames.astype(jnp.float32), ((2, 0), (1, 1), (1, 1), (0, 0)))
    grads_wide = grads.astype(jnp.float32)
    anchor = jnp.int32(0)

    def one_tap(tap_id):
        frame_tap, row_tap, col_tap = tap_offsets(tap_id)
        window = lax.dynamic_slice(padded, (frame_tap, row_tap, col_tap, anchor), (NF, NH, WCOL, C))
        return jnp.einsum('fhwc,fhwd->cd', window, grads_wide, precision=lax.Precision.HIGHEST)
    return lax.map(one_tap, jnp.arange(27, dtype=jnp.int32)).reshape(3, 3, 3, C, C)

def partner(values, degree):
    stride_len = 2 ** degree
    grouped = values.reshape((NF // (2 * stride_len), 2, stride_len) + values.shape[1:])
    return grouped[:, ::-1].reshape(values.shape)

def side_sign(degree):
    frame_ids = jnp.arange(NF, dtype=jnp.int32)
    upper_bit = frame_ids // 2 ** degree % 2
    return (2 * upper_bit - 1).astype(jnp.float32).reshape(NF, 1, 1, 1)

def reference(frames, kernel, cotangent):
    linear = forward_conv(frames, kernel)
    gate_value = jax.nn.sigmoid(linear)
    active = (linear * gate_value).astype(jnp.bfloat16)
    coarse = active
    detail = jnp.zeros(linear.shape, jnp.float32)
    for degree in range(LEVELS):
        current = coarse.astype(jnp.float32)
        remote = partner(coarse, degree).astype(jnp.float32)
        smooth = (current + remote) * root_half
        detail = detail + side_sign(degree) * (current - remote) * root_half
        coarse = smooth.astype(jnp.bfloat16) if degree < LEVELS - 1 else smooth
    code = (coarse + band_weight * detail).astype(jnp.bfloat16)
    upstream = cotangent.astype(jnp.float32)
    top_level = LEVELS - 1
    pair_sum = upstream + partner(cotangent, top_level).astype(jnp.float32)
    carried = (pair_sum * root_half + band_weight * side_sign(top_level) * (pair_sum * root_half)).astype(jnp.bfloat16)
    for degree in range(LEVELS - 2, -1, -1):
        returned = carried.astype(jnp.float32)
        peer_back = partner(carried, degree).astype(jnp.float32)
        peer_flow = partner(cotangent, degree).astype(jnp.float32)
        summed = (returned + peer_back) * root_half + band_weight * side_sign(degree) * ((upstream + peer_flow) * root_half)
        carried = summed.astype(jnp.bfloat16) if degree > 0 else summed
    derivative = gate_value * (1.0 + linear * (1.0 - gate_value))
    grad_linear = (carried * derivative).astype(jnp.bfloat16)
    grad_frames = transpose_conv(grad_linear, kernel).astype(jnp.bfloat16)
    norm_factor = 1.0 / math.sqrt(NF * NH * WCOL)
    grad_kernel = weight_grads(frames, grad_linear) * norm_factor
    return (code, grad_frames, grad_kernel)
```

```python
import functools
import math

import jax
import jax.numpy as jnp
from jax import lax
from jax.experimental import pallas as pl
from jax.experimental.pallas import tpu as pltpu
from jax.sharding import Mesh
from jax.sharding import PartitionSpec as P

CHIPS = (4, 8, 8, 2)
LEVELS = 3
GROUP = 1 << LEVELS
ROWS = 8
STRIP = 16
TILE = ROWS * STRIP
TALL = ROWS + 2
HELD = TALL * STRIP + 2 * STRIP
CH = 128
WIDE = 9 * CH
FRAMES = GROUP + 2
EDGES = 2 * ROWS
PART = 8

band_weight = 0.75
root_half = 0.7071067811865476
f32 = jnp.float32
bf16 = jnp.bfloat16
VMEM_LIMIT = 48 * 1024 * 1024


def kernel_call(body, outs, scratch=(), flops=0):
    return pl.pallas_call(
        body,
        out_shape=outs,
        scratch_shapes=list(scratch),
        compiler_params=pltpu.CompilerParams(vmem_limit_bytes=VMEM_LIMIT),
        cost_estimate=pl.CostEstimate(flops=flops, bytes_accessed=4 << 20, transcendentals=0),
    )


def pack_body(x_ref, up_ref, down_ref, cot_ref, out_ref, left_ref, right_ref):
    left_ref[...] = jnp.zeros_like(left_ref)
    right_ref[...] = jnp.zeros_like(right_ref)
    for tall_row in range(TALL):
        if tall_row == 0:
            line = up_ref[0]
        elif tall_row == TALL - 1:
            line = down_ref[0]
        else:
            line = x_ref[tall_row - 1]
        wide = line.astype(f32)
        for strip in range(GROUP):
            low = strip * STRIP
            out_ref[strip, pl.ds(tall_row * STRIP, STRIP), :] = line[low : low + STRIP]
            if strip > 0:
                left_ref[strip, pl.ds(tall_row, 1), :] = wide[low - 1 : low]
            if strip < GROUP - 1:
                right_ref[strip, pl.ds(tall_row, 1), :] = wide[low + STRIP : low + STRIP + 1]
    for strip in range(GROUP):
        out_ref[strip, pl.ds(TALL * STRIP, STRIP), :] = left_ref[strip].astype(bf16)
        out_ref[strip, pl.ds(TALL * STRIP + STRIP, STRIP), :] = right_ref[strip].astype(bf16)
        for row in range(ROWS):
            out_ref[strip, pl.ds(HELD + row * STRIP, STRIP), :] = cot_ref[
                row, pl.ds(strip * STRIP, STRIP), :
            ]


def place_line(col_ref, base, tall_row, line, left, right):
    at = lax.broadcasted_iota(jnp.int32, (STRIP, CH), 0)
    wide = line.astype(f32)
    before = jnp.where(at == 0, left, pltpu.roll(wide, 1, 0)).astype(bf16)
    after = jnp.where(at == STRIP - 1, right, pltpu.roll(wide, STRIP - 1, 0)).astype(bf16)
    for row_tap in range(3):
        row = tall_row - row_tap
        if 0 <= row < ROWS:
            start = pl.multiple_of(base + row * STRIP, STRIP)
            for col_tap, piece in enumerate((before, line, after)):
                tap = row_tap * 3 + col_tap
                col_ref[pl.ds(start, STRIP), pl.ds(tap * CH, CH)] = piece


def forward_body(held_ref, early_ref, w_ref, code_ref, g_ref, dw_ref, col_ref, lin_ref, gt_ref):
    def spread(ref, frame, place):
        left = ref[frame, pl.ds(TALL * STRIP, STRIP), :].astype(f32)
        right = ref[frame, pl.ds(TALL * STRIP + STRIP, STRIP), :].astype(f32)
        for tall_row in range(TALL):
            line = ref[frame, pl.ds(tall_row * STRIP, STRIP), :]
            place_line(
                col_ref,
                place * TILE,
                tall_row,
                line,
                left[tall_row : tall_row + 1],
                right[tall_row : tall_row + 1],
            )

    @pl.loop(0, 2)
    def _(frame):
        spread(early_ref, frame, frame)

    @pl.loop(0, GROUP)
    def _(frame):
        spread(held_ref, frame, frame + 2)

    lin_ref[...] = (
        jnp.dot(col_ref[0 : GROUP * TILE, :], w_ref[0], preferred_element_type=f32)
        + jnp.dot(col_ref[TILE : (GROUP + 1) * TILE, :], w_ref[1], preferred_element_type=f32)
        + jnp.dot(col_ref[2 * TILE : (GROUP + 2) * TILE, :], w_ref[2], preferred_element_type=f32)
    )

    @pl.loop(0, ROWS)
    def _(row):
        low = pl.multiple_of(row * STRIP, STRIP)
        linear = [lin_ref[pl.ds(frame * TILE + low, STRIP), :] for frame in range(GROUP)]
        gate = [jax.nn.sigmoid(value) for value in linear]
        band = [(value * part).astype(bf16).astype(f32) for value, part in zip(linear, gate)]
        detail = [None] * GROUP
        for level in range(LEVELS):
            step = 1 << level
            following = [None] * GROUP
            for frame in range(0, GROUP, 2 * step):
                lower, upper = band[frame], band[frame + step]
                smooth = (lower + upper) * root_half
                if level < LEVELS - 1:
                    smooth = smooth.astype(bf16).astype(f32)
                change = (upper - lower) * root_half
                following[frame] = smooth
                for member in range(frame, frame + 2 * step, 2):
                    detail[member] = change if level == 0 else detail[member] + change
            band = following
        for member in range(0, GROUP, 2):
            code = (band[0] + band_weight * detail[member]).astype(bf16)
            code_ref[member, pl.ds(low, STRIP), :] = code
            code_ref[member + 1, pl.ds(low, STRIP), :] = code

        cot = [
            held_ref[frame, pl.ds(HELD + low, STRIP), :].astype(f32) for frame in range(GROUP)
        ]
        back = [None] * GROUP
        for level in range(LEVELS - 1, -1, -1):
            step = 1 << level
            following = [None] * GROUP
            for frame in range(GROUP):
                if frame & step:
                    continue
                pair = (cot[frame] + cot[frame + step]) * root_half
                if level == LEVELS - 1:
                    total = pair
                else:
                    total = (back[frame] + back[frame + step]) * root_half
                for member, side in ((frame, -1.0), (frame + step, 1.0)):
                    value = total + (band_weight * side) * pair
                    if level > 0:
                        value = value.astype(bf16).astype(f32)
                    following[member] = value
            back = following
        for frame in range(GROUP):
            slope = gate[frame] * (1.0 + linear[frame] * (1.0 - gate[frame]))
            g_ref[frame, pl.ds(low, STRIP), :] = (back[frame] * slope).astype(bf16)

    gt_ref[...] = jnp.zeros_like(gt_ref)
    for frame in range(GROUP):
        turned = g_ref[frame].astype(f32).T.astype(bf16)
        for tap in range(3):
            gt_ref[pl.ds(tap * CH, CH), pl.ds((frame + tap) * TILE, TILE)] = turned
    for tap in range(9):
        product = jnp.dot(
            gt_ref[...], col_ref[:, tap * CH : (tap + 1) * CH], preferred_element_type=f32
        )
        for frame_tap in range(3):
            block = product[frame_tap * CH : (frame_tap + 1) * CH]
            dw_ref[frame_tap * 9 + tap] = block.T.astype(bf16)


def backward_body(g_ref, up_ref, down_ref, late_ref, code_ref, w_ref, out_ref, col_ref, side_ref):
    nothing = jnp.zeros((1, CH), f32)

    def spread(lines, place):
        for tall_row, line in enumerate(lines):
            place_line(col_ref, place * TILE, tall_row, line, nothing, nothing)

    @pl.loop(0, GROUP)
    def _(frame):
        rows = [g_ref[frame, pl.ds(row * STRIP, STRIP), :] for row in range(ROWS)]
        spread([up_ref[frame]] + rows + [down_ref[frame]], frame)

    @pl.loop(0, 2)
    def _(frame):
        lines = [late_ref[frame, pl.ds(row * STRIP, STRIP), :] for row in range(TALL)]
        spread(lines, frame + GROUP)

    total = (
        jnp.dot(col_ref[0 : GROUP * TILE, :], w_ref[0], preferred_element_type=f32)
        + jnp.dot(col_ref[TILE : (GROUP + 1) * TILE, :], w_ref[1], preferred_element_type=f32)
        + jnp.dot(col_ref[2 * TILE : (GROUP + 2) * TILE, :], w_ref[2], preferred_element_type=f32)
    )
    for frame in range(GROUP):
        out_ref[frame, 0:TILE, :] = code_ref[frame]
        out_ref[frame, TILE : 2 * TILE, :] = total[frame * TILE : (frame + 1) * TILE].astype(bf16)
    for side, (offset, col_tap) in enumerate(((0, 2), (STRIP - 1, 0))):
        for frame in range(FRAMES):
            for row in range(ROWS):
                at = frame * TILE + row * STRIP + (0 if side == 0 else STRIP - 8)
                for row_tap in range(3):
                    mid = (row_tap * 3 + 1) * CH
                    piece = col_ref[pl.ds(frame * TILE + row * STRIP, STRIP), pl.ds(mid, CH)]
                    one = piece.astype(f32)[offset : offset + 1]
                    side_ref[pl.ds(frame * ROWS + row, 1), pl.ds(row_tap * CH, CH)] = one
        summed = None
        for frame_tap in range(3):
            rows = side_ref[pl.ds(frame_tap * ROWS, GROUP * ROWS), :].astype(bf16)
            for row_tap in range(3):
                tap = row_tap * 3 + col_tap
                part = jnp.dot(
                    rows[:, row_tap * CH : (row_tap + 1) * CH],
                    w_ref[frame_tap, pl.ds(tap * CH, CH), :],
                    preferred_element_type=f32,
                )
                summed = part if summed is None else summed + part
        if side == 0:
            first = summed
    for frame in range(GROUP):
        pair = [value[frame * ROWS : (frame + 1) * ROWS] for value in (first, summed)]
        out_ref[frame, 2 * TILE : 2 * TILE + EDGES, :] = jnp.concatenate(pair, axis=0).astype(bf16)


def unpack_body(got_ref, code_ref, grad_ref):
    at = lax.broadcasted_iota(jnp.int32, (STRIP, CH), 0)
    for strip in range(GROUP):
        columns = pl.ds(strip * STRIP, STRIP)
        if strip > 0:
            before = got_ref[strip - 1, pl.ds(2 * TILE, EDGES), :].astype(f32)
        if strip < GROUP - 1:
            after = got_ref[strip + 1, pl.ds(2 * TILE, EDGES), :].astype(f32)
        for row in range(ROWS):
            code_ref[row, columns, :] = got_ref[strip, pl.ds(row * STRIP, STRIP), :]
            value = got_ref[strip, pl.ds(TILE + row * STRIP, STRIP), :].astype(f32)
            if strip > 0:
                value = value + jnp.where(at == 0, before[ROWS + row : ROWS + row + 1], 0.0)
            if strip < GROUP - 1:
                value = value + jnp.where(at == STRIP - 1, after[row : row + 1], 0.0)
            grad_ref[row, columns, :] = value.astype(bf16)


def shifted(value, axes, by):
    count = lax.axis_size(axes)
    route = [(i, i + by) for i in range(count) if 0 <= i + by < count]
    return lax.ppermute(value, axes, route)


def swapped(value):
    return lax.ppermute(value, "core", [(0, 1), (1, 0)])


def summed_everywhere(terms, norm):
    chips = ("x", "y", "z")
    count = lax.axis_size(chips)
    core = lax.axis_index("core")
    rows = terms.shape[0] // 2
    halves = terms.reshape(2, rows, CH)
    mine = lax.dynamic_index_in_dim(halves, core, 0, keepdims=False)
    other = lax.dynamic_index_in_dim(halves, 1 - core, 0, keepdims=False)
    chip_sum = (mine.astype(f32) + swapped(other).astype(f32)).astype(bf16)
    share = PART * -(-rows // (PART * count))
    padded = jnp.pad(chip_sum, ((0, share * count - rows), (0, 0)))
    spread = lax.all_to_all(padded.reshape(count, share, CH), chips, 0, 0)
    total = (spread.astype(f32).sum(axis=0) * norm).astype(bf16)
    copies = jnp.broadcast_to(total[None], (count, share, CH))
    half = lax.all_to_all(copies, chips, 0, 0).reshape(count * share, CH)[:rows]
    paired = swapped(half)
    low = jnp.where(core == 0, half, paired)
    high = jnp.where(core == 0, paired, half)
    return jnp.concatenate([low, high], axis=0).astype(f32)


def shards(frames, kernel, cotangent):
    x = frames[0]
    weights = kernel.reshape(3, WIDE, CH)
    turned = jnp.swapaxes(kernel[::-1, ::-1, ::-1], 3, 4).reshape(3, WIDE, CH)
    lines = ("z", "core")
    up = shifted(x[ROWS - 1 : ROWS], lines, 1)
    down = shifted(x[0:1], lines, -1)
    packed = kernel_call(
        pack_body,
        jax.ShapeDtypeStruct((GROUP, HELD + TILE, CH), bf16),
        [pltpu.VMEM((GROUP, STRIP, CH), f32)] * 2,
    )(x, up, down, cotangent[0])
    held = lax.all_to_all(packed, "y", 0, 0)
    early = shifted(held[GROUP - 2 :, :HELD], "x", 1)

    flops = 2 * GROUP * TILE * 27 * CH * CH
    code, g, terms = kernel_call(
        forward_body,
        (
            jax.ShapeDtypeStruct((GROUP, TILE, CH), bf16),
            jax.ShapeDtypeStruct((GROUP, TILE, CH), bf16),
            jax.ShapeDtypeStruct((27, CH, CH), bf16),
        ),
        [
            pltpu.VMEM((FRAMES * TILE, WIDE), bf16),
            pltpu.VMEM((GROUP * TILE, CH), f32),
            pltpu.VMEM((3 * CH, FRAMES * TILE), bf16),
        ],
        flops=2 * flops,
    )(held, early, weights)

    norm = 1.0 / math.sqrt(lax.axis_size(("x", "y", "z", "core")) * GROUP * TILE)
    grad_kernel = summed_everywhere(terms.reshape(27 * CH, CH), norm)

    g_up = shifted(g[:, TILE - STRIP :], lines, 1)
    g_down = shifted(g[:, :STRIP], lines, -1)
    late = shifted(jnp.concatenate([g_up[:2], g[:2], g_down[:2]], axis=1), "x", -1)
    sent = kernel_call(
        backward_body,
        jax.ShapeDtypeStruct((GROUP, 2 * TILE + EDGES, CH), bf16),
        [
            pltpu.VMEM((FRAMES * TILE, WIDE), bf16),
            pltpu.VMEM((FRAMES * ROWS, 3 * CH), f32),
        ],
        flops=flops,
    )(g, g_up, g_down, late, code, turned)
    got = lax.all_to_all(sent, "y", 0, 0)
    whole = jax.ShapeDtypeStruct((ROWS, GROUP * STRIP, CH), bf16)
    code_out, grad_frames = kernel_call(unpack_body, (whole, whole))(got)
    return (code_out[None], grad_frames[None], grad_kernel.reshape(3, 3, 3, CH, CH))


def solution(mesh):
    split = Mesh(mesh.devices.reshape(CHIPS), ("x", "y", "z", "core"))
    block = P(("x", "y"), ("z", "core"), None, None)
    return jax.shard_map(
        shards,
        mesh=split,
        in_specs=(block, P(), block),
        out_specs=(block, block, P()),
        check_vma=False,
    )
```

```python
import functools
import math

import jax
import jax.numpy as jnp
from jax import lax
from jax.experimental import pallas as pl
from jax.experimental.pallas import tpu as pltpu
from jax.sharding import Mesh
from jax.sharding import PartitionSpec as P

CHIPS = (4, 8, 8, 2)
LEVELS = 3
GROUP = 1 << LEVELS
ROWS = 8
STRIP = 16
TILE = ROWS * STRIP
TALL = ROWS + 2
CH = 128
WIDE = 9 * CH
FRAMES = GROUP + 2
EDGES = 2 * ROWS
HELD = TILE + EDGES
PART = 8

band_weight = 0.75
root_half = 0.7071067811865476
f32 = jnp.float32
bf16 = jnp.bfloat16
VMEM_LIMIT = 48 * 1024 * 1024


def kernel_call(body, outs, scratch=(), flops=0):
    return pl.pallas_call(
        body,
        out_shape=outs,
        scratch_shapes=list(scratch),
        compiler_params=pltpu.CompilerParams(vmem_limit_bytes=VMEM_LIMIT),
        cost_estimate=pl.CostEstimate(flops=flops, bytes_accessed=4 << 20, transcendentals=0),
    )


def pack_body(x_hbm, cot_hbm, out_ref, cot_out_ref, x_ref, cot_ref, left_ref, right_ref, sems):
    x_copy = pltpu.make_async_copy(x_hbm, x_ref, sems.at[0])
    cot_copy = pltpu.make_async_copy(cot_hbm, cot_ref, sems.at[1])
    x_copy.start()
    cot_copy.start()
    left_ref[...] = jnp.zeros_like(left_ref)
    right_ref[...] = jnp.zeros_like(right_ref)
    x_copy.wait()
    for row in range(ROWS):
        line = x_ref[row]
        wide = line.astype(f32)
        for strip in range(GROUP):
            low = strip * STRIP
            out_ref[strip, pl.ds(row * STRIP, STRIP), :] = line[low : low + STRIP]
            if strip > 0:
                left_ref[strip, pl.ds(row, 1), :] = wide[low - 1 : low]
            if strip < GROUP - 1:
                right_ref[strip, pl.ds(row, 1), :] = wide[low + STRIP : low + STRIP + 1]
    for strip in range(GROUP):
        pair = jnp.concatenate([left_ref[strip], right_ref[strip]], axis=0)
        out_ref[strip, pl.ds(TILE, EDGES), :] = pair.astype(bf16)
    cot_copy.wait()
    for strip in range(GROUP):
        for row in range(ROWS):
            cot_out_ref[strip, pl.ds(row * STRIP, STRIP), :] = cot_ref[
                row, pl.ds(strip * STRIP, STRIP), :
            ]


def place_line(col_ref, base, tall_row, line, left, right):
    at = lax.broadcasted_iota(jnp.int32, (STRIP, CH), 0)
    wide = line.astype(f32)
    before = jnp.where(at == 0, left, pltpu.roll(wide, 1, 0)).astype(bf16)
    after = jnp.where(at == STRIP - 1, right, pltpu.roll(wide, STRIP - 1, 0)).astype(bf16)
    for row_tap in range(3):
        row = tall_row - row_tap
        if 0 <= row < ROWS:
            start = pl.multiple_of(base + row * STRIP, STRIP)
            for col_tap, piece in enumerate((before, line, after)):
                tap = row_tap * 3 + col_tap
                col_ref[pl.ds(start, STRIP), pl.ds(tap * CH, CH)] = piece


def forward_body(
    held_ref,
    early_ref,
    up_ref,
    down_ref,
    cot_ref,
    w_ref,
    code_ref,
    g_ref,
    dw_ref,
    col_ref,
    lin_ref,
    gt_ref,
):
    def spread(ref, frame, place):
        for tall_row in range(TALL):
            if tall_row == 0:
                source, at, low, row = up_ref, place, 0, ROWS - 1
            elif tall_row == TALL - 1:
                source, at, low, row = down_ref, place, 0, 0
            else:
                source, at, row = ref, frame, tall_row - 1
                low = row * STRIP
            line = source[at, pl.ds(low, STRIP), :]
            edge = source[at, pl.ds(source.shape[1] - EDGES, EDGES), :].astype(f32)
            place_line(
                col_ref,
                place * TILE,
                tall_row,
                line,
                edge[row : row + 1],
                edge[ROWS + row : ROWS + row + 1],
            )

    @pl.loop(0, 2)
    def _(frame):
        spread(early_ref, frame, frame)

    @pl.loop(0, GROUP)
    def _(frame):
        spread(held_ref, frame, frame + 2)

    lin_ref[...] = (
        jnp.dot(col_ref[0 : GROUP * TILE, :], w_ref[0], preferred_element_type=f32)
        + jnp.dot(col_ref[TILE : (GROUP + 1) * TILE, :], w_ref[1], preferred_element_type=f32)
        + jnp.dot(col_ref[2 * TILE : (GROUP + 2) * TILE, :], w_ref[2], preferred_element_type=f32)
    )

    @pl.loop(0, ROWS)
    def _(row):
        low = pl.multiple_of(row * STRIP, STRIP)
        linear = [lin_ref[pl.ds(frame * TILE + low, STRIP), :] for frame in range(GROUP)]
        gate = [jax.nn.sigmoid(value) for value in linear]
        band = [(value * part).astype(bf16).astype(f32) for value, part in zip(linear, gate)]
        detail = [None] * GROUP
        for level in range(LEVELS):
            step = 1 << level
            following = [None] * GROUP
            for frame in range(0, GROUP, 2 * step):
                lower, upper = band[frame], band[frame + step]
                smooth = (lower + upper) * root_half
                if level < LEVELS - 1:
                    smooth = smooth.astype(bf16).astype(f32)
                change = (upper - lower) * root_half
                following[frame] = smooth
                for member in range(frame, frame + 2 * step, 2):
                    detail[member] = change if level == 0 else detail[member] + change
            band = following
        for member in range(0, GROUP, 2):
            code = (band[0] + band_weight * detail[member]).astype(bf16)
            code_ref[member, pl.ds(low, STRIP), :] = code
            code_ref[member + 1, pl.ds(low, STRIP), :] = code

        cot = [cot_ref[frame, pl.ds(low, STRIP), :].astype(f32) for frame in range(GROUP)]
        back = [None] * GROUP
        for level in range(LEVELS - 1, -1, -1):
            step = 1 << level
            following = [None] * GROUP
            for frame in range(GROUP):
                if frame & step:
                    continue
                pair = (cot[frame] + cot[frame + step]) * root_half
                if level == LEVELS - 1:
                    total = pair
                else:
                    total = (back[frame] + back[frame + step]) * root_half
                for member, side in ((frame, -1.0), (frame + step, 1.0)):
                    value = total + (band_weight * side) * pair
                    if level > 0:
                        value = value.astype(bf16).astype(f32)
                    following[member] = value
            back = following
        for frame in range(GROUP):
            slope = gate[frame] * (1.0 + linear[frame] * (1.0 - gate[frame]))
            g_ref[frame, pl.ds(low, STRIP), :] = (back[frame] * slope).astype(bf16)

    gt_ref[...] = jnp.zeros_like(gt_ref)
    for frame in range(GROUP):
        turned = g_ref[frame].astype(f32).T.astype(bf16)
        for tap in range(3):
            gt_ref[pl.ds(tap * CH, CH), pl.ds((frame + tap) * TILE, TILE)] = turned
    for tap in range(9):
        product = jnp.dot(
            gt_ref[...], col_ref[:, tap * CH : (tap + 1) * CH], preferred_element_type=f32
        )
        for frame_tap in range(3):
            block = product[frame_tap * CH : (frame_tap + 1) * CH]
            dw_ref[frame_tap * 9 + tap] = block.T.astype(bf16)


def backward_body(g_ref, up_ref, down_ref, late_ref, code_ref, w_ref, out_ref, col_ref, side_ref):
    nothing = jnp.zeros((1, CH), f32)

    def spread(lines, place):
        for tall_row, line in enumerate(lines):
            place_line(col_ref, place * TILE, tall_row, line, nothing, nothing)

    @pl.loop(0, GROUP)
    def _(frame):
        rows = [g_ref[frame, pl.ds(row * STRIP, STRIP), :] for row in range(ROWS)]
        spread([up_ref[frame]] + rows + [down_ref[frame]], frame)

    @pl.loop(0, 2)
    def _(frame):
        lines = [late_ref[frame, pl.ds(row * STRIP, STRIP), :] for row in range(TALL)]
        spread(lines, frame + GROUP)

    total = (
        jnp.dot(col_ref[0 : GROUP * TILE, :], w_ref[0], preferred_element_type=f32)
        + jnp.dot(col_ref[TILE : (GROUP + 1) * TILE, :], w_ref[1], preferred_element_type=f32)
        + jnp.dot(col_ref[2 * TILE : (GROUP + 2) * TILE, :], w_ref[2], preferred_element_type=f32)
    )
    for frame in range(GROUP):
        out_ref[frame, 0:TILE, :] = code_ref[frame]
        out_ref[frame, TILE : 2 * TILE, :] = total[frame * TILE : (frame + 1) * TILE].astype(bf16)
    for side, (offset, col_tap) in enumerate(((0, 2), (STRIP - 1, 0))):
        for frame in range(FRAMES):
            for row in range(ROWS):
                at = frame * TILE + row * STRIP + (0 if side == 0 else STRIP - 8)
                for row_tap in range(3):
                    mid = (row_tap * 3 + 1) * CH
                    piece = col_ref[pl.ds(frame * TILE + row * STRIP, STRIP), pl.ds(mid, CH)]
                    one = piece.astype(f32)[offset : offset + 1]
                    side_ref[pl.ds(frame * ROWS + row, 1), pl.ds(row_tap * CH, CH)] = one
        summed = None
        for frame_tap in range(3):
            rows = side_ref[pl.ds(frame_tap * ROWS, GROUP * ROWS), :].astype(bf16)
            for row_tap in range(3):
                tap = row_tap * 3 + col_tap
                part = jnp.dot(
                    rows[:, row_tap * CH : (row_tap + 1) * CH],
                    w_ref[frame_tap, pl.ds(tap * CH, CH), :],
                    preferred_element_type=f32,
                )
                summed = part if summed is None else summed + part
        if side == 0:
            first = summed
    for frame in range(GROUP):
        pair = [value[frame * ROWS : (frame + 1) * ROWS] for value in (first, summed)]
        out_ref[frame, 2 * TILE : 2 * TILE + EDGES, :] = jnp.concatenate(pair, axis=0).astype(bf16)


def unpack_body(got_ref, code_ref, grad_ref):
    at = lax.broadcasted_iota(jnp.int32, (STRIP, CH), 0)
    for strip in range(GROUP):
        columns = pl.ds(strip * STRIP, STRIP)
        if strip > 0:
            before = got_ref[strip - 1, pl.ds(2 * TILE, EDGES), :].astype(f32)
        if strip < GROUP - 1:
            after = got_ref[strip + 1, pl.ds(2 * TILE, EDGES), :].astype(f32)
        for row in range(ROWS):
            code_ref[row, columns, :] = got_ref[strip, pl.ds(row * STRIP, STRIP), :]
            value = got_ref[strip, pl.ds(TILE + row * STRIP, STRIP), :].astype(f32)
            if strip > 0:
                value = value + jnp.where(at == 0, before[ROWS + row : ROWS + row + 1], 0.0)
            if strip < GROUP - 1:
                value = value + jnp.where(at == STRIP - 1, after[row : row + 1], 0.0)
            grad_ref[row, columns, :] = value.astype(bf16)


def shifted(value, axes, by):
    count = lax.axis_size(axes)
    route = [(i, i + by) for i in range(count) if 0 <= i + by < count]
    return lax.ppermute(value, axes, route)


def swapped(value):
    return lax.ppermute(value, "core", [(0, 1), (1, 0)])


def own_share(terms, norm):
    chips = ("x", "y", "z")
    count = lax.axis_size(chips)
    core = lax.axis_index("core")
    rows = terms.shape[0] // 2
    halves = terms.reshape(2, rows, CH)
    mine = lax.dynamic_index_in_dim(halves, core, 0, keepdims=False)
    other = lax.dynamic_index_in_dim(halves, 1 - core, 0, keepdims=False)
    chip_sum = (mine.astype(f32) + swapped(other).astype(f32)).astype(bf16)
    share = PART * -(-rows // (PART * count))
    padded = jnp.pad(chip_sum, ((0, share * count - rows), (0, 0)))
    spread = lax.all_to_all(padded.reshape(count, share, CH), chips, 0, 0)
    return (spread.astype(f32).sum(axis=0) * norm).astype(bf16), rows


def all_shares(total, rows):
    chips = ("x", "y", "z")
    core = lax.axis_index("core")
    copies = jnp.broadcast_to(total[None], (lax.axis_size(chips),) + total.shape)
    half = lax.all_to_all(copies, chips, 0, 0).reshape(-1, CH)[:rows]
    paired = swapped(half)
    low = jnp.where(core == 0, half, paired)
    high = jnp.where(core == 0, paired, half)
    return jnp.concatenate([low, high], axis=0).astype(f32)


def shards(frames, kernel, cotangent):
    x = frames[0]
    weights = kernel.reshape(3, WIDE, CH)
    turned = jnp.swapaxes(kernel[::-1, ::-1, ::-1], 3, 4).reshape(3, WIDE, CH)
    lines = ("z", "core")
    packed, cot_packed = pl.pallas_call(
        pack_body,
        out_shape=(
            jax.ShapeDtypeStruct((GROUP, HELD, CH), bf16),
            jax.ShapeDtypeStruct((GROUP, TILE, CH), bf16),
        ),
        in_specs=[pl.BlockSpec(memory_space=pl.ANY)] * 2,
        scratch_shapes=[
            pltpu.VMEM((ROWS, GROUP * STRIP, CH), bf16),
            pltpu.VMEM((ROWS, GROUP * STRIP, CH), bf16),
            pltpu.VMEM((GROUP, ROWS, CH), f32),
            pltpu.VMEM((GROUP, ROWS, CH), f32),
            pltpu.SemaphoreType.DMA((2,)),
        ],
        compiler_params=pltpu.CompilerParams(vmem_limit_bytes=VMEM_LIMIT),
    )(frames[0], cotangent[0])
    held = lax.all_to_all(packed, "y", 0, 0)
    cot = lax.all_to_all(cot_packed, "y", 0, 0)
    early = shifted(held[GROUP - 2 :], "x", 1)
    last, first = [
        jnp.concatenate([value[:, low : low + STRIP] for value in (early, held)], axis=0)
        for low in (TILE - STRIP, 0)
    ]
    edges = jnp.concatenate([early[:, TILE:], held[:, TILE:]], axis=0)
    up = shifted(jnp.concatenate([last, edges], axis=1), lines, 1)
    down = shifted(jnp.concatenate([first, edges], axis=1), lines, -1)

    flops = 2 * GROUP * TILE * 27 * CH * CH
    code, g, terms = kernel_call(
        forward_body,
        (
            jax.ShapeDtypeStruct((GROUP, TILE, CH), bf16),
            jax.ShapeDtypeStruct((GROUP, TILE, CH), bf16),
            jax.ShapeDtypeStruct((27, CH, CH), bf16),
        ),
        [
            pltpu.VMEM((FRAMES * TILE, WIDE), bf16),
            pltpu.VMEM((GROUP * TILE, CH), f32),
            pltpu.VMEM((3 * CH, FRAMES * TILE), bf16),
        ],
        flops=2 * flops,
    )(held, early, up, down, cot, weights)

    norm = 1.0 / math.sqrt(lax.axis_size(("x", "y", "z", "core")) * GROUP * TILE)
    total, half_rows = own_share(terms.reshape(27 * CH, CH), norm)

    g_up = shifted(g[:, TILE - STRIP :], lines, 1)
    g_down = shifted(g[:, :STRIP], lines, -1)
    late = shifted(jnp.concatenate([g_up[:2], g[:2], g_down[:2]], axis=1), "x", -1)
    sent = kernel_call(
        backward_body,
        jax.ShapeDtypeStruct((GROUP, 2 * TILE + EDGES, CH), bf16),
        [
            pltpu.VMEM((FRAMES * TILE, WIDE), bf16),
            pltpu.VMEM((FRAMES * ROWS, 3 * CH), f32),
        ],
        flops=flops,
    )(g, g_up, g_down, late, code, turned)
    total, sent = lax.optimization_barrier((total, sent))
    grad_kernel = all_shares(total, half_rows)
    got = lax.all_to_all(sent, "y", 0, 0)
    whole = jax.ShapeDtypeStruct((ROWS, GROUP * STRIP, CH), bf16)
    code_out, grad_frames = kernel_call(unpack_body, (whole, whole))(got)
    return (code_out[None], grad_frames[None], grad_kernel.reshape(3, 3, 3, CH, CH))


def solution(mesh):
    split = Mesh(mesh.devices.reshape(CHIPS), ("x", "y", "z", "core"))
    block = P(("x", "y"), ("z", "core"), None, None)
    return jax.shard_map(
        shards,
        mesh=split,
        in_specs=(block, P(), block),
        out_specs=(block, block, P()),
        check_vma=False,
    )
```

```python
import functools
import math

import jax
import jax.numpy as jnp
from jax import lax
from jax.experimental import pallas as pl
from jax.experimental.pallas import tpu as pltpu
from jax.sharding import Mesh
from jax.sharding import PartitionSpec as P

CHIPS = (4, 8, 8, 2)
LEVELS = 3
GROUP = 1 << LEVELS
ROWS = 8
STRIP = 16
TILE = ROWS * STRIP
TALL = ROWS + 2
CH = 128
WIDE = 9 * CH
FRAMES = GROUP + 2
EDGES = 2 * ROWS
HELD = TILE + EDGES
PART = 8

band_weight = 0.75
root_half = 0.7071067811865476
f32 = jnp.float32
bf16 = jnp.bfloat16
VMEM_LIMIT = 48 * 1024 * 1024


def kernel_call(body, outs, scratch=(), flops=0):
    return pl.pallas_call(
        body,
        out_shape=outs,
        scratch_shapes=list(scratch),
        compiler_params=pltpu.CompilerParams(vmem_limit_bytes=VMEM_LIMIT),
        cost_estimate=pl.CostEstimate(flops=flops, bytes_accessed=4 << 20, transcendentals=0),
    )


def pack_body(x_hbm, cot_hbm, out_ref, cot_out_ref, x_ref, cot_ref, left_ref, right_ref, sems):
    x_copy = pltpu.make_async_copy(x_hbm, x_ref, sems.at[0])
    cot_copy = pltpu.make_async_copy(cot_hbm, cot_ref, sems.at[1])
    x_copy.start()
    cot_copy.start()
    left_ref[...] = jnp.zeros_like(left_ref)
    right_ref[...] = jnp.zeros_like(right_ref)
    x_copy.wait()
    for row in range(ROWS):
        line = x_ref[row]
        wide = line.astype(f32)
        for strip in range(GROUP):
            low = strip * STRIP
            out_ref[strip, pl.ds(row * STRIP, STRIP), :] = line[low : low + STRIP]
            if strip > 0:
                left_ref[strip, pl.ds(row, 1), :] = wide[low - 1 : low]
            if strip < GROUP - 1:
                right_ref[strip, pl.ds(row, 1), :] = wide[low + STRIP : low + STRIP + 1]
    for strip in range(GROUP):
        pair = jnp.concatenate([left_ref[strip], right_ref[strip]], axis=0)
        out_ref[strip, pl.ds(TILE, EDGES), :] = pair.astype(bf16)
    cot_copy.wait()
    for strip in range(GROUP):
        for row in range(ROWS):
            cot_out_ref[strip, pl.ds(row * STRIP, STRIP), :] = cot_ref[
                row, pl.ds(strip * STRIP, STRIP), :
            ]


def place_line(col_ref, base, tall_row, line, left, right):
    at = lax.broadcasted_iota(jnp.int32, (STRIP, CH), 0)
    wide = line.astype(f32)
    before = jnp.where(at == 0, left, pltpu.roll(wide, 1, 0)).astype(bf16)
    after = jnp.where(at == STRIP - 1, right, pltpu.roll(wide, STRIP - 1, 0)).astype(bf16)
    for row_tap in range(3):
        row = tall_row - row_tap
        if 0 <= row < ROWS:
            start = pl.multiple_of(base + row * STRIP, STRIP)
            for col_tap, piece in enumerate((before, line, after)):
                tap = row_tap * 3 + col_tap
                col_ref[pl.ds(start, STRIP), pl.ds(tap * CH, CH)] = piece


def forward_body(
    held_ref,
    early_ref,
    up_ref,
    down_ref,
    cot_ref,
    w_ref,
    code_ref,
    g_ref,
    dw_ref,
    col_ref,
    lin_ref,
    gt_ref,
):
    def spread(ref, frame, place):
        for tall_row in range(TALL):
            if tall_row == 0:
                source, at, low, row = up_ref, place, 0, ROWS - 1
            elif tall_row == TALL - 1:
                source, at, low, row = down_ref, place, 0, 0
            else:
                source, at, row = ref, frame, tall_row - 1
                low = row * STRIP
            line = source[at, pl.ds(low, STRIP), :]
            edge = source[at, pl.ds(source.shape[1] - EDGES, EDGES), :].astype(f32)
            place_line(
                col_ref,
                place * TILE,
                tall_row,
                line,
                edge[row : row + 1],
                edge[ROWS + row : ROWS + row + 1],
            )

    @pl.loop(0, 2)
    def _(frame):
        spread(early_ref, frame, frame)

    @pl.loop(0, GROUP)
    def _(frame):
        spread(held_ref, frame, frame + 2)

    lin_ref[...] = (
        jnp.dot(col_ref[0 : GROUP * TILE, :], w_ref[0], preferred_element_type=f32)
        + jnp.dot(col_ref[TILE : (GROUP + 1) * TILE, :], w_ref[1], preferred_element_type=f32)
        + jnp.dot(col_ref[2 * TILE : (GROUP + 2) * TILE, :], w_ref[2], preferred_element_type=f32)
    )

    @pl.loop(0, ROWS)
    def _(row):
        low = pl.multiple_of(row * STRIP, STRIP)
        linear = [lin_ref[pl.ds(frame * TILE + low, STRIP), :] for frame in range(GROUP)]
        gate = [jax.nn.sigmoid(value) for value in linear]
        band = [(value * part).astype(bf16).astype(f32) for value, part in zip(linear, gate)]
        detail = [None] * GROUP
        for level in range(LEVELS):
            step = 1 << level
            following = [None] * GROUP
            for frame in range(0, GROUP, 2 * step):
                lower, upper = band[frame], band[frame + step]
                smooth = (lower + upper) * root_half
                if level < LEVELS - 1:
                    smooth = smooth.astype(bf16).astype(f32)
                change = (upper - lower) * root_half
                following[frame] = smooth
                for member in range(frame, frame + 2 * step, 2):
                    detail[member] = change if level == 0 else detail[member] + change
            band = following
        for member in range(0, GROUP, 2):
            code = (band[0] + band_weight * detail[member]).astype(bf16)
            code_ref[member, pl.ds(low, STRIP), :] = code
            code_ref[member + 1, pl.ds(low, STRIP), :] = code

        cot = [cot_ref[frame, pl.ds(low, STRIP), :].astype(f32) for frame in range(GROUP)]
        back = [None] * GROUP
        for level in range(LEVELS - 1, -1, -1):
            step = 1 << level
            following = [None] * GROUP
            for frame in range(GROUP):
                if frame & step:
                    continue
                pair = (cot[frame] + cot[frame + step]) * root_half
                if level == LEVELS - 1:
                    total = pair
                else:
                    total = (back[frame] + back[frame + step]) * root_half
                for member, side in ((frame, -1.0), (frame + step, 1.0)):
                    value = total + (band_weight * side) * pair
                    if level > 0:
                        value = value.astype(bf16).astype(f32)
                    following[member] = value
            back = following
        for frame in range(GROUP):
            slope = gate[frame] * (1.0 + linear[frame] * (1.0 - gate[frame]))
            g_ref[frame, pl.ds(low, STRIP), :] = (back[frame] * slope).astype(bf16)

    gt_ref[...] = jnp.zeros_like(gt_ref)
    for frame in range(GROUP):
        turned = g_ref[frame].astype(f32).T.astype(bf16)
        for tap in range(3):
            gt_ref[pl.ds(tap * CH, CH), pl.ds((frame + tap) * TILE, TILE)] = turned
    for tap in range(9):
        product = jnp.dot(
            gt_ref[...], col_ref[:, tap * CH : (tap + 1) * CH], preferred_element_type=f32
        )
        for frame_tap in range(3):
            block = product[frame_tap * CH : (frame_tap + 1) * CH]
            dw_ref[frame_tap * 9 + tap] = block.T.astype(bf16)


def backward_body(g_ref, up_ref, down_ref, late_ref, code_ref, w_ref, out_ref, col_ref, side_ref):
    nothing = jnp.zeros((1, CH), f32)

    def spread(lines, place):
        for tall_row, line in enumerate(lines):
            place_line(col_ref, place * TILE, tall_row, line, nothing, nothing)

    @pl.loop(0, GROUP)
    def _(frame):
        rows = [g_ref[frame, pl.ds(row * STRIP, STRIP), :] for row in range(ROWS)]
        spread([up_ref[frame]] + rows + [down_ref[frame]], frame)

    @pl.loop(0, 2)
    def _(frame):
        lines = [late_ref[frame, pl.ds(row * STRIP, STRIP), :] for row in range(TALL)]
        spread(lines, frame + GROUP)

    total = (
        jnp.dot(col_ref[0 : GROUP * TILE, :], w_ref[0], preferred_element_type=f32)
        + jnp.dot(col_ref[TILE : (GROUP + 1) * TILE, :], w_ref[1], preferred_element_type=f32)
        + jnp.dot(col_ref[2 * TILE : (GROUP + 2) * TILE, :], w_ref[2], preferred_element_type=f32)
    )
    for frame in range(GROUP):
        out_ref[frame, 0:TILE, :] = code_ref[frame]
        out_ref[frame, TILE : 2 * TILE, :] = total[frame * TILE : (frame + 1) * TILE].astype(bf16)
    for side, (offset, col_tap) in enumerate(((0, 2), (STRIP - 1, 0))):
        for frame in range(FRAMES):
            for row in range(ROWS):
                at = frame * TILE + row * STRIP + (0 if side == 0 else STRIP - 8)
                for row_tap in range(3):
                    mid = (row_tap * 3 + 1) * CH
                    piece = col_ref[pl.ds(frame * TILE + row * STRIP, STRIP), pl.ds(mid, CH)]
                    one = piece.astype(f32)[offset : offset + 1]
                    side_ref[pl.ds(frame * ROWS + row, 1), pl.ds(row_tap * CH, CH)] = one
        summed = None
        for frame_tap in range(3):
            rows = side_ref[pl.ds(frame_tap * ROWS, GROUP * ROWS), :].astype(bf16)
            for row_tap in range(3):
                tap = row_tap * 3 + col_tap
                part = jnp.dot(
                    rows[:, row_tap * CH : (row_tap + 1) * CH],
                    w_ref[frame_tap, pl.ds(tap * CH, CH), :],
                    preferred_element_type=f32,
                )
                summed = part if summed is None else summed + part
        if side == 0:
            first = summed
    for frame in range(GROUP):
        pair = [value[frame * ROWS : (frame + 1) * ROWS] for value in (first, summed)]
        out_ref[frame, 2 * TILE : 2 * TILE + EDGES, :] = jnp.concatenate(pair, axis=0).astype(bf16)


def unpack_body(got_ref, code_ref, grad_ref):
    at = lax.broadcasted_iota(jnp.int32, (STRIP, CH), 0)
    for strip in range(GROUP):
        columns = pl.ds(strip * STRIP, STRIP)
        if strip > 0:
            before = got_ref[strip - 1, pl.ds(2 * TILE, EDGES), :].astype(f32)
        if strip < GROUP - 1:
            after = got_ref[strip + 1, pl.ds(2 * TILE, EDGES), :].astype(f32)
        for row in range(ROWS):
            code_ref[row, columns, :] = got_ref[strip, pl.ds(row * STRIP, STRIP), :]
            value = got_ref[strip, pl.ds(TILE + row * STRIP, STRIP), :].astype(f32)
            if strip > 0:
                value = value + jnp.where(at == 0, before[ROWS + row : ROWS + row + 1], 0.0)
            if strip < GROUP - 1:
                value = value + jnp.where(at == STRIP - 1, after[row : row + 1], 0.0)
            grad_ref[row, columns, :] = value.astype(bf16)


def shifted(value, axes, by):
    count = lax.axis_size(axes)
    route = [(i, i + by) for i in range(count) if 0 <= i + by < count]
    return lax.ppermute(value, axes, route)


def swapped(value):
    return lax.ppermute(value, "core", [(0, 1), (1, 0)])


def order_body(x_ref, own_ref, one_ref, two_ref, three_ref, out_ref):
    for step, ref in enumerate((own_ref, one_ref, two_ref, three_ref)):
        out_ref[lax.rem(x_ref[0] + step, 4)] = ref[...]


def finish_body(core_ref, own_ref, other_ref, out_ref):
    core = core_ref[0]
    out_ref[core] = own_ref[...].astype(f32)
    out_ref[1 - core] = other_ref[...].astype(f32)


def indexed_call(body, out, index, *arrays):
    return pl.pallas_call(
        body,
        out_shape=out,
        in_specs=[pl.BlockSpec(memory_space=pltpu.SMEM)]
        + [pl.BlockSpec(memory_space=pltpu.VMEM)] * len(arrays),
        compiler_params=pltpu.CompilerParams(vmem_limit_bytes=VMEM_LIMIT),
    )(index.astype(jnp.int32).reshape(1), *arrays)


def own_share(terms, norm):
    core = lax.axis_index("core")
    wide, planes = lax.axis_size("x"), lax.axis_size(("y", "z"))
    rows = terms.shape[0] // 2
    halves = terms.reshape(2, rows, CH)
    mine = lax.dynamic_index_in_dim(halves, core, 0, keepdims=False)
    other = lax.dynamic_index_in_dim(halves, 1 - core, 0, keepdims=False)
    chip_sum = (mine.astype(f32) + swapped(other).astype(f32)).astype(bf16)
    parts = lax.all_to_all(chip_sum.reshape(wide, rows // wide, CH), "x", 0, 0)
    part = parts.astype(f32).sum(axis=0).astype(bf16)
    share = PART * -(-part.shape[0] // (PART * planes))
    padded = jnp.pad(part, ((0, share * planes - part.shape[0]), (0, 0)))
    spread = lax.all_to_all(padded.reshape(planes, share, CH), ("y", "z"), 0, 0)
    return (spread.astype(f32).sum(axis=0) * norm).astype(bf16), part.shape[0]


def all_shares(total, rows):
    wide, planes = lax.axis_size("x"), lax.axis_size(("y", "z"))
    copies = jnp.broadcast_to(total[None], (planes,) + total.shape)
    part = lax.all_to_all(copies, ("y", "z"), 0, 0).reshape(-1, CH)[:rows]
    others = [
        lax.ppermute(part, "x", [(i, (i - step) % wide) for i in range(wide)])
        for step in range(1, wide)
    ]
    half = indexed_call(
        order_body,
        jax.ShapeDtypeStruct((wide, rows, CH), bf16),
        lax.axis_index("x"),
        part,
        *others,
    ).reshape(wide * rows, CH)
    return indexed_call(
        finish_body,
        jax.ShapeDtypeStruct((2, wide * rows, CH), f32),
        lax.axis_index("core"),
        half,
        swapped(half),
    )


def shards(frames, kernel, cotangent):
    x = frames[0]
    weights = kernel.reshape(3, WIDE, CH)
    turned = jnp.swapaxes(kernel[::-1, ::-1, ::-1], 3, 4).reshape(3, WIDE, CH)
    lines = ("z", "core")
    packed, cot_packed = pl.pallas_call(
        pack_body,
        out_shape=(
            jax.ShapeDtypeStruct((GROUP, HELD, CH), bf16),
            jax.ShapeDtypeStruct((GROUP, TILE, CH), bf16),
        ),
        in_specs=[pl.BlockSpec(memory_space=pl.ANY)] * 2,
        scratch_shapes=[
            pltpu.VMEM((ROWS, GROUP * STRIP, CH), bf16),
            pltpu.VMEM((ROWS, GROUP * STRIP, CH), bf16),
            pltpu.VMEM((GROUP, ROWS, CH), f32),
            pltpu.VMEM((GROUP, ROWS, CH), f32),
            pltpu.SemaphoreType.DMA((2,)),
        ],
    )(frames[0], cotangent[0])
    held = lax.all_to_all(packed, "y", 0, 0)
    cot = lax.all_to_all(cot_packed, "y", 0, 0)
    early = shifted(held[GROUP - 2 :], "x", 1)
    last, first = [
        jnp.concatenate([value[:, low : low + STRIP] for value in (early, held)], axis=0)
        for low in (TILE - STRIP, 0)
    ]
    edges = jnp.concatenate([early[:, TILE:], held[:, TILE:]], axis=0)
    up = shifted(jnp.concatenate([last, edges], axis=1), lines, 1)
    down = shifted(jnp.concatenate([first, edges], axis=1), lines, -1)

    flops = 2 * GROUP * TILE * 27 * CH * CH
    code, g, terms = kernel_call(
        forward_body,
        (
            jax.ShapeDtypeStruct((GROUP, TILE, CH), bf16),
            jax.ShapeDtypeStruct((GROUP, TILE, CH), bf16),
            jax.ShapeDtypeStruct((27, CH, CH), bf16),
        ),
        [
            pltpu.VMEM((FRAMES * TILE, WIDE), bf16),
            pltpu.VMEM((GROUP * TILE, CH), f32),
            pltpu.VMEM((3 * CH, FRAMES * TILE), bf16),
        ],
        flops=2 * flops,
    )(held, early, up, down, cot, weights)

    norm = 1.0 / math.sqrt(lax.axis_size(("x", "y", "z", "core")) * GROUP * TILE)
    total, part_rows = own_share(terms.reshape(27 * CH, CH), norm)

    g_up = shifted(g[:, TILE - STRIP :], lines, 1)
    g_down = shifted(g[:, :STRIP], lines, -1)
    late = shifted(jnp.concatenate([g_up[:2], g[:2], g_down[:2]], axis=1), "x", -1)
    sent = kernel_call(
        backward_body,
        jax.ShapeDtypeStruct((GROUP, 2 * TILE + EDGES, CH), bf16),
        [
            pltpu.VMEM((FRAMES * TILE, WIDE), bf16),
            pltpu.VMEM((FRAMES * ROWS, 3 * CH), f32),
        ],
        flops=flops,
    )(g, g_up, g_down, late, code, turned)
    total, sent = lax.optimization_barrier((total, sent))
    grad_kernel = all_shares(total, part_rows)
    got = lax.all_to_all(sent, "y", 0, 0)
    whole = jax.ShapeDtypeStruct((ROWS, GROUP * STRIP, CH), bf16)
    code_out, grad_frames = kernel_call(unpack_body, (whole, whole))(got)
    return (code_out[None], grad_frames[None], grad_kernel.reshape(3, 3, 3, CH, CH))


def solution(mesh):
    split = Mesh(mesh.devices.reshape(CHIPS), ("x", "y", "z", "core"))
    block = P(("x", "y"), ("z", "core"), None, None)
    return jax.shard_map(
        shards,
        mesh=split,
        in_specs=(block, P(), block),
        out_specs=(block, block, P()),
        check_vma=False,
    )
```

```python
import functools
import math

import jax
import jax.numpy as jnp
from jax import lax
from jax.experimental import pallas as pl
from jax.experimental.pallas import tpu as pltpu
from jax.sharding import Mesh
from jax.sharding import PartitionSpec as P

CHIPS = (4, 8, 8, 2)
LEVELS = 3
GROUP = 1 << LEVELS
ROWS = 8
STRIP = 16
TILE = ROWS * STRIP
TALL = ROWS + 2
CH = 128
WIDE = 9 * CH
FRAMES = GROUP + 2
EDGES = 2 * ROWS
HELD = TILE + EDGES
SENT_ROWS = 2 * STRIP + EDGES
RIM = 2 * STRIP
PART = 8

band_weight = 0.75
root_half = 0.7071067811865476
f32 = jnp.float32
bf16 = jnp.bfloat16
VMEM_LIMIT = 48 * 1024 * 1024


def kernel_call(body, outs, scratch=(), flops=0):
    return pl.pallas_call(
        body,
        out_shape=outs,
        scratch_shapes=list(scratch),
        compiler_params=pltpu.CompilerParams(vmem_limit_bytes=VMEM_LIMIT),
        cost_estimate=pl.CostEstimate(flops=flops, bytes_accessed=4 << 20, transcendentals=0),
    )


def pack_body(x_hbm, cot_hbm, out_ref, cot_out_ref, x_ref, cot_ref, left_ref, right_ref, sems):
    x_copy = pltpu.make_async_copy(x_hbm, x_ref, sems.at[0])
    cot_copy = pltpu.make_async_copy(cot_hbm, cot_ref, sems.at[1])
    x_copy.start()
    cot_copy.start()
    left_ref[...] = jnp.zeros_like(left_ref)
    right_ref[...] = jnp.zeros_like(right_ref)
    x_copy.wait()
    for row in range(ROWS):
        line = x_ref[row]
        wide = line.astype(f32)
        for strip in range(GROUP):
            low = strip * STRIP
            out_ref[strip, pl.ds(row * STRIP, STRIP), :] = line[low : low + STRIP]
            if strip > 0:
                left_ref[strip, pl.ds(row, 1), :] = wide[low - 1 : low]
            if strip < GROUP - 1:
                right_ref[strip, pl.ds(row, 1), :] = wide[low + STRIP : low + STRIP + 1]
    for strip in range(GROUP):
        pair = jnp.concatenate([left_ref[strip], right_ref[strip]], axis=0)
        out_ref[strip, pl.ds(TILE, EDGES), :] = pair.astype(bf16)
    cot_copy.wait()
    for strip in range(GROUP):
        for row in range(ROWS):
            cot_out_ref[strip, pl.ds(row * STRIP, STRIP), :] = cot_ref[
                row, pl.ds(strip * STRIP, STRIP), :
            ]


def place_line(col_ref, line, left, right, places):
    at = lax.broadcasted_iota(jnp.int32, (STRIP, CH), 0)
    wide = line.astype(f32)
    before = jnp.where(at == 0, left, pltpu.roll(wide, 1, 0)).astype(bf16)
    after = jnp.where(at == STRIP - 1, right, pltpu.roll(wide, STRIP - 1, 0)).astype(bf16)
    for row_tap, place in places:
        start = pl.multiple_of(place, STRIP)
        for col_tap, piece in enumerate((before, line, after)):
            tap = row_tap * 3 + col_tap
            col_ref[pl.ds(start, STRIP), pl.ds(tap * CH, CH)] = piece


def adjoint_bands(cot):
    back = [None] * GROUP
    for level in range(LEVELS - 1, -1, -1):
        step = 1 << level
        following = [None] * GROUP
        for frame in range(GROUP):
            if frame & step:
                continue
            pair = (cot[frame] + cot[frame + step]) * root_half
            if level == LEVELS - 1:
                total = pair
            else:
                total = (back[frame] + back[frame + step]) * root_half
            for member, side in ((frame, -1.0), (frame + step, 1.0)):
                value = total + (band_weight * side) * pair
                if level > 0:
                    value = value.astype(bf16).astype(f32)
                following[member] = value
        back = following
    return back


def slope_of(linear, gate):
    return gate * (1.0 + linear * (1.0 - gate))


def forward_body(
    held_ref,
    early_ref,
    up_ref,
    down_ref,
    cot_ref,
    w_ref,
    code_ref,
    g_ref,
    g_up_ref,
    g_down_ref,
    dw_ref,
    col_ref,
    lin_ref,
    gt_ref,
):
    def spread(ref, frame, place):
        for tall_row in range(-2, ROWS + 2):
            if tall_row < 0:
                source, low, edge_row = up_ref, (tall_row + 2) * STRIP, ROWS + tall_row
                base = place * SENT_ROWS
            elif tall_row >= ROWS:
                source, low, edge_row = down_ref, (tall_row - ROWS) * STRIP, tall_row - ROWS
                base = place * SENT_ROWS
            else:
                source, low, edge_row = ref, tall_row * STRIP, tall_row
                base = None
            if base is None:
                line = source[frame, pl.ds(low, STRIP), :]
                edge = source[frame, pl.ds(TILE, EDGES), :].astype(f32)
            else:
                line = source[pl.ds(pl.multiple_of(base + low, STRIP), STRIP), :]
                edge_low = pl.multiple_of(base + 2 * STRIP, STRIP)
                edge = source[pl.ds(edge_low, EDGES), :].astype(f32)
            places = []
            for row_tap in range(3):
                row = tall_row + 1 - row_tap
                if 0 <= row < ROWS:
                    places.append((row_tap, place * TILE + row * STRIP))
                elif row == -1:
                    places.append((row_tap, FRAMES * TILE + place * RIM))
                elif row == ROWS:
                    places.append((row_tap, FRAMES * TILE + place * RIM + STRIP))
            place_line(
                col_ref,
                line,
                edge[edge_row : edge_row + 1],
                edge[ROWS + edge_row : ROWS + edge_row + 1],
                places,
            )

    @pl.loop(0, 2)
    def _(frame):
        spread(early_ref, frame, frame)

    @pl.loop(0, GROUP)
    def _(frame):
        spread(held_ref, frame, frame + 2)

    for low, step in ((0, TILE), (FRAMES * TILE, RIM)):
        total = None
        for tap in range(3):
            rows = col_ref[low + tap * step : low + (tap + GROUP) * step, :]
            part = jnp.dot(rows, w_ref[tap], preferred_element_type=f32)
            total = part if total is None else total + part
        place = 0 if step == TILE else GROUP * TILE
        lin_ref[place : place + GROUP * step, :] = total

    @pl.loop(0, ROWS)
    def _(row):
        low = pl.multiple_of(row * STRIP, STRIP)
        linear = [lin_ref[pl.ds(frame * TILE + low, STRIP), :] for frame in range(GROUP)]
        gate = [jax.nn.sigmoid(value) for value in linear]
        band = [(value * part).astype(bf16).astype(f32) for value, part in zip(linear, gate)]
        detail = [None] * GROUP
        for level in range(LEVELS):
            step = 1 << level
            following = [None] * GROUP
            for frame in range(0, GROUP, 2 * step):
                lower, upper = band[frame], band[frame + step]
                smooth = (lower + upper) * root_half
                if level < LEVELS - 1:
                    smooth = smooth.astype(bf16).astype(f32)
                change = (upper - lower) * root_half
                following[frame] = smooth
                for member in range(frame, frame + 2 * step, 2):
                    detail[member] = change if level == 0 else detail[member] + change
            band = following
        for member in range(0, GROUP, 2):
            code = (band[0] + band_weight * detail[member]).astype(bf16)
            code_ref[member, pl.ds(low, STRIP), :] = code
            code_ref[member + 1, pl.ds(low, STRIP), :] = code
        cot = [cot_ref[frame, pl.ds(low, STRIP), :].astype(f32) for frame in range(GROUP)]
        back = adjoint_bands(cot)
        for frame in range(GROUP):
            g_ref[frame, pl.ds(low, STRIP), :] = (
                back[frame] * slope_of(linear[frame], gate[frame])
            ).astype(bf16)

    for offset, source, rim_ref in ((0, up_ref, g_up_ref), (STRIP, down_ref, g_down_ref)):
        cot = [
            source[pl.ds(FRAMES * SENT_ROWS + frame * STRIP, STRIP), :].astype(f32)
            for frame in range(GROUP)
        ]
        back = adjoint_bands(cot)
        for frame in range(GROUP):
            linear = lin_ref[pl.ds(GROUP * TILE + frame * RIM + offset, STRIP), :]
            slope = slope_of(linear, jax.nn.sigmoid(linear))
            rim_ref[frame] = (back[frame] * slope).astype(bf16)

    gt_ref[...] = jnp.zeros_like(gt_ref)
    for frame in range(GROUP):
        turned = g_ref[frame].astype(f32).T.astype(bf16)
        for tap in range(3):
            gt_ref[pl.ds(tap * CH, CH), pl.ds((frame + tap) * TILE, TILE)] = turned
    for tap in range(9):
        product = jnp.dot(
            gt_ref[...],
            col_ref[0 : FRAMES * TILE, tap * CH : (tap + 1) * CH],
            preferred_element_type=f32,
        )
        for frame_tap in range(3):
            block = product[frame_tap * CH : (frame_tap + 1) * CH]
            dw_ref[frame_tap * 9 + tap] = block.T.astype(bf16)


def backward_body(g_ref, up_ref, down_ref, late_ref, code_ref, w_ref, out_ref, col_ref, side_ref):
    nothing = jnp.zeros((1, CH), f32)

    def spread(lines, place):
        for tall_row, line in enumerate(lines):
            places = [
                (row_tap, place * TILE + (tall_row - row_tap) * STRIP)
                for row_tap in range(3)
                if 0 <= tall_row - row_tap < ROWS
            ]
            place_line(col_ref, line, nothing, nothing, places)

    @pl.loop(0, GROUP)
    def _(frame):
        rows = [g_ref[frame, pl.ds(row * STRIP, STRIP), :] for row in range(ROWS)]
        spread([up_ref[frame]] + rows + [down_ref[frame]], frame)

    @pl.loop(0, 2)
    def _(frame):
        lines = [late_ref[frame, pl.ds(row * STRIP, STRIP), :] for row in range(TALL)]
        spread(lines, frame + GROUP)

    total = (
        jnp.dot(col_ref[0 : GROUP * TILE, :], w_ref[0], preferred_element_type=f32)
        + jnp.dot(col_ref[TILE : (GROUP + 1) * TILE, :], w_ref[1], preferred_element_type=f32)
        + jnp.dot(col_ref[2 * TILE : (GROUP + 2) * TILE, :], w_ref[2], preferred_element_type=f32)
    )
    for frame in range(GROUP):
        out_ref[frame, 0:TILE, :] = code_ref[frame]
        out_ref[frame, TILE : 2 * TILE, :] = total[frame * TILE : (frame + 1) * TILE].astype(bf16)
    for side, (offset, col_tap) in enumerate(((0, 2), (STRIP - 1, 0))):
        for frame in range(FRAMES):
            for row in range(ROWS):
                at = frame * TILE + row * STRIP + (0 if side == 0 else STRIP - 8)
                for row_tap in range(3):
                    mid = (row_tap * 3 + 1) * CH
                    piece = col_ref[pl.ds(frame * TILE + row * STRIP, STRIP), pl.ds(mid, CH)]
                    one = piece.astype(f32)[offset : offset + 1]
                    side_ref[pl.ds(frame * ROWS + row, 1), pl.ds(row_tap * CH, CH)] = one
        summed = None
        for frame_tap in range(3):
            rows = side_ref[pl.ds(frame_tap * ROWS, GROUP * ROWS), :].astype(bf16)
            for row_tap in range(3):
                tap = row_tap * 3 + col_tap
                part = jnp.dot(
                    rows[:, row_tap * CH : (row_tap + 1) * CH],
                    w_ref[frame_tap, pl.ds(tap * CH, CH), :],
                    preferred_element_type=f32,
                )
                summed = part if summed is None else summed + part
        if side == 0:
            first = summed
    for frame in range(GROUP):
        pair = [value[frame * ROWS : (frame + 1) * ROWS] for value in (first, summed)]
        out_ref[frame, 2 * TILE : 2 * TILE + EDGES, :] = jnp.concatenate(pair, axis=0).astype(bf16)


def unpack_body(got_ref, code_ref, grad_ref):
    at = lax.broadcasted_iota(jnp.int32, (STRIP, CH), 0)
    for strip in range(GROUP):
        columns = pl.ds(strip * STRIP, STRIP)
        if strip > 0:
            before = got_ref[strip - 1, pl.ds(2 * TILE, EDGES), :].astype(f32)
        if strip < GROUP - 1:
            after = got_ref[strip + 1, pl.ds(2 * TILE, EDGES), :].astype(f32)
        for row in range(ROWS):
            code_ref[row, columns, :] = got_ref[strip, pl.ds(row * STRIP, STRIP), :]
            value = got_ref[strip, pl.ds(TILE + row * STRIP, STRIP), :].astype(f32)
            if strip > 0:
                value = value + jnp.where(at == 0, before[ROWS + row : ROWS + row + 1], 0.0)
            if strip < GROUP - 1:
                value = value + jnp.where(at == STRIP - 1, after[row : row + 1], 0.0)
            grad_ref[row, columns, :] = value.astype(bf16)


def shifted(value, axes, by):
    count = lax.axis_size(axes)
    route = [(i, i + by) for i in range(count) if 0 <= i + by < count]
    return lax.ppermute(value, axes, route)


def swapped(value):
    return lax.ppermute(value, "core", [(0, 1), (1, 0)])


def own_share(terms, norm):
    core = lax.axis_index("core")
    deep, planes = lax.axis_size("z"), lax.axis_size(("x", "y"))
    rows = terms.shape[0] // (2 * deep)
    halves = terms.reshape(deep, 2, rows, CH)
    mine = lax.dynamic_index_in_dim(halves, core, 1, keepdims=False)
    other = lax.dynamic_index_in_dim(halves, 1 - core, 1, keepdims=False)
    chip_sum = (mine.astype(f32) + swapped(other).astype(f32)).astype(bf16)
    parts = lax.all_to_all(chip_sum, "z", 0, 0)
    part = parts.astype(f32).sum(axis=0).astype(bf16)
    share = PART * -(-rows // (PART * planes))
    padded = jnp.pad(part, ((0, share * planes - rows), (0, 0)))
    spread = lax.all_to_all(padded.reshape(planes, share, CH), ("x", "y"), 0, 0)
    return (spread.astype(f32).sum(axis=0) * norm).astype(bf16), rows


def all_shares(total, rows):
    planes = lax.axis_size(("x", "y"))
    copies = jnp.broadcast_to(total[None], (planes,) + total.shape)
    part = lax.all_to_all(copies, ("x", "y"), 0, 0).reshape(-1, CH)[:rows]
    return lax.all_gather(part, ("z", "core"), tiled=True).astype(f32)


def shards(frames, kernel, cotangent):
    x = frames[0]
    weights = kernel.reshape(3, WIDE, CH)
    turned = jnp.swapaxes(kernel[::-1, ::-1, ::-1], 3, 4).reshape(3, WIDE, CH)
    lines = ("z", "core")
    packed, cot_packed = pl.pallas_call(
        pack_body,
        out_shape=(
            jax.ShapeDtypeStruct((GROUP, HELD, CH), bf16),
            jax.ShapeDtypeStruct((GROUP, TILE, CH), bf16),
        ),
        in_specs=[pl.BlockSpec(memory_space=pl.ANY)] * 2,
        scratch_shapes=[
            pltpu.VMEM((ROWS, GROUP * STRIP, CH), bf16),
            pltpu.VMEM((ROWS, GROUP * STRIP, CH), bf16),
            pltpu.VMEM((GROUP, ROWS, CH), f32),
            pltpu.VMEM((GROUP, ROWS, CH), f32),
            pltpu.SemaphoreType.DMA((2,)),
        ],
    )(frames[0], cotangent[0])
    held = lax.all_to_all(packed, "y", 0, 0)
    cot = lax.all_to_all(cot_packed, "y", 0, 0)
    early = shifted(held[GROUP - 2 :], "x", 1)
    both = [jnp.concatenate([early[:, low:], held[:, low:]], axis=0) for low in (TILE - RIM, TILE)]
    first = jnp.concatenate([early[:, :RIM], held[:, :RIM]], axis=0)
    up_rows = both[0].reshape(FRAMES * SENT_ROWS, CH)
    down_rows = jnp.concatenate([first, both[1]], axis=1).reshape(FRAMES * SENT_ROWS, CH)
    up_cot = cot[:, TILE - STRIP :].reshape(GROUP * STRIP, CH)
    down_cot = cot[:, :STRIP].reshape(GROUP * STRIP, CH)
    up = shifted(jnp.concatenate([up_rows, up_cot], axis=0), lines, 1)
    down = shifted(jnp.concatenate([down_rows, down_cot], axis=0), lines, -1)

    flops = 2 * GROUP * TILE * 27 * CH * CH
    code, g, g_up, g_down, terms = kernel_call(
        forward_body,
        (
            jax.ShapeDtypeStruct((GROUP, TILE, CH), bf16),
            jax.ShapeDtypeStruct((GROUP, TILE, CH), bf16),
            jax.ShapeDtypeStruct((GROUP, STRIP, CH), bf16),
            jax.ShapeDtypeStruct((GROUP, STRIP, CH), bf16),
            jax.ShapeDtypeStruct((27, CH, CH), bf16),
        ),
        [
            pltpu.VMEM((FRAMES * (TILE + RIM), WIDE), bf16),
            pltpu.VMEM((GROUP * (TILE + RIM), CH), f32),
            pltpu.VMEM((3 * CH, FRAMES * TILE), bf16),
        ],
        flops=2 * flops,
    )(held, early, up, down, cot, weights)

    norm = 1.0 / math.sqrt(lax.axis_size(("x", "y", "z", "core")) * GROUP * TILE)
    total, part_rows = own_share(terms.reshape(27 * CH, CH), norm)

    late = shifted(jnp.concatenate([g_up[:2], g[:2], g_down[:2]], axis=1), "x", -1)
    sent = kernel_call(
        backward_body,
        jax.ShapeDtypeStruct((GROUP, 2 * TILE + EDGES, CH), bf16),
        [
            pltpu.VMEM((FRAMES * TILE, WIDE), bf16),
            pltpu.VMEM((FRAMES * ROWS, 3 * CH), f32),
        ],
        flops=flops,
    )(g, g_up, g_down, late, code, turned)
    total, sent = lax.optimization_barrier((total, sent))
    grad_kernel = all_shares(total, part_rows)
    got = lax.all_to_all(sent, "y", 0, 0)
    whole = jax.ShapeDtypeStruct((ROWS, GROUP * STRIP, CH), bf16)
    code_out, grad_frames = kernel_call(unpack_body, (whole, whole))(got)
    return (code_out[None], grad_frames[None], grad_kernel.reshape(3, 3, 3, CH, CH))


def solution(mesh):
    split = Mesh(mesh.devices.reshape(CHIPS), ("x", "y", "z", "core"))
    block = P(("x", "y"), ("z", "core"), None, None)
    return jax.shard_map(
        shards,
        mesh=split,
        in_specs=(block, P(), block),
        out_specs=(block, block, P()),
        check_vma=False,
    )
```

```python
import functools
import math

import jax
import jax.numpy as jnp
from jax import lax
from jax.experimental import pallas as pl
from jax.experimental.pallas import tpu as pltpu
from jax.sharding import Mesh
from jax.sharding import PartitionSpec as P

CHIPS = (4, 8, 8, 2)
LEVELS = 3
GROUP = 1 << LEVELS
ROWS = 8
STRIP = 16
TILE = ROWS * STRIP
TALL = ROWS + 2
CH = 128
WIDE = 9 * CH
FRAMES = GROUP + 2
EDGES = 2 * ROWS
HELD = TILE + EDGES
RIM = 2 * STRIP
PART = 8

band_weight = 0.75
root_half = 0.7071067811865476
f32 = jnp.float32
bf16 = jnp.bfloat16
VMEM_LIMIT = 48 * 1024 * 1024


def kernel_call(body, outs, scratch=(), flops=0, **specs):
    return pl.pallas_call(
        body,
        **specs,
        out_shape=outs,
        scratch_shapes=list(scratch),
        compiler_params=pltpu.CompilerParams(vmem_limit_bytes=VMEM_LIMIT),
        cost_estimate=pl.CostEstimate(flops=flops, bytes_accessed=4 << 20, transcendentals=0),
    )


def pack_body(x_hbm, out_ref, x_ref, left_ref, right_ref, sem):
    copy = pltpu.make_async_copy(x_hbm, x_ref, sem)
    copy.start()
    left_ref[...] = jnp.zeros_like(left_ref)
    right_ref[...] = jnp.zeros_like(right_ref)
    copy.wait()
    for row in range(ROWS):
        line = x_ref[row]
        wide = line.astype(f32)
        for strip in range(GROUP):
            low = strip * STRIP
            out_ref[strip, pl.ds(row * STRIP, STRIP), :] = line[low : low + STRIP]
            if strip > 0:
                left_ref[strip, pl.ds(row, 1), :] = wide[low - 1 : low]
            if strip < GROUP - 1:
                right_ref[strip, pl.ds(row, 1), :] = wide[low + STRIP : low + STRIP + 1]
    for strip in range(GROUP):
        pair = jnp.concatenate([left_ref[strip], right_ref[strip]], axis=0)
        out_ref[strip, pl.ds(TILE, EDGES), :] = pair.astype(bf16)


def pack_cot_body(cot_hbm, up_ref, down_ref, out_ref, cot_ref, sem):
    copy = pltpu.make_async_copy(cot_hbm, cot_ref, sem)
    copy.start()
    copy.wait()
    for tall_row in range(TALL):
        if tall_row == 0:
            line = up_ref[0]
        elif tall_row == TALL - 1:
            line = down_ref[0]
        else:
            line = cot_ref[tall_row - 1]
        for strip in range(GROUP):
            out_ref[strip, pl.ds(tall_row * STRIP, STRIP), :] = line[
                strip * STRIP : (strip + 1) * STRIP
            ]


def place_line(col_ref, line, left, right, places):
    at = lax.broadcasted_iota(jnp.int32, (STRIP, CH), 0)
    wide = line.astype(f32)
    before = jnp.where(at == 0, left, pltpu.roll(wide, 1, 0)).astype(bf16)
    after = jnp.where(at == STRIP - 1, right, pltpu.roll(wide, STRIP - 1, 0)).astype(bf16)
    for row_tap, place in places:
        start = pl.multiple_of(place, STRIP)
        for col_tap, piece in enumerate((before, line, after)):
            tap = row_tap * 3 + col_tap
            col_ref[pl.ds(start, STRIP), pl.ds(tap * CH, CH)] = piece


def adjoint_bands(cot):
    back = [None] * GROUP
    for level in range(LEVELS - 1, -1, -1):
        step = 1 << level
        following = [None] * GROUP
        for frame in range(GROUP):
            if frame & step:
                continue
            pair = (cot[frame] + cot[frame + step]) * root_half
            if level == LEVELS - 1:
                total = pair
            else:
                total = (back[frame] + back[frame + step]) * root_half
            for member, side in ((frame, -1.0), (frame + step, 1.0)):
                value = total + (band_weight * side) * pair
                if level > 0:
                    value = value.astype(bf16).astype(f32)
                following[member] = value
        back = following
    return back


def slope_of(linear, gate):
    return gate * (1.0 + linear * (1.0 - gate))


def forward_body(
    core_ref,
    held_ref,
    early_ref,
    up_ref,
    down_ref,
    cot_ref,
    w_ref,
    code_ref,
    g_ref,
    g_up_ref,
    g_down_ref,
    keep_ref,
    send_ref,
    col_ref,
    lin_ref,
    gt_ref,
    terms_ref,
):
    def spread(ref, frame, place):
        for tall_row in range(-2, ROWS + 2):
            if tall_row < 0:
                source, at, low, edge_row = up_ref, place, (tall_row + 2) * STRIP, ROWS + tall_row
            elif tall_row >= ROWS:
                source, at, low, edge_row = down_ref, place, (tall_row - ROWS) * STRIP, tall_row - ROWS
            else:
                source, at, low, edge_row = ref, frame, tall_row * STRIP, tall_row
            line = source[at, pl.ds(low, STRIP), :]
            edge = source[at, pl.ds(source.shape[1] - EDGES, EDGES), :].astype(f32)
            places = []
            for row_tap in range(3):
                row = tall_row + 1 - row_tap
                if 0 <= row < ROWS:
                    places.append((row_tap, place * TILE + row * STRIP))
                elif row == -1:
                    places.append((row_tap, FRAMES * TILE + place * RIM))
                elif row == ROWS:
                    places.append((row_tap, FRAMES * TILE + place * RIM + STRIP))
            place_line(
                col_ref,
                line,
                edge[edge_row : edge_row + 1],
                edge[ROWS + edge_row : ROWS + edge_row + 1],
                places,
            )

    @pl.loop(0, 2)
    def _(frame):
        spread(early_ref, frame, frame)

    @pl.loop(0, GROUP)
    def _(frame):
        spread(held_ref, frame, frame + 2)

    for low, step in ((0, TILE), (FRAMES * TILE, RIM)):
        total = None
        for tap in range(3):
            rows = col_ref[low + tap * step : low + (tap + GROUP) * step, :]
            part = jnp.dot(rows, w_ref[tap], preferred_element_type=f32)
            total = part if total is None else total + part
        place = 0 if step == TILE else GROUP * TILE
        lin_ref[place : place + GROUP * step, :] = total

    @pl.loop(0, ROWS)
    def _(row):
        low = pl.multiple_of(row * STRIP, STRIP)
        linear = [lin_ref[pl.ds(frame * TILE + low, STRIP), :] for frame in range(GROUP)]
        gate = [jax.nn.sigmoid(value) for value in linear]
        band = [(value * part).astype(bf16).astype(f32) for value, part in zip(linear, gate)]
        detail = [None] * GROUP
        for level in range(LEVELS):
            step = 1 << level
            following = [None] * GROUP
            for frame in range(0, GROUP, 2 * step):
                lower, upper = band[frame], band[frame + step]
                smooth = (lower + upper) * root_half
                if level < LEVELS - 1:
                    smooth = smooth.astype(bf16).astype(f32)
                change = (upper - lower) * root_half
                following[frame] = smooth
                for member in range(frame, frame + 2 * step, 2):
                    detail[member] = change if level == 0 else detail[member] + change
            band = following
        for member in range(0, GROUP, 2):
            code = (band[0] + band_weight * detail[member]).astype(bf16)
            code_ref[member, pl.ds(low, STRIP), :] = code
            code_ref[member + 1, pl.ds(low, STRIP), :] = code
        tall = pl.multiple_of(low + STRIP, STRIP)
        cot = [cot_ref[frame, pl.ds(tall, STRIP), :].astype(f32) for frame in range(GROUP)]
        back = adjoint_bands(cot)
        for frame in range(GROUP):
            g_ref[frame, pl.ds(low, STRIP), :] = (
                back[frame] * slope_of(linear[frame], gate[frame])
            ).astype(bf16)

    for offset, tall, rim_ref in ((0, 0, g_up_ref), (STRIP, TALL - 1, g_down_ref)):
        cot = [
            cot_ref[frame, pl.ds(tall * STRIP, STRIP), :].astype(f32) for frame in range(GROUP)
        ]
        back = adjoint_bands(cot)
        for frame in range(GROUP):
            linear = lin_ref[pl.ds(GROUP * TILE + frame * RIM + offset, STRIP), :]
            slope = slope_of(linear, jax.nn.sigmoid(linear))
            rim_ref[frame] = (back[frame] * slope).astype(bf16)

    gt_ref[...] = jnp.zeros_like(gt_ref)
    for frame in range(GROUP):
        turned = g_ref[frame].astype(f32).T.astype(bf16)
        for tap in range(3):
            gt_ref[pl.ds(tap * CH, CH), pl.ds((frame + tap) * TILE, TILE)] = turned
    terms_ref[...] = jnp.zeros_like(terms_ref)
    _, wide, planes, share = terms_ref.shape[:4]
    blocks = 27 * CH // PART
    slots = share // PART
    lines = 2 * (planes // GROUP)
    for low in range(0, 9, 2):
        high = min(low + 2, 9)
        product = jnp.dot(
            gt_ref[...],
            col_ref[0 : FRAMES * TILE, low * CH : high * CH],
            preferred_element_type=f32,
        )
        for tap in range(low, high):
            for frame_tap in range(3):
                block = product[
                    frame_tap * CH : (frame_tap + 1) * CH, (tap - low) * CH : (tap - low + 1) * CH
                ].T
                for piece in range(CH // PART):
                    at = (frame_tap * 9 + tap) * (CH // PART) + piece
                    line, within = divmod(at, blocks // lines)
                    owner, slot = divmod(within, slots)
                    depth, core = divmod(line, 2)
                    column, ring = divmod(owner, GROUP)
                    peer = ring * (planes // GROUP) + depth
                    terms_ref[core, column, peer, pl.ds(slot * PART, PART), :] = block[
                        piece * PART : (piece + 1) * PART
                    ]
    for core in range(2):

        @pl.when(core_ref[0] == core)
        def _():
            for column in range(wide):
                keep_ref[column] = terms_ref[core, column].reshape(-1, CH).astype(bf16)
                send_ref[column] = terms_ref[1 - core, column].reshape(-1, CH).astype(bf16)


def backward_body(g_ref, up_ref, down_ref, late_ref, code_ref, w_ref, out_ref, col_ref, side_ref):
    nothing = jnp.zeros((1, CH), f32)

    def spread(lines, place):
        for tall_row, line in enumerate(lines):
            places = [
                (row_tap, place * TILE + (tall_row - row_tap) * STRIP)
                for row_tap in range(3)
                if 0 <= tall_row - row_tap < ROWS
            ]
            place_line(col_ref, line, nothing, nothing, places)

    @pl.loop(0, GROUP)
    def _(frame):
        rows = [g_ref[frame, pl.ds(row * STRIP, STRIP), :] for row in range(ROWS)]
        spread([up_ref[frame]] + rows + [down_ref[frame]], frame)

    @pl.loop(0, 2)
    def _(frame):
        lines = [late_ref[frame, pl.ds(row * STRIP, STRIP), :] for row in range(TALL)]
        spread(lines, frame + GROUP)

    total = (
        jnp.dot(col_ref[0 : GROUP * TILE, :], w_ref[0], preferred_element_type=f32)
        + jnp.dot(col_ref[TILE : (GROUP + 1) * TILE, :], w_ref[1], preferred_element_type=f32)
        + jnp.dot(col_ref[2 * TILE : (GROUP + 2) * TILE, :], w_ref[2], preferred_element_type=f32)
    )
    for frame in range(GROUP):
        out_ref[frame, 0:TILE, :] = code_ref[frame]
        out_ref[frame, TILE : 2 * TILE, :] = total[frame * TILE : (frame + 1) * TILE].astype(bf16)
    for side, (offset, col_tap) in enumerate(((0, 2), (STRIP - 1, 0))):
        for frame in range(FRAMES):
            for row in range(ROWS):
                at = frame * TILE + row * STRIP + (0 if side == 0 else STRIP - 8)
                for row_tap in range(3):
                    mid = (row_tap * 3 + 1) * CH
                    piece = col_ref[pl.ds(frame * TILE + row * STRIP, STRIP), pl.ds(mid, CH)]
                    one = piece.astype(f32)[offset : offset + 1]
                    side_ref[pl.ds(frame * ROWS + row, 1), pl.ds(row_tap * CH, CH)] = one
        summed = None
        for frame_tap in range(3):
            rows = side_ref[pl.ds(frame_tap * ROWS, GROUP * ROWS), :].astype(bf16)
            for row_tap in range(3):
                tap = row_tap * 3 + col_tap
                part = jnp.dot(
                    rows[:, row_tap * CH : (row_tap + 1) * CH],
                    w_ref[frame_tap, pl.ds(tap * CH, CH), :],
                    preferred_element_type=f32,
                )
                summed = part if summed is None else summed + part
        if side == 0:
            first = summed
    for frame in range(GROUP):
        pair = [value[frame * ROWS : (frame + 1) * ROWS] for value in (first, summed)]
        out_ref[frame, 2 * TILE : 2 * TILE + EDGES, :] = jnp.concatenate(pair, axis=0).astype(bf16)


def unpack_body(got_ref, code_ref, grad_ref):
    at = lax.broadcasted_iota(jnp.int32, (STRIP, CH), 0)
    for strip in range(GROUP):
        columns = pl.ds(strip * STRIP, STRIP)
        if strip > 0:
            before = got_ref[strip - 1, pl.ds(2 * TILE, EDGES), :].astype(f32)
        if strip < GROUP - 1:
            after = got_ref[strip + 1, pl.ds(2 * TILE, EDGES), :].astype(f32)
        for row in range(ROWS):
            code_ref[row, columns, :] = got_ref[strip, pl.ds(row * STRIP, STRIP), :]
            value = got_ref[strip, pl.ds(TILE + row * STRIP, STRIP), :].astype(f32)
            if strip > 0:
                value = value + jnp.where(at == 0, before[ROWS + row : ROWS + row + 1], 0.0)
            if strip < GROUP - 1:
                value = value + jnp.where(at == STRIP - 1, after[row : row + 1], 0.0)
            grad_ref[row, columns, :] = value.astype(bf16)


def shifted(value, axes, by):
    count = lax.axis_size(axes)
    route = [(i, i + by) for i in range(count) if 0 <= i + by < count]
    return lax.ppermute(value, axes, route)


def swapped(value):
    return lax.ppermute(value, "core", [(0, 1), (1, 0)])


def own_share(chip_sum, norm):
    planes = lax.axis_size(("y", "z"))
    parts = lax.all_to_all(chip_sum, "x", 0, 0)
    part = parts.astype(f32).sum(axis=0).astype(bf16).reshape(planes, -1, CH)
    spread = lax.all_to_all(part, ("y", "z"), 0, 0)
    return (spread.astype(f32).sum(axis=0) * norm).astype(bf16)


def all_shares(total):
    owners, lines = lax.axis_size(("x", "y")), lax.axis_size(("z", "core"))
    copies = jnp.broadcast_to(total[None], (owners,) + total.shape)
    part = lax.all_to_all(copies, ("x", "y"), 0, 0).reshape(-1, CH)[: 27 * CH // lines]
    return lax.all_gather(part, ("z", "core"), tiled=True).astype(f32)


def shards(frames, kernel, cotangent):
    weights = kernel.reshape(3, WIDE, CH)
    turned = jnp.swapaxes(kernel[::-1, ::-1, ::-1], 3, 4).reshape(3, WIDE, CH)
    lines = ("z", "core")
    whole_vmem = pltpu.VMEM((ROWS, GROUP * STRIP, CH), bf16)
    in_hbm = pl.BlockSpec(memory_space=pl.ANY)
    in_vmem = pl.BlockSpec(memory_space=pltpu.VMEM)
    packed = pl.pallas_call(
        pack_body,
        out_shape=jax.ShapeDtypeStruct((GROUP, HELD, CH), bf16),
        in_specs=[in_hbm],
        scratch_shapes=[whole_vmem]
        + [pltpu.VMEM((GROUP, ROWS, CH), f32)] * 2
        + [pltpu.SemaphoreType.DMA],
    )(frames[0])
    held = lax.all_to_all(packed, "y", 0, 0)
    cot_up = shifted(cotangent[0, ROWS - 1 :], lines, 1)
    cot_down = shifted(cotangent[0, :1], lines, -1)
    cot_packed = pl.pallas_call(
        pack_cot_body,
        out_shape=jax.ShapeDtypeStruct((GROUP, TALL * STRIP, CH), bf16),
        in_specs=[in_hbm, in_vmem, in_vmem],
        scratch_shapes=[whole_vmem, pltpu.SemaphoreType.DMA],
    )(cotangent[0], cot_up, cot_down)
    cot = lax.all_to_all(cot_packed, "y", 0, 0)
    early = shifted(held[GROUP - 2 :], "x", 1)
    edges = jnp.concatenate([early[:, TILE:], held[:, TILE:]], axis=0)
    last = jnp.concatenate([early[:, TILE - RIM :], held[:, TILE - RIM :]], axis=0)
    first = jnp.concatenate([early[:, :RIM], held[:, :RIM]], axis=0)
    up = shifted(last, lines, 1)
    down = shifted(jnp.concatenate([first, edges], axis=1), lines, -1)
    turned, held = lax.optimization_barrier((turned, held))

    wide, planes = lax.axis_size("x"), lax.axis_size(("y", "z"))
    devices = lax.axis_size(("x", "y", "z", "core"))
    share = PART * -(-27 * CH // (PART * devices))
    mail = jax.ShapeDtypeStruct((wide, planes * share, CH), bf16)
    flops = 2 * GROUP * TILE * 27 * CH * CH
    code, g, g_up, g_down, keep, send = kernel_call(
        forward_body,
        (
            jax.ShapeDtypeStruct((GROUP, TILE, CH), bf16),
            jax.ShapeDtypeStruct((GROUP, TILE, CH), bf16),
            jax.ShapeDtypeStruct((GROUP, STRIP, CH), bf16),
            jax.ShapeDtypeStruct((GROUP, STRIP, CH), bf16),
            mail,
            mail,
        ),
        [
            pltpu.VMEM((FRAMES * (TILE + RIM), WIDE), bf16),
            pltpu.VMEM((GROUP * (TILE + RIM), CH), f32),
            pltpu.VMEM((3 * CH, FRAMES * TILE), bf16),
            pltpu.VMEM((2, wide, planes, share, CH), f32),
        ],
        flops=2 * flops,
        in_specs=[pl.BlockSpec(memory_space=pltpu.SMEM)] + [in_vmem] * 6,
    )(lax.axis_index("core").astype(jnp.int32).reshape(1), held, early, up, down, cot, weights)

    norm = 1.0 / math.sqrt(devices * GROUP * TILE)
    chip_sum = (keep.astype(f32) + swapped(send).astype(f32)).astype(bf16)
    total = own_share(chip_sum, norm)

    late = shifted(jnp.concatenate([g_up[:2], g[:2], g_down[:2]], axis=1), "x", -1)
    sent = kernel_call(
        backward_body,
        jax.ShapeDtypeStruct((GROUP, 2 * TILE + EDGES, CH), bf16),
        [
            pltpu.VMEM((FRAMES * TILE, WIDE), bf16),
            pltpu.VMEM((FRAMES * ROWS, 3 * CH), f32),
        ],
        flops=flops,
    )(g, g_up, g_down, late, code, turned)
    total, sent = lax.optimization_barrier((total, sent))
    grad_kernel = all_shares(total)
    got = lax.all_to_all(sent, "y", 0, 0)
    whole = jax.ShapeDtypeStruct((ROWS, GROUP * STRIP, CH), bf16)
    code_out, grad_frames = kernel_call(unpack_body, (whole, whole))(got)
    return (code_out[None], grad_frames[None], grad_kernel.reshape(3, 3, 3, CH, CH))


def solution(mesh):
    split = Mesh(mesh.devices.reshape(CHIPS), ("x", "y", "z", "core"))
    block = P(("x", "y"), ("z", "core"), None, None)
    return jax.shard_map(
        shards,
        mesh=split,
        in_specs=(block, P(), block),
        out_specs=(block, block, P()),
        check_vma=False,
    )
```

```python
import functools
import math

import jax
import jax.numpy as jnp
from jax import lax
from jax.experimental import pallas as pl
from jax.experimental.pallas import tpu as pltpu
from jax.sharding import Mesh
from jax.sharding import PartitionSpec as P

CHIPS = (4, 8, 8, 2)
LEVELS = 3
GROUP = 1 << LEVELS
ROWS = 8
STRIP = 16
TILE = ROWS * STRIP
TALL = ROWS + 2
CH = 128
WIDE = 9 * CH
FRAMES = GROUP + 2
EDGES = 2 * ROWS
HELD = TILE + EDGES
LOAD = HELD + TILE
SENT = TILE + EDGES
RIM = 2 * STRIP
PART = 8

band_weight = 0.75
root_half = 0.7071067811865476
f32 = jnp.float32
bf16 = jnp.bfloat16
VMEM_LIMIT = 48 * 1024 * 1024


def kernel_call(body, outs, scratch=(), flops=0, **specs):
    return pl.pallas_call(
        body,
        **specs,
        out_shape=outs,
        scratch_shapes=list(scratch),
        compiler_params=pltpu.CompilerParams(vmem_limit_bytes=VMEM_LIMIT),
        cost_estimate=pl.CostEstimate(flops=flops, bytes_accessed=4 << 20, transcendentals=0),
    )


def pack_body(x_hbm, cot_hbm, out_ref, x_ref, cot_ref, left_ref, right_ref, sems):
    x_copy = pltpu.make_async_copy(x_hbm, x_ref, sems.at[0])
    cot_copy = pltpu.make_async_copy(cot_hbm, cot_ref, sems.at[1])
    x_copy.start()
    cot_copy.start()
    left_ref[...] = jnp.zeros_like(left_ref)
    right_ref[...] = jnp.zeros_like(right_ref)
    x_copy.wait()
    for row in range(ROWS):
        line = x_ref[row]
        wide = line.astype(f32)
        for strip in range(GROUP):
            low = strip * STRIP
            out_ref[strip, pl.ds(row * STRIP, STRIP), :] = line[low : low + STRIP]
            if strip > 0:
                left_ref[strip, pl.ds(row, 1), :] = wide[low - 1 : low]
            if strip < GROUP - 1:
                right_ref[strip, pl.ds(row, 1), :] = wide[low + STRIP : low + STRIP + 1]
    for strip in range(GROUP):
        pair = jnp.concatenate([left_ref[strip], right_ref[strip]], axis=0)
        out_ref[strip, pl.ds(TILE, EDGES), :] = pair.astype(bf16)
    cot_copy.wait()
    for row in range(ROWS):
        line = cot_ref[row]
        for strip in range(GROUP):
            out_ref[strip, pl.ds(cot_place(row), STRIP), :] = line[
                strip * STRIP : (strip + 1) * STRIP
            ]


def cot_place(row):
    return HELD + (row + 1) % ROWS * STRIP


def place_line(col_ref, line, left, right, places):
    at = lax.broadcasted_iota(jnp.int32, (STRIP, CH), 0)
    wide = line.astype(f32)
    before = jnp.where(at == 0, left, pltpu.roll(wide, 1, 0)).astype(bf16)
    after = jnp.where(at == STRIP - 1, right, pltpu.roll(wide, STRIP - 1, 0)).astype(bf16)
    for row_tap, place in places:
        start = pl.multiple_of(place, STRIP)
        for col_tap, piece in enumerate((before, line, after)):
            tap = row_tap * 3 + col_tap
            col_ref[pl.ds(start, STRIP), pl.ds(tap * CH, CH)] = piece


def adjoint_bands(cot):
    back = [None] * GROUP
    for level in range(LEVELS - 1, -1, -1):
        step = 1 << level
        following = [None] * GROUP
        for frame in range(GROUP):
            if frame & step:
                continue
            pair = (cot[frame] + cot[frame + step]) * root_half
            if level == LEVELS - 1:
                total = pair
            else:
                total = (back[frame] + back[frame + step]) * root_half
            for member, side in ((frame, -1.0), (frame + step, 1.0)):
                value = total + (band_weight * side) * pair
                if level > 0:
                    value = value.astype(bf16).astype(f32)
                following[member] = value
        back = following
    return back


def slope_of(linear, gate):
    return gate * (1.0 + linear * (1.0 - gate))


def forward_body(
    core_ref,
    held_ref,
    early_ref,
    up_ref,
    down_ref,
    w_ref,
    code_ref,
    g_ref,
    g_up_ref,
    g_down_ref,
    keep_ref,
    send_ref,
    col_ref,
    lin_ref,
    gt_ref,
    terms_ref,
):
    def spread(ref, frame, place):
        for tall_row in range(-2, ROWS + 2):
            if tall_row < 0:
                source, at, low, edge_row = up_ref, place, (tall_row + 2) * STRIP, ROWS + tall_row
            elif tall_row >= ROWS:
                source, at, low, edge_row = down_ref, place, (tall_row - ROWS) * STRIP, tall_row - ROWS
            else:
                source, at, low, edge_row = ref, frame, tall_row * STRIP, tall_row
            line = source[at, pl.ds(low, STRIP), :]
            edge_low = TILE if source is ref else RIM
            edge = source[at, pl.ds(edge_low, EDGES), :].astype(f32)
            places = []
            for row_tap in range(3):
                row = tall_row + 1 - row_tap
                if 0 <= row < ROWS:
                    places.append((row_tap, place * TILE + row * STRIP))
                elif row == -1:
                    places.append((row_tap, FRAMES * TILE + place * RIM))
                elif row == ROWS:
                    places.append((row_tap, FRAMES * TILE + place * RIM + STRIP))
            place_line(
                col_ref,
                line,
                edge[edge_row : edge_row + 1],
                edge[ROWS + edge_row : ROWS + edge_row + 1],
                places,
            )

    @pl.loop(0, 2)
    def _(frame):
        spread(early_ref, frame, frame)

    @pl.loop(0, GROUP)
    def _(frame):
        spread(held_ref, frame, frame + 2)

    for low, step in ((0, TILE), (FRAMES * TILE, RIM)):
        total = None
        for tap in range(3):
            rows = col_ref[low + tap * step : low + (tap + GROUP) * step, :]
            part = jnp.dot(rows, w_ref[tap], preferred_element_type=f32)
            total = part if total is None else total + part
        place = 0 if step == TILE else GROUP * TILE
        lin_ref[place : place + GROUP * step, :] = total

    @pl.loop(0, ROWS)
    def _(row):
        low = pl.multiple_of(row * STRIP, STRIP)
        linear = [lin_ref[pl.ds(frame * TILE + low, STRIP), :] for frame in range(GROUP)]
        gate = [jax.nn.sigmoid(value) for value in linear]
        band = [(value * part).astype(bf16).astype(f32) for value, part in zip(linear, gate)]
        detail = [None] * GROUP
        for level in range(LEVELS):
            step = 1 << level
            following = [None] * GROUP
            for frame in range(0, GROUP, 2 * step):
                lower, upper = band[frame], band[frame + step]
                smooth = (lower + upper) * root_half
                if level < LEVELS - 1:
                    smooth = smooth.astype(bf16).astype(f32)
                change = (upper - lower) * root_half
                following[frame] = smooth
                for member in range(frame, frame + 2 * step, 2):
                    detail[member] = change if level == 0 else detail[member] + change
            band = following
        for member in range(0, GROUP, 2):
            code = (band[0] + band_weight * detail[member]).astype(bf16)
            code_ref[member, pl.ds(low, STRIP), :] = code
            code_ref[member + 1, pl.ds(low, STRIP), :] = code
        place = pl.multiple_of(HELD + lax.rem(row + 1, ROWS) * STRIP, STRIP)
        cot = [held_ref[frame, pl.ds(place, STRIP), :].astype(f32) for frame in range(GROUP)]
        back = adjoint_bands(cot)
        for frame in range(GROUP):
            g_ref[frame, pl.ds(low, STRIP), :] = (
                back[frame] * slope_of(linear[frame], gate[frame])
            ).astype(bf16)

    for offset, source, rim_ref in ((0, up_ref, g_up_ref), (STRIP, down_ref, g_down_ref)):
        cot = [
            source[frame + 2, pl.ds(RIM + EDGES, STRIP), :].astype(f32) for frame in range(GROUP)
        ]
        back = adjoint_bands(cot)
        for frame in range(GROUP):
            linear = lin_ref[pl.ds(GROUP * TILE + frame * RIM + offset, STRIP), :]
            slope = slope_of(linear, jax.nn.sigmoid(linear))
            rim_ref[frame] = (back[frame] * slope).astype(bf16)

    gt_ref[...] = jnp.zeros_like(gt_ref)
    for frame in range(GROUP):
        turned = g_ref[frame].astype(f32).T.astype(bf16)
        for tap in range(3):
            gt_ref[pl.ds(tap * CH, CH), pl.ds((frame + tap) * TILE, TILE)] = turned
    terms_ref[...] = jnp.zeros_like(terms_ref)
    _, peers, ring, share = terms_ref.shape[:4]
    blocks = 27 * CH // PART
    slots = share // PART
    deep = peers // CHIPS[0]
    lines = 2 * deep
    for low in range(0, 9, 2):
        high = min(low + 2, 9)
        product = jnp.dot(
            gt_ref[...],
            col_ref[0 : FRAMES * TILE, low * CH : high * CH],
            preferred_element_type=f32,
        )
        for tap in range(low, high):
            for frame_tap in range(3):
                block = product[
                    frame_tap * CH : (frame_tap + 1) * CH, (tap - low) * CH : (tap - low + 1) * CH
                ].T
                for piece in range(CH // PART):
                    at = (frame_tap * 9 + tap) * (CH // PART) + piece
                    line, within = divmod(at, blocks // lines)
                    owner, slot = divmod(within, slots)
                    depth, core = divmod(line, 2)
                    column, place = divmod(owner, ring)
                    peer = column * deep + depth
                    terms_ref[core, peer, place, pl.ds(slot * PART, PART), :] = block[
                        piece * PART : (piece + 1) * PART
                    ]
    for core in range(2):

        @pl.when(core_ref[0] == core)
        def _():
            for peer in range(peers):
                keep_ref[peer] = terms_ref[core, peer].reshape(-1, CH).astype(bf16)
                send_ref[peer] = terms_ref[1 - core, peer].reshape(-1, CH).astype(bf16)


def backward_body(g_ref, up_ref, down_ref, late_ref, w_ref, out_ref, col_ref, side_ref):
    nothing = jnp.zeros((1, CH), f32)

    def spread(lines, place):
        for tall_row, line in enumerate(lines):
            places = [
                (row_tap, place * TILE + (tall_row - row_tap) * STRIP)
                for row_tap in range(3)
                if 0 <= tall_row - row_tap < ROWS
            ]
            place_line(col_ref, line, nothing, nothing, places)

    @pl.loop(0, GROUP)
    def _(frame):
        rows = [g_ref[frame, pl.ds(row * STRIP, STRIP), :] for row in range(ROWS)]
        spread([up_ref[frame]] + rows + [down_ref[frame]], frame)

    @pl.loop(0, 2)
    def _(frame):
        lines = [late_ref[frame, pl.ds(row * STRIP, STRIP), :] for row in range(TALL)]
        spread(lines, frame + GROUP)

    total = (
        jnp.dot(col_ref[0 : GROUP * TILE, :], w_ref[0], preferred_element_type=f32)
        + jnp.dot(col_ref[TILE : (GROUP + 1) * TILE, :], w_ref[1], preferred_element_type=f32)
        + jnp.dot(col_ref[2 * TILE : (GROUP + 2) * TILE, :], w_ref[2], preferred_element_type=f32)
    )
    for frame in range(GROUP):
        out_ref[frame, 0:TILE, :] = total[frame * TILE : (frame + 1) * TILE].astype(bf16)
    for side, (offset, col_tap) in enumerate(((0, 2), (STRIP - 1, 0))):
        for frame in range(FRAMES):
            for row in range(ROWS):
                at = frame * TILE + row * STRIP + (0 if side == 0 else STRIP - 8)
                for row_tap in range(3):
                    mid = (row_tap * 3 + 1) * CH
                    piece = col_ref[pl.ds(frame * TILE + row * STRIP, STRIP), pl.ds(mid, CH)]
                    one = piece.astype(f32)[offset : offset + 1]
                    side_ref[pl.ds(frame * ROWS + row, 1), pl.ds(row_tap * CH, CH)] = one
        summed = None
        for frame_tap in range(3):
            rows = side_ref[pl.ds(frame_tap * ROWS, GROUP * ROWS), :].astype(bf16)
            for row_tap in range(3):
                tap = row_tap * 3 + col_tap
                part = jnp.dot(
                    rows[:, row_tap * CH : (row_tap + 1) * CH],
                    w_ref[frame_tap, pl.ds(tap * CH, CH), :],
                    preferred_element_type=f32,
                )
                summed = part if summed is None else summed + part
        if side == 0:
            first = summed
    for frame in range(GROUP):
        pair = [value[frame * ROWS : (frame + 1) * ROWS] for value in (first, summed)]
        out_ref[frame, TILE:SENT, :] = jnp.concatenate(pair, axis=0).astype(bf16)


def load_body(parts_ref, sent_ref, code_ref, out_ref):
    ring, share = GROUP, parts_ref.shape[1] // GROUP
    part = parts_ref[0].astype(f32)
    for peer in range(1, parts_ref.shape[0]):
        part = part + parts_ref[peer].astype(f32)
    empty = jnp.zeros((-share % STRIP, CH), f32)
    for place in range(ring):
        piece = part[place * share : (place + 1) * share]
        if empty.shape[0]:
            piece = jnp.concatenate([piece, empty], axis=0)
        out_ref[place, 0 : piece.shape[0], :] = piece.astype(bf16)
        low = piece.shape[0]
        out_ref[place, low : low + TILE, :] = code_ref[place]
        out_ref[place, low + TILE : low + TILE + SENT, :] = sent_ref[place]


def share_body(got_ref, out_ref, norm):
    share = out_ref.shape[1]
    total = got_ref[0].astype(f32)
    for strip in range(1, GROUP):
        total = total + got_ref[strip].astype(f32)
    copies = (total[:share] * norm).astype(bf16)
    for owner in range(out_ref.shape[0]):
        out_ref[owner] = copies


def unpack_body(got_ref, code_ref, grad_ref):
    head = got_ref.shape[1] - TILE - SENT
    code_low, grad_low, edge_low = head, head + TILE, head + 2 * TILE
    at = lax.broadcasted_iota(jnp.int32, (STRIP, CH), 0)
    for strip in range(GROUP):
        columns = pl.ds(strip * STRIP, STRIP)
        if strip > 0:
            before = got_ref[strip - 1, pl.ds(edge_low, EDGES), :].astype(f32)
        if strip < GROUP - 1:
            after = got_ref[strip + 1, pl.ds(edge_low, EDGES), :].astype(f32)
        for row in range(ROWS):
            code_ref[row, columns, :] = got_ref[strip, pl.ds(code_low + row * STRIP, STRIP), :]
            value = got_ref[strip, pl.ds(grad_low + row * STRIP, STRIP), :].astype(f32)
            if strip > 0:
                value = value + jnp.where(at == 0, before[ROWS + row : ROWS + row + 1], 0.0)
            if strip < GROUP - 1:
                value = value + jnp.where(at == STRIP - 1, after[row : row + 1], 0.0)
            grad_ref[row, columns, :] = value.astype(bf16)


def shifted(value, axes, by):
    count = lax.axis_size(axes)
    route = [(i, i + by) for i in range(count) if 0 <= i + by < count]
    return lax.ppermute(value, axes, route)


def swapped(value):
    return lax.ppermute(value, "core", [(0, 1), (1, 0)])


def shards(frames, kernel, cotangent):
    weights = kernel.reshape(3, WIDE, CH)
    turned = jnp.swapaxes(kernel[::-1, ::-1, ::-1], 3, 4).reshape(3, WIDE, CH)
    lines = ("z", "core")
    whole_vmem = pltpu.VMEM((ROWS, GROUP * STRIP, CH), bf16)
    packed = pl.pallas_call(
        pack_body,
        out_shape=jax.ShapeDtypeStruct((GROUP, LOAD, CH), bf16),
        in_specs=[pl.BlockSpec(memory_space=pl.ANY)] * 2,
        scratch_shapes=[whole_vmem] * 2
        + [pltpu.VMEM((GROUP, ROWS, CH), f32)] * 2
        + [pltpu.SemaphoreType.DMA((2,))],
    )(frames[0], cotangent[0])
    held = lax.all_to_all(packed, "y", 0, 0)
    early = shifted(held[GROUP - 2 :, : HELD + 2 * STRIP], "x", 1)

    def edge_rows(*places):
        pieces = [
            jnp.concatenate([early[:, low:high], held[:, low:high]], axis=0)
            for low, high in places
        ]
        return pieces[0] if len(pieces) == 1 else jnp.concatenate(pieces, axis=1)

    up = shifted(edge_rows((TILE - RIM, HELD + STRIP)), lines, 1)
    down = shifted(edge_rows((0, RIM), (TILE, HELD), (HELD + STRIP, HELD + 2 * STRIP)), lines, -1)

    devices = lax.axis_size(("x", "y", "z", "core"))
    peers, owners = lax.axis_size(("x", "z")), lax.axis_size(("x", "y"))
    share = PART * -(-27 * CH // (PART * devices))
    mail = jax.ShapeDtypeStruct((peers, GROUP * share, CH), bf16)
    flops = 2 * GROUP * TILE * 27 * CH * CH
    code, g, g_up, g_down, keep, send = kernel_call(
        forward_body,
        (
            jax.ShapeDtypeStruct((GROUP, TILE, CH), bf16),
            jax.ShapeDtypeStruct((GROUP, TILE, CH), bf16),
            jax.ShapeDtypeStruct((GROUP, STRIP, CH), bf16),
            jax.ShapeDtypeStruct((GROUP, STRIP, CH), bf16),
            mail,
            mail,
        ),
        [
            pltpu.VMEM((FRAMES * (TILE + RIM), WIDE), bf16),
            pltpu.VMEM((GROUP * (TILE + RIM), CH), f32),
            pltpu.VMEM((3 * CH, FRAMES * TILE), bf16),
            pltpu.VMEM((2, peers, GROUP, share, CH), f32),
        ],
        flops=2 * flops,
        in_specs=[pl.BlockSpec(memory_space=pltpu.SMEM)]
        + [pl.BlockSpec(memory_space=pltpu.VMEM)] * 5,
    )(lax.axis_index("core").astype(jnp.int32).reshape(1), held, early, up, down, weights)

    chip_sum = (keep.astype(f32) + swapped(send).astype(f32)).astype(bf16)
    parts = lax.all_to_all(chip_sum, ("x", "z"), 0, 0)
    late = shifted(jnp.concatenate([g_up[:2], g[:2], g_down[:2]], axis=1), "x", -1)
    sent = kernel_call(
        backward_body,
        jax.ShapeDtypeStruct((GROUP, SENT, CH), bf16),
        [
            pltpu.VMEM((FRAMES * TILE, WIDE), bf16),
            pltpu.VMEM((FRAMES * ROWS, 3 * CH), f32),
        ],
        flops=flops,
    )(g, g_up, g_down, late, turned)
    head = STRIP * -(-share // STRIP)
    load = kernel_call(
        load_body, jax.ShapeDtypeStruct((GROUP, head + TILE + SENT, CH), bf16)
    )(parts, sent, code)
    got = lax.all_to_all(load, "y", 0, 0)
    norm = 1.0 / math.sqrt(devices * GROUP * TILE)
    copies = kernel_call(
        functools.partial(share_body, norm=norm),
        jax.ShapeDtypeStruct((owners, share, CH), bf16),
    )(got[:, :head])
    line = lax.all_to_all(copies, ("x", "y"), 0, 0).reshape(-1, CH)
    line = line[: 27 * CH // lax.axis_size(lines)]
    grad_kernel = lax.all_gather(line, lines, tiled=True).astype(f32)

    whole = jax.ShapeDtypeStruct((ROWS, GROUP * STRIP, CH), bf16)
    code_out, grad_frames = kernel_call(unpack_body, (whole, whole))(got)
    return (code_out[None], grad_frames[None], grad_kernel.reshape(3, 3, 3, CH, CH))


def solution(mesh):
    split = Mesh(mesh.devices.reshape(CHIPS), ("x", "y", "z", "core"))
    block = P(("x", "y"), ("z", "core"), None, None)
    return jax.shard_map(
        shards,
        mesh=split,
        in_specs=(block, P(), block),
        out_specs=(block, block, P()),
        check_vma=False,
    )
```

```python
import functools
import math

import jax
import jax.numpy as jnp
from jax import lax
from jax.experimental import pallas as pl
from jax.experimental.pallas import tpu as pltpu
from jax.sharding import Mesh
from jax.sharding import PartitionSpec as P

CHIPS = (4, 8, 8, 2)
LEVELS = 3
GROUP = 1 << LEVELS
ROWS = 8
STRIP = 16
TILE = ROWS * STRIP
TALL = ROWS + 2
CH = 128
WIDE = 9 * CH
FRAMES = GROUP + 2
EDGES = 2 * ROWS
HELD = TILE + EDGES
LOAD = HELD + TILE
SENT = TILE + EDGES
RIM = 2 * STRIP
PART = 8

band_weight = 0.75
root_half = 0.7071067811865476
f32 = jnp.float32
bf16 = jnp.bfloat16
VMEM_LIMIT = 48 * 1024 * 1024


def kernel_call(body, outs, scratch=(), flops=0, **specs):
    return pl.pallas_call(
        body,
        **specs,
        out_shape=outs,
        scratch_shapes=list(scratch),
        compiler_params=pltpu.CompilerParams(vmem_limit_bytes=VMEM_LIMIT),
        cost_estimate=pl.CostEstimate(flops=flops, bytes_accessed=4 << 20, transcendentals=0),
    )


def pack_body(x_hbm, cot_hbm, out_ref, left_ref, right_ref, sems):
    copies = [
        pltpu.make_async_copy(
            hbm.at[row], out_ref.at[:, pl.ds(place(row), STRIP), :], sems.at[side, row]
        )
        for side, (hbm, place) in enumerate(((x_hbm, x_place), (cot_hbm, cot_place)))
        for row in range(ROWS)
    ]
    for copy in copies:
        copy.start()
    left_ref[...] = jnp.zeros_like(left_ref)
    right_ref[...] = jnp.zeros_like(right_ref)
    for row in range(ROWS):
        copies[row].wait()
        for strip in range(GROUP):
            wide = out_ref[strip, pl.ds(x_place(row), STRIP), :].astype(f32)
            if strip < GROUP - 1:
                left_ref[strip + 1, pl.ds(row, 1), :] = wide[STRIP - 1 : STRIP]
            if strip > 0:
                right_ref[strip - 1, pl.ds(row, 1), :] = wide[0:1]
    for strip in range(GROUP):
        pair = jnp.concatenate([left_ref[strip], right_ref[strip]], axis=0)
        out_ref[strip, pl.ds(TILE, EDGES), :] = pair.astype(bf16)
    for copy in copies[ROWS:]:
        copy.wait()


def x_place(row):
    return row * STRIP


def cot_place(row):
    return HELD + (row + 1) % ROWS * STRIP


def place_line(col_ref, line, left, right, places):
    at = lax.broadcasted_iota(jnp.int32, (STRIP, CH), 0)
    wide = line.astype(f32)
    before = jnp.where(at == 0, left, pltpu.roll(wide, 1, 0)).astype(bf16)
    after = jnp.where(at == STRIP - 1, right, pltpu.roll(wide, STRIP - 1, 0)).astype(bf16)
    for row_tap, place in places:
        start = pl.multiple_of(place, STRIP)
        for col_tap, piece in enumerate((before, line, after)):
            tap = row_tap * 3 + col_tap
            col_ref[pl.ds(start, STRIP), pl.ds(tap * CH, CH)] = piece


def adjoint_bands(cot):
    back = [None] * GROUP
    for level in range(LEVELS - 1, -1, -1):
        step = 1 << level
        following = [None] * GROUP
        for frame in range(GROUP):
            if frame & step:
                continue
            pair = (cot[frame] + cot[frame + step]) * root_half
            if level == LEVELS - 1:
                total = pair
            else:
                total = (back[frame] + back[frame + step]) * root_half
            for member, side in ((frame, -1.0), (frame + step, 1.0)):
                value = total + (band_weight * side) * pair
                if level > 0:
                    value = value.astype(bf16).astype(f32)
                following[member] = value
        back = following
    return back


def slope_of(linear, gate):
    return gate * (1.0 + linear * (1.0 - gate))


def forward_body(
    core_ref,
    held_ref,
    early_ref,
    up_ref,
    down_ref,
    w_ref,
    code_ref,
    g_ref,
    g_up_ref,
    g_down_ref,
    keep_ref,
    send_ref,
    col_ref,
    lin_ref,
    gt_ref,
    terms_ref,
):
    def spread(ref, frame, place):
        for tall_row in range(-2, ROWS + 2):
            if tall_row < 0:
                source, at, low, edge_row = up_ref, place, (tall_row + 2) * STRIP, ROWS + tall_row
            elif tall_row >= ROWS:
                source, at, low, edge_row = down_ref, place, (tall_row - ROWS) * STRIP, tall_row - ROWS
            else:
                source, at, low, edge_row = ref, frame, tall_row * STRIP, tall_row
            line = source[at, pl.ds(low, STRIP), :]
            edge_low = TILE if source is ref else RIM
            edge = source[at, pl.ds(edge_low, EDGES), :].astype(f32)
            places = []
            for row_tap in range(3):
                row = tall_row + 1 - row_tap
                if 0 <= row < ROWS:
                    places.append((row_tap, place * TILE + row * STRIP))
                elif row == -1:
                    places.append((row_tap, FRAMES * TILE + place * RIM))
                elif row == ROWS:
                    places.append((row_tap, FRAMES * TILE + place * RIM + STRIP))
            place_line(
                col_ref,
                line,
                edge[edge_row : edge_row + 1],
                edge[ROWS + edge_row : ROWS + edge_row + 1],
                places,
            )

    @pl.loop(0, 2)
    def _(frame):
        spread(early_ref, frame, frame)

    @pl.loop(0, GROUP)
    def _(frame):
        spread(held_ref, frame, frame + 2)

    for low, step in ((0, TILE), (FRAMES * TILE, RIM)):
        total = None
        for tap in range(3):
            rows = col_ref[low + tap * step : low + (tap + GROUP) * step, :]
            part = jnp.dot(rows, w_ref[tap], preferred_element_type=f32)
            total = part if total is None else total + part
        place = 0 if step == TILE else GROUP * TILE
        lin_ref[place : place + GROUP * step, :] = total

    @pl.loop(0, ROWS)
    def _(row):
        low = pl.multiple_of(row * STRIP, STRIP)
        linear = [lin_ref[pl.ds(frame * TILE + low, STRIP), :] for frame in range(GROUP)]
        gate = [jax.nn.sigmoid(value) for value in linear]
        band = [(value * part).astype(bf16).astype(f32) for value, part in zip(linear, gate)]
        detail = [None] * GROUP
        for level in range(LEVELS):
            step = 1 << level
            following = [None] * GROUP
            for frame in range(0, GROUP, 2 * step):
                lower, upper = band[frame], band[frame + step]
                smooth = (lower + upper) * root_half
                if level < LEVELS - 1:
                    smooth = smooth.astype(bf16).astype(f32)
                change = (upper - lower) * root_half
                following[frame] = smooth
                for member in range(frame, frame + 2 * step, 2):
                    detail[member] = change if level == 0 else detail[member] + change
            band = following
        for member in range(0, GROUP, 2):
            code = (band[0] + band_weight * detail[member]).astype(bf16)
            code_ref[member, pl.ds(low, STRIP), :] = code
            code_ref[member + 1, pl.ds(low, STRIP), :] = code
        place = pl.multiple_of(HELD + lax.rem(row + 1, ROWS) * STRIP, STRIP)
        cot = [held_ref[frame, pl.ds(place, STRIP), :].astype(f32) for frame in range(GROUP)]
        back = adjoint_bands(cot)
        for frame in range(GROUP):
            g_ref[frame, pl.ds(low, STRIP), :] = (
                back[frame] * slope_of(linear[frame], gate[frame])
            ).astype(bf16)

    for offset, source, rim_ref in ((0, up_ref, g_up_ref), (STRIP, down_ref, g_down_ref)):
        cot = [
            source[frame + 2, pl.ds(RIM + EDGES, STRIP), :].astype(f32) for frame in range(GROUP)
        ]
        back = adjoint_bands(cot)
        for frame in range(GROUP):
            linear = lin_ref[pl.ds(GROUP * TILE + frame * RIM + offset, STRIP), :]
            slope = slope_of(linear, jax.nn.sigmoid(linear))
            rim_ref[frame] = (back[frame] * slope).astype(bf16)

    gt_ref[...] = jnp.zeros_like(gt_ref)
    for frame in range(GROUP):
        turned = g_ref[frame].astype(f32).T.astype(bf16)
        for tap in range(3):
            gt_ref[pl.ds(tap * CH, CH), pl.ds((frame + tap) * TILE, TILE)] = turned
    _, peers, ring, share = terms_ref.shape[:4]
    blocks = 27 * CH // PART
    slots = share // PART
    deep = peers // CHIPS[0]
    lines = 2 * deep
    unused = terms_ref.at[:, peers - deep :]
    unused[...] = jnp.zeros_like(unused)
    for low in range(0, 9, 2):
        high = min(low + 2, 9)
        product = jnp.dot(
            gt_ref[...],
            col_ref[0 : FRAMES * TILE, low * CH : high * CH],
            preferred_element_type=f32,
        )
        for tap in range(low, high):
            for frame_tap in range(3):
                block = product[
                    frame_tap * CH : (frame_tap + 1) * CH, (tap - low) * CH : (tap - low + 1) * CH
                ].T
                for piece in range(CH // PART):
                    at = (frame_tap * 9 + tap) * (CH // PART) + piece
                    line, within = divmod(at, blocks // lines)
                    owner, slot = divmod(within, slots)
                    depth, core = divmod(line, 2)
                    column, place = divmod(owner, ring)
                    peer = column * deep + depth
                    terms_ref[core, peer, place, pl.ds(slot * PART, PART), :] = block[
                        piece * PART : (piece + 1) * PART
                    ]
    for core in range(2):

        @pl.when(core_ref[0] == core)
        def _():
            for peer in range(peers):
                keep_ref[peer] = terms_ref[core, peer].reshape(-1, CH).astype(bf16)
                send_ref[peer] = terms_ref[1 - core, peer].reshape(-1, CH).astype(bf16)


def backward_body(g_ref, up_ref, down_ref, late_ref, w_ref, out_ref, col_ref, side_ref):
    nothing = jnp.zeros((1, CH), f32)

    def spread(lines, place):
        for tall_row, line in enumerate(lines):
            places = [
                (row_tap, place * TILE + (tall_row - row_tap) * STRIP)
                for row_tap in range(3)
                if 0 <= tall_row - row_tap < ROWS
            ]
            place_line(col_ref, line, nothing, nothing, places)

    @pl.loop(0, GROUP)
    def _(frame):
        rows = [g_ref[frame, pl.ds(row * STRIP, STRIP), :] for row in range(ROWS)]
        spread([up_ref[frame]] + rows + [down_ref[frame]], frame)

    @pl.loop(0, 2)
    def _(frame):
        lines = [late_ref[frame, pl.ds(row * STRIP, STRIP), :] for row in range(TALL)]
        spread(lines, frame + GROUP)

    total = (
        jnp.dot(col_ref[0 : GROUP * TILE, :], w_ref[0], preferred_element_type=f32)
        + jnp.dot(col_ref[TILE : (GROUP + 1) * TILE, :], w_ref[1], preferred_element_type=f32)
        + jnp.dot(col_ref[2 * TILE : (GROUP + 2) * TILE, :], w_ref[2], preferred_element_type=f32)
    )
    for frame in range(GROUP):
        out_ref[frame, 0:TILE, :] = total[frame * TILE : (frame + 1) * TILE].astype(bf16)
    for side, (offset, col_tap) in enumerate(((0, 2), (STRIP - 1, 0))):
        for frame in range(FRAMES):
            for row in range(ROWS):
                at = frame * TILE + row * STRIP + (0 if side == 0 else STRIP - 8)
                for row_tap in range(3):
                    mid = (row_tap * 3 + 1) * CH
                    piece = col_ref[pl.ds(frame * TILE + row * STRIP, STRIP), pl.ds(mid, CH)]
                    one = piece.astype(f32)[offset : offset + 1]
                    side_ref[pl.ds(frame * ROWS + row, 1), pl.ds(row_tap * CH, CH)] = one
        summed = None
        for frame_tap in range(3):
            rows = side_ref[pl.ds(frame_tap * ROWS, GROUP * ROWS), :].astype(bf16)
            for row_tap in range(3):
                tap = row_tap * 3 + col_tap
                part = jnp.dot(
                    rows[:, row_tap * CH : (row_tap + 1) * CH],
                    w_ref[frame_tap, pl.ds(tap * CH, CH), :],
                    preferred_element_type=f32,
                )
                summed = part if summed is None else summed + part
        if side == 0:
            first = summed
    for frame in range(GROUP):
        pair = [value[frame * ROWS : (frame + 1) * ROWS] for value in (first, summed)]
        out_ref[frame, TILE:SENT, :] = jnp.concatenate(pair, axis=0).astype(bf16)


def load_body(parts_ref, sent_ref, code_ref, out_ref):
    part = parts_ref[0].astype(f32)
    for peer in range(1, parts_ref.shape[0]):
        part = part + parts_ref[peer].astype(f32)
    part = part.astype(bf16)
    low = part.shape[0]
    for place in range(GROUP):
        out_ref[place, 0:low, :] = part
        out_ref[place, low : low + TILE, :] = code_ref[place]
        out_ref[place, low + TILE : low + TILE + SENT, :] = sent_ref[place]


def share_body(got_ref, out_ref, norm):
    rows = out_ref.shape[1]
    total = got_ref[0, 0:rows, :].astype(f32)
    for strip in range(1, GROUP):
        total = total + got_ref[strip, 0:rows, :].astype(f32)
    copies = (total * norm).astype(bf16)
    for owner in range(out_ref.shape[0]):
        out_ref[owner] = copies


def unpack_body(got_ref, code_ref, grad_ref):
    head = got_ref.shape[1] - TILE - SENT
    code_low, grad_low, edge_low = head, head + TILE, head + 2 * TILE
    at = lax.broadcasted_iota(jnp.int32, (STRIP, CH), 0)
    for strip in range(GROUP):
        columns = pl.ds(strip * STRIP, STRIP)
        if strip > 0:
            before = got_ref[strip - 1, pl.ds(edge_low, EDGES), :].astype(f32)
        if strip < GROUP - 1:
            after = got_ref[strip + 1, pl.ds(edge_low, EDGES), :].astype(f32)
        for row in range(ROWS):
            code_ref[row, columns, :] = got_ref[strip, pl.ds(code_low + row * STRIP, STRIP), :]
            value = got_ref[strip, pl.ds(grad_low + row * STRIP, STRIP), :].astype(f32)
            if strip > 0:
                value = value + jnp.where(at == 0, before[ROWS + row : ROWS + row + 1], 0.0)
            if strip < GROUP - 1:
                value = value + jnp.where(at == STRIP - 1, after[row : row + 1], 0.0)
            grad_ref[row, columns, :] = value.astype(bf16)


def shifted(value, axes, by):
    count = lax.axis_size(axes)
    route = [(i, i + by) for i in range(count) if 0 <= i + by < count]
    return lax.ppermute(value, axes, route)


def swapped(value):
    return lax.ppermute(value, "core", [(0, 1), (1, 0)])


def shards(frames, kernel, cotangent):
    weights = kernel.reshape(3, WIDE, CH)
    turned = jnp.swapaxes(kernel[::-1, ::-1, ::-1], 3, 4).reshape(3, WIDE, CH)
    lines = ("z", "core")
    packed = pl.pallas_call(
        pack_body,
        out_shape=jax.ShapeDtypeStruct((GROUP, LOAD, CH), bf16),
        in_specs=[pl.BlockSpec(memory_space=pl.ANY)] * 2,
        scratch_shapes=[pltpu.VMEM((GROUP, ROWS, CH), f32)] * 2
        + [pltpu.SemaphoreType.DMA((2, ROWS))],
    )(frames.reshape(ROWS, GROUP, STRIP, CH), cotangent.reshape(ROWS, GROUP, STRIP, CH))
    held = lax.all_to_all(packed, "y", 0, 0)
    early = shifted(held[GROUP - 2 :, : HELD + 2 * STRIP], "x", 1)

    def edge_rows(*places):
        pieces = [
            jnp.concatenate([early[:, low:high], held[:, low:high]], axis=0)
            for low, high in places
        ]
        return pieces[0] if len(pieces) == 1 else jnp.concatenate(pieces, axis=1)

    up = shifted(edge_rows((TILE - RIM, HELD + STRIP)), lines, 1)
    down = shifted(edge_rows((0, RIM), (TILE, HELD), (HELD + STRIP, HELD + 2 * STRIP)), lines, -1)

    devices = lax.axis_size(("x", "y", "z", "core"))
    peers, wide = lax.axis_size(("x", "z")), lax.axis_size("x")
    share = PART * -(-27 * CH // (PART * devices))
    mail = jax.ShapeDtypeStruct((peers, GROUP * share, CH), bf16)
    flops = 2 * GROUP * TILE * 27 * CH * CH
    code, g, g_up, g_down, keep, send = kernel_call(
        forward_body,
        (
            jax.ShapeDtypeStruct((GROUP, TILE, CH), bf16),
            jax.ShapeDtypeStruct((GROUP, TILE, CH), bf16),
            jax.ShapeDtypeStruct((GROUP, STRIP, CH), bf16),
            jax.ShapeDtypeStruct((GROUP, STRIP, CH), bf16),
            mail,
            mail,
        ),
        [
            pltpu.VMEM((FRAMES * (TILE + RIM), WIDE), bf16),
            pltpu.VMEM((GROUP * (TILE + RIM), CH), f32),
            pltpu.VMEM((3 * CH, FRAMES * TILE), bf16),
            pltpu.VMEM((2, peers, GROUP, share, CH), f32),
        ],
        flops=2 * flops,
        in_specs=[pl.BlockSpec(memory_space=pltpu.SMEM)]
        + [pl.BlockSpec(memory_space=pltpu.VMEM)] * 5,
    )(lax.axis_index("core").astype(jnp.int32).reshape(1), held, early, up, down, weights)

    chip_sum = (keep.astype(f32) + swapped(send).astype(f32)).astype(bf16)
    parts = lax.all_to_all(chip_sum, ("x", "z"), 0, 0)
    late = shifted(jnp.concatenate([g_up[:2], g[:2], g_down[:2]], axis=1), "x", -1)
    sent = kernel_call(
        backward_body,
        jax.ShapeDtypeStruct((GROUP, SENT, CH), bf16),
        [
            pltpu.VMEM((FRAMES * TILE, WIDE), bf16),
            pltpu.VMEM((FRAMES * ROWS, 3 * CH), f32),
        ],
        flops=flops,
    )(g, g_up, g_down, late, turned)
    head = GROUP * share
    load = kernel_call(
        load_body, jax.ShapeDtypeStruct((GROUP, head + TILE + SENT, CH), bf16)
    )(parts, sent, code)
    got = lax.all_to_all(load, "y", 0, 0)
    norm = 1.0 / math.sqrt(devices * GROUP * TILE)
    copies = kernel_call(
        functools.partial(share_body, norm=norm),
        jax.ShapeDtypeStruct((wide, head, CH), bf16),
    )(got)
    line = lax.all_to_all(copies, "x", 0, 0).reshape(-1, CH)
    line = line[: 27 * CH // lax.axis_size(lines)]
    grad_kernel = lax.all_gather(line, lines, tiled=True).astype(f32)

    whole = jax.ShapeDtypeStruct((ROWS, GROUP * STRIP, CH), bf16)
    code_out, grad_frames = kernel_call(unpack_body, (whole, whole))(got)
    return (code_out[None], grad_frames[None], grad_kernel.reshape(3, 3, 3, CH, CH))


def solution(mesh):
    split = Mesh(mesh.devices.reshape(CHIPS), ("x", "y", "z", "core"))
    block = P(("x", "y"), ("z", "core"), None, None)
    return jax.shard_map(
        shards,
        mesh=split,
        in_specs=(block, P(), block),
        out_specs=(block, block, P()),
        check_vma=False,
    )
```

```python
import functools
import math

import jax
import jax.numpy as jnp
from jax import lax
from jax.experimental import pallas as pl
from jax.experimental.pallas import tpu as pltpu
from jax.sharding import Mesh
from jax.sharding import PartitionSpec as P

CHIPS = (4, 8, 8, 2)
LEVELS = 3
GROUP = 1 << LEVELS
ROWS = 8
STRIP = 16
TILE = ROWS * STRIP
TALL = ROWS + 2
CH = 128
WIDE = 9 * CH
FRAMES = GROUP + 2
EDGES = 2 * ROWS
HELD = TILE + EDGES
LOAD = HELD + TILE
SENT = 2 * TILE + EDGES
RIM = 2 * STRIP
PART = 8

band_weight = 0.75
root_half = 0.7071067811865476
f32 = jnp.float32
bf16 = jnp.bfloat16
VMEM_LIMIT = 48 * 1024 * 1024


def kernel_call(body, outs, scratch=(), flops=0, **specs):
    return pl.pallas_call(
        body,
        **specs,
        out_shape=outs,
        scratch_shapes=list(scratch),
        compiler_params=pltpu.CompilerParams(vmem_limit_bytes=VMEM_LIMIT),
        cost_estimate=pl.CostEstimate(flops=flops, bytes_accessed=4 << 20, transcendentals=0),
    )


def pack_body(x_hbm, cot_hbm, out_ref, left_ref, right_ref, sems):
    copies = [
        pltpu.make_async_copy(
            hbm.at[row], out_ref.at[:, pl.ds(place(row), STRIP), :], sems.at[side, row]
        )
        for side, (hbm, place) in enumerate(((x_hbm, x_place), (cot_hbm, cot_place)))
        for row in range(ROWS)
    ]
    for copy in copies:
        copy.start()
    left_ref[...] = jnp.zeros_like(left_ref)
    right_ref[...] = jnp.zeros_like(right_ref)
    for row in range(ROWS):
        copies[row].wait()
        for strip in range(GROUP):
            wide = out_ref[strip, pl.ds(x_place(row), STRIP), :].astype(f32)
            if strip < GROUP - 1:
                left_ref[strip + 1, pl.ds(row, 1), :] = wide[STRIP - 1 : STRIP]
            if strip > 0:
                right_ref[strip - 1, pl.ds(row, 1), :] = wide[0:1]
    for strip in range(GROUP):
        pair = jnp.concatenate([left_ref[strip], right_ref[strip]], axis=0)
        out_ref[strip, pl.ds(TILE, EDGES), :] = pair.astype(bf16)
    for copy in copies[ROWS:]:
        copy.wait()


def x_place(row):
    return row * STRIP


def cot_place(row):
    return HELD + (row + 1) % ROWS * STRIP


def place_line(col_ref, line, left, right, places):
    at = lax.broadcasted_iota(jnp.int32, (STRIP, CH), 0)
    wide = line.astype(f32)
    before = jnp.where(at == 0, left, pltpu.roll(wide, 1, 0)).astype(bf16)
    after = jnp.where(at == STRIP - 1, right, pltpu.roll(wide, STRIP - 1, 0)).astype(bf16)
    for row_tap, place in places:
        start = pl.multiple_of(place, STRIP)
        for col_tap, piece in enumerate((before, line, after)):
            tap = row_tap * 3 + col_tap
            col_ref[pl.ds(start, STRIP), pl.ds(tap * CH, CH)] = piece


def adjoint_bands(cot):
    back = [None] * GROUP
    for level in range(LEVELS - 1, -1, -1):
        step = 1 << level
        following = [None] * GROUP
        for frame in range(GROUP):
            if frame & step:
                continue
            pair = (cot[frame] + cot[frame + step]) * root_half
            if level == LEVELS - 1:
                total = pair
            else:
                total = (back[frame] + back[frame + step]) * root_half
            for member, side in ((frame, -1.0), (frame + step, 1.0)):
                value = total + (band_weight * side) * pair
                if level > 0:
                    value = value.astype(bf16).astype(f32)
                following[member] = value
        back = following
    return back


def slope_of(linear, gate):
    return gate * (1.0 + linear * (1.0 - gate))


def forward_body(
    core_ref,
    held_ref,
    early_ref,
    up_ref,
    down_ref,
    w_ref,
    code_ref,
    g_ref,
    g_up_ref,
    g_down_ref,
    keep_ref,
    send_ref,
    col_ref,
    lin_ref,
    gt_ref,
    terms_ref,
):
    def spread(ref, frame, place):
        for tall_row in range(-2, ROWS + 2):
            if tall_row < 0:
                source, at, low, edge_row = up_ref, place, (tall_row + 2) * STRIP, ROWS + tall_row
            elif tall_row >= ROWS:
                source, at, low, edge_row = down_ref, place, (tall_row - ROWS) * STRIP, tall_row - ROWS
            else:
                source, at, low, edge_row = ref, frame, tall_row * STRIP, tall_row
            line = source[at, pl.ds(low, STRIP), :]
            edge_low = TILE if source is ref else RIM
            edge = source[at, pl.ds(edge_low, EDGES), :].astype(f32)
            places = []
            for row_tap in range(3):
                row = tall_row + 1 - row_tap
                if 0 <= row < ROWS:
                    places.append((row_tap, place * TILE + row * STRIP))
                elif row == -1:
                    places.append((row_tap, FRAMES * TILE + place * RIM))
                elif row == ROWS:
                    places.append((row_tap, FRAMES * TILE + place * RIM + STRIP))
            place_line(
                col_ref,
                line,
                edge[edge_row : edge_row + 1],
                edge[ROWS + edge_row : ROWS + edge_row + 1],
                places,
            )

    @pl.loop(0, 2)
    def _(frame):
        spread(early_ref, frame, frame)

    @pl.loop(0, GROUP)
    def _(frame):
        spread(held_ref, frame, frame + 2)

    for low, step in ((0, TILE), (FRAMES * TILE, RIM)):
        total = None
        for tap in range(3):
            rows = col_ref[low + tap * step : low + (tap + GROUP) * step, :]
            part = jnp.dot(rows, w_ref[tap], preferred_element_type=f32)
            total = part if total is None else total + part
        place = 0 if step == TILE else GROUP * TILE
        lin_ref[place : place + GROUP * step, :] = total

    @pl.loop(0, ROWS)
    def _(row):
        low = pl.multiple_of(row * STRIP, STRIP)
        linear = [lin_ref[pl.ds(frame * TILE + low, STRIP), :] for frame in range(GROUP)]
        gate = [jax.nn.sigmoid(value) for value in linear]
        band = [(value * part).astype(bf16).astype(f32) for value, part in zip(linear, gate)]
        detail = [None] * GROUP
        for level in range(LEVELS):
            step = 1 << level
            following = [None] * GROUP
            for frame in range(0, GROUP, 2 * step):
                lower, upper = band[frame], band[frame + step]
                smooth = (lower + upper) * root_half
                if level < LEVELS - 1:
                    smooth = smooth.astype(bf16).astype(f32)
                change = (upper - lower) * root_half
                following[frame] = smooth
                for member in range(frame, frame + 2 * step, 2):
                    detail[member] = change if level == 0 else detail[member] + change
            band = following
        for member in range(0, GROUP, 2):
            code = (band[0] + band_weight * detail[member]).astype(bf16)
            code_ref[member, pl.ds(low, STRIP), :] = code
            code_ref[member + 1, pl.ds(low, STRIP), :] = code
        place = pl.multiple_of(HELD + lax.rem(row + 1, ROWS) * STRIP, STRIP)
        cot = [held_ref[frame, pl.ds(place, STRIP), :].astype(f32) for frame in range(GROUP)]
        back = adjoint_bands(cot)
        for frame in range(GROUP):
            g_ref[frame, pl.ds(low, STRIP), :] = (
                back[frame] * slope_of(linear[frame], gate[frame])
            ).astype(bf16)

    for offset, source, rim_ref in ((0, up_ref, g_up_ref), (STRIP, down_ref, g_down_ref)):
        cot = [
            source[frame + 2, pl.ds(RIM + EDGES, STRIP), :].astype(f32) for frame in range(GROUP)
        ]
        back = adjoint_bands(cot)
        for frame in range(GROUP):
            linear = lin_ref[pl.ds(GROUP * TILE + frame * RIM + offset, STRIP), :]
            slope = slope_of(linear, jax.nn.sigmoid(linear))
            rim_ref[frame] = (back[frame] * slope).astype(bf16)

    gt_ref[...] = jnp.zeros_like(gt_ref)
    for frame in range(GROUP):
        turned = g_ref[frame].astype(f32).T.astype(bf16)
        for tap in range(3):
            gt_ref[pl.ds(tap * CH, CH), pl.ds((frame + tap) * TILE, TILE)] = turned
    _, peers, ring, share = terms_ref.shape[:4]
    blocks = 27 * CH // PART
    slots = share // PART
    deep = peers // CHIPS[0]
    lines = 2 * deep
    unused = terms_ref.at[:, peers - deep :]
    unused[...] = jnp.zeros_like(unused)
    for low in range(0, 9, 2):
        high = min(low + 2, 9)
        product = jnp.dot(
            gt_ref[...],
            col_ref[0 : FRAMES * TILE, low * CH : high * CH],
            preferred_element_type=f32,
        )
        for tap in range(low, high):
            for frame_tap in range(3):
                block = product[
                    frame_tap * CH : (frame_tap + 1) * CH, (tap - low) * CH : (tap - low + 1) * CH
                ].T
                for piece in range(CH // PART):
                    at = (frame_tap * 9 + tap) * (CH // PART) + piece
                    line, within = divmod(at, blocks // lines)
                    owner, slot = divmod(within, slots)
                    depth, core = divmod(line, 2)
                    column, place = divmod(owner, ring)
                    peer = column * deep + depth
                    terms_ref[core, peer, place, pl.ds(slot * PART, PART), :] = block[
                        piece * PART : (piece + 1) * PART
                    ]
    for core in range(2):

        @pl.when(core_ref[0] == core)
        def _():
            for peer in range(peers):
                keep_ref[peer] = terms_ref[core, peer].reshape(-1, CH).astype(bf16)
                send_ref[peer] = terms_ref[1 - core, peer].reshape(-1, CH).astype(bf16)


def backward_body(g_ref, up_ref, down_ref, late_ref, code_ref, w_ref, out_ref, col_ref, side_ref):
    nothing = jnp.zeros((1, CH), f32)

    def spread(lines, place):
        for tall_row, line in enumerate(lines):
            places = [
                (row_tap, place * TILE + (tall_row - row_tap) * STRIP)
                for row_tap in range(3)
                if 0 <= tall_row - row_tap < ROWS
            ]
            place_line(col_ref, line, nothing, nothing, places)

    @pl.loop(0, GROUP)
    def _(frame):
        rows = [g_ref[frame, pl.ds(row * STRIP, STRIP), :] for row in range(ROWS)]
        spread([up_ref[frame]] + rows + [down_ref[frame]], frame)

    @pl.loop(0, 2)
    def _(frame):
        lines = [late_ref[frame, pl.ds(row * STRIP, STRIP), :] for row in range(TALL)]
        spread(lines, frame + GROUP)

    total = (
        jnp.dot(col_ref[0 : GROUP * TILE, :], w_ref[0], preferred_element_type=f32)
        + jnp.dot(col_ref[TILE : (GROUP + 1) * TILE, :], w_ref[1], preferred_element_type=f32)
        + jnp.dot(col_ref[2 * TILE : (GROUP + 2) * TILE, :], w_ref[2], preferred_element_type=f32)
    )
    for frame in range(GROUP):
        out_ref[frame, 0:TILE, :] = code_ref[frame]
        out_ref[frame, TILE : 2 * TILE, :] = total[frame * TILE : (frame + 1) * TILE].astype(bf16)
    for side, (offset, col_tap) in enumerate(((0, 2), (STRIP - 1, 0))):
        for frame in range(FRAMES):
            for row in range(ROWS):
                at = frame * TILE + row * STRIP + (0 if side == 0 else STRIP - 8)
                for row_tap in range(3):
                    mid = (row_tap * 3 + 1) * CH
                    piece = col_ref[pl.ds(frame * TILE + row * STRIP, STRIP), pl.ds(mid, CH)]
                    one = piece.astype(f32)[offset : offset + 1]
                    side_ref[pl.ds(frame * ROWS + row, 1), pl.ds(row_tap * CH, CH)] = one
        summed = None
        for frame_tap in range(3):
            rows = side_ref[pl.ds(frame_tap * ROWS, GROUP * ROWS), :].astype(bf16)
            for row_tap in range(3):
                tap = row_tap * 3 + col_tap
                part = jnp.dot(
                    rows[:, row_tap * CH : (row_tap + 1) * CH],
                    w_ref[frame_tap, pl.ds(tap * CH, CH), :],
                    preferred_element_type=f32,
                )
                summed = part if summed is None else summed + part
        if side == 0:
            first = summed
    for frame in range(GROUP):
        pair = [value[frame * ROWS : (frame + 1) * ROWS] for value in (first, summed)]
        out_ref[frame, 2 * TILE : SENT, :] = jnp.concatenate(pair, axis=0).astype(bf16)


def part_body(parts_ref, out_ref):
    part = parts_ref[0].astype(f32)
    for peer in range(1, parts_ref.shape[0]):
        part = part + parts_ref[peer].astype(f32)
    part = part.astype(bf16)
    for place in range(out_ref.shape[0]):
        out_ref[place] = part


def share_body(got_ref, out_ref, norm):
    total = got_ref[0].astype(f32)
    for place in range(1, got_ref.shape[0]):
        total = total + got_ref[place].astype(f32)
    copies = (total * norm).astype(bf16)
    for owner in range(out_ref.shape[0]):
        out_ref[owner] = copies


def unpack_body(got_ref, code_ref, grad_ref):
    at = lax.broadcasted_iota(jnp.int32, (STRIP, CH), 0)
    for strip in range(GROUP):
        columns = pl.ds(strip * STRIP, STRIP)
        if strip > 0:
            before = got_ref[strip - 1, pl.ds(2 * TILE, EDGES), :].astype(f32)
        if strip < GROUP - 1:
            after = got_ref[strip + 1, pl.ds(2 * TILE, EDGES), :].astype(f32)
        for row in range(ROWS):
            code_ref[row, columns, :] = got_ref[strip, pl.ds(row * STRIP, STRIP), :]
            value = got_ref[strip, pl.ds(TILE + row * STRIP, STRIP), :].astype(f32)
            if strip > 0:
                value = value + jnp.where(at == 0, before[ROWS + row : ROWS + row + 1], 0.0)
            if strip < GROUP - 1:
                value = value + jnp.where(at == STRIP - 1, after[row : row + 1], 0.0)
            grad_ref[row, columns, :] = value.astype(bf16)


def shifted(value, axes, by):
    count = lax.axis_size(axes)
    route = [(i, i + by) for i in range(count) if 0 <= i + by < count]
    return lax.ppermute(value, axes, route)


def swapped(value):
    return lax.ppermute(value, "core", [(0, 1), (1, 0)])


def shards(frames, kernel, cotangent):
    weights = kernel.reshape(3, WIDE, CH)
    turned = jnp.swapaxes(kernel[::-1, ::-1, ::-1], 3, 4).reshape(3, WIDE, CH)
    lines = ("z", "core")
    packed = pl.pallas_call(
        pack_body,
        out_shape=jax.ShapeDtypeStruct((GROUP, LOAD, CH), bf16),
        in_specs=[pl.BlockSpec(memory_space=pl.ANY)] * 2,
        scratch_shapes=[pltpu.VMEM((GROUP, ROWS, CH), f32)] * 2
        + [pltpu.SemaphoreType.DMA((2, ROWS))],
    )(frames.reshape(ROWS, GROUP, STRIP, CH), cotangent.reshape(ROWS, GROUP, STRIP, CH))
    held = lax.all_to_all(packed, "y", 0, 0)
    early = shifted(held[GROUP - 2 :, : HELD + 2 * STRIP], "x", 1)

    def edge_rows(*places):
        pieces = [
            jnp.concatenate([early[:, low:high], held[:, low:high]], axis=0)
            for low, high in places
        ]
        return pieces[0] if len(pieces) == 1 else jnp.concatenate(pieces, axis=1)

    up = shifted(edge_rows((TILE - RIM, HELD + STRIP)), lines, 1)
    down = shifted(edge_rows((0, RIM), (TILE, HELD), (HELD + STRIP, HELD + 2 * STRIP)), lines, -1)

    devices = lax.axis_size(("x", "y", "z", "core"))
    peers, wide = lax.axis_size(("x", "z")), lax.axis_size("x")
    share = PART * -(-27 * CH // (PART * devices))
    mail = jax.ShapeDtypeStruct((peers, GROUP * share, CH), bf16)
    flops = 2 * GROUP * TILE * 27 * CH * CH
    code, g, g_up, g_down, keep, send = kernel_call(
        forward_body,
        (
            jax.ShapeDtypeStruct((GROUP, TILE, CH), bf16),
            jax.ShapeDtypeStruct((GROUP, TILE, CH), bf16),
            jax.ShapeDtypeStruct((GROUP, STRIP, CH), bf16),
            jax.ShapeDtypeStruct((GROUP, STRIP, CH), bf16),
            mail,
            mail,
        ),
        [
            pltpu.VMEM((FRAMES * (TILE + RIM), WIDE), bf16),
            pltpu.VMEM((GROUP * (TILE + RIM), CH), f32),
            pltpu.VMEM((3 * CH, FRAMES * TILE), bf16),
            pltpu.VMEM((2, peers, GROUP, share, CH), f32),
        ],
        flops=2 * flops,
        in_specs=[pl.BlockSpec(memory_space=pltpu.SMEM)]
        + [pl.BlockSpec(memory_space=pltpu.VMEM)] * 5,
    )(lax.axis_index("core").astype(jnp.int32).reshape(1), held, early, up, down, weights)

    chip_sum = (keep.astype(f32) + swapped(send).astype(f32)).astype(bf16)
    parts = lax.all_to_all(chip_sum, ("x", "z"), 0, 0)
    late = shifted(jnp.concatenate([g_up[:2], g[:2], g_down[:2]], axis=1), "x", -1)
    sent = kernel_call(
        backward_body,
        jax.ShapeDtypeStruct((GROUP, SENT, CH), bf16),
        [
            pltpu.VMEM((FRAMES * TILE, WIDE), bf16),
            pltpu.VMEM((FRAMES * ROWS, 3 * CH), f32),
        ],
        flops=flops,
    )(g, g_up, g_down, late, code, turned)
    parts, sent = lax.optimization_barrier((parts, sent))
    part = kernel_call(part_body, jax.ShapeDtypeStruct((GROUP, GROUP * share, CH), bf16))(parts)
    norm = 1.0 / math.sqrt(devices * GROUP * TILE)
    copies = kernel_call(
        functools.partial(share_body, norm=norm),
        jax.ShapeDtypeStruct((wide, GROUP * share, CH), bf16),
    )(lax.all_to_all(part, "y", 0, 0))
    line = lax.all_to_all(copies, "x", 0, 0).reshape(-1, CH)
    line = line[: 27 * CH // lax.axis_size(lines)]
    grad_kernel = lax.all_gather(line, lines, tiled=True).astype(f32)

    got = lax.all_to_all(sent, "y", 0, 0)
    whole = jax.ShapeDtypeStruct((ROWS, GROUP * STRIP, CH), bf16)
    code_out, grad_frames = kernel_call(unpack_body, (whole, whole))(got)
    return (code_out[None], grad_frames[None], grad_kernel.reshape(3, 3, 3, CH, CH))


def solution(mesh):
    split = Mesh(mesh.devices.reshape(CHIPS), ("x", "y", "z", "core"))
    block = P(("x", "y"), ("z", "core"), None, None)
    return jax.shard_map(
        shards,
        mesh=split,
        in_specs=(block, P(), block),
        out_specs=(block, block, P()),
        check_vma=False,
    )
```

```python
import functools
import math

import jax
import jax.numpy as jnp
from jax import lax
from jax.experimental import pallas as pl
from jax.experimental.pallas import tpu as pltpu
from jax.sharding import Mesh
from jax.sharding import PartitionSpec as P

CHIPS = (4, 8, 8, 2)
LEVELS = 3
GROUP = 1 << LEVELS
ROWS = 8
STRIP = 16
TILE = ROWS * STRIP
TALL = ROWS + 2
CH = 128
WIDE = 9 * CH
FRAMES = GROUP + 2
EDGES = 2 * ROWS
HELD = TILE + EDGES
LOAD = HELD + TILE
SENT = 2 * TILE + EDGES
RIM = 2 * STRIP
PART = 8
CHUNK = 8

band_weight = 0.75
root_half = 0.7071067811865476
f32 = jnp.float32
bf16 = jnp.bfloat16
VMEM_LIMIT = 48 * 1024 * 1024


def kernel_call(body, outs, scratch=(), flops=0, **specs):
    return pl.pallas_call(
        body,
        **specs,
        out_shape=outs,
        scratch_shapes=list(scratch),
        compiler_params=pltpu.CompilerParams(vmem_limit_bytes=VMEM_LIMIT),
        cost_estimate=pl.CostEstimate(flops=flops, bytes_accessed=4 << 20, transcendentals=0),
    )


def pack_body(x_hbm, cot_hbm, out_ref, left_ref, right_ref, sems):
    copies = [
        pltpu.make_async_copy(
            hbm.at[row], out_ref.at[:, pl.ds(place(row), STRIP), :], sems.at[side, row]
        )
        for side, (hbm, place) in enumerate(((x_hbm, x_place), (cot_hbm, cot_place)))
        for row in range(ROWS)
    ]
    for copy in copies:
        copy.start()
    left_ref[...] = jnp.zeros_like(left_ref)
    right_ref[...] = jnp.zeros_like(right_ref)
    for row in range(ROWS):
        copies[row].wait()
        for strip in range(GROUP):
            wide = out_ref[strip, pl.ds(x_place(row), STRIP), :].astype(f32)
            if strip < GROUP - 1:
                left_ref[strip + 1, pl.ds(row, 1), :] = wide[STRIP - 1 : STRIP]
            if strip > 0:
                right_ref[strip - 1, pl.ds(row, 1), :] = wide[0:1]
    for strip in range(GROUP):
        pair = jnp.concatenate([left_ref[strip], right_ref[strip]], axis=0)
        out_ref[strip, pl.ds(TILE, EDGES), :] = pair.astype(bf16)
    for copy in copies[ROWS:]:
        copy.wait()


def x_place(row):
    return row * STRIP


def cot_place(row):
    return HELD + (row + 1) % ROWS * STRIP


def place_line(col_ref, line, left, right, places):
    at = lax.broadcasted_iota(jnp.int32, (STRIP, CH), 0)
    wide = line.astype(f32)
    before = jnp.where(at == 0, left, pltpu.roll(wide, 1, 0)).astype(bf16)
    after = jnp.where(at == STRIP - 1, right, pltpu.roll(wide, STRIP - 1, 0)).astype(bf16)
    for row_tap, place in places:
        start = pl.multiple_of(place, STRIP)
        for col_tap, piece in enumerate((before, line, after)):
            tap = row_tap * 3 + col_tap
            col_ref[pl.ds(start, STRIP), pl.ds(tap * CH, CH)] = piece


def adjoint_bands(cot):
    back = [None] * GROUP
    for level in range(LEVELS - 1, -1, -1):
        step = 1 << level
        following = [None] * GROUP
        for frame in range(GROUP):
            if frame & step:
                continue
            pair = (cot[frame] + cot[frame + step]) * root_half
            if level == LEVELS - 1:
                total = pair
            else:
                total = (back[frame] + back[frame + step]) * root_half
            for member, side in ((frame, -1.0), (frame + step, 1.0)):
                value = total + (band_weight * side) * pair
                if level > 0:
                    value = value.astype(bf16).astype(f32)
                following[member] = value
        back = following
    return back


def slope_of(linear, gate):
    return gate * (1.0 + linear * (1.0 - gate))


def forward_body(
    core_ref,
    held_ref,
    early_ref,
    near_ref,
    far_ref,
    w_ref,
    code_ref,
    g_ref,
    g_up_ref,
    g_down_ref,
    keep_ref,
    send_ref,
    col_ref,
    lin_ref,
    gt_ref,
    terms_ref,
    up_ref,
    down_ref,
):
    for core, (above, below) in enumerate(((far_ref, near_ref), (near_ref, far_ref))):

        @pl.when(core_ref[0] == core)
        def _():
            up_ref[...] = above[...]
            down_ref[...] = below[...]

    def spread(ref, frame, place):
        for tall_row in range(-2, ROWS + 2):
            if tall_row < 0:
                source, at, low, edge_row = up_ref, place, (tall_row + 2) * STRIP, ROWS + tall_row
            elif tall_row >= ROWS:
                source, at, low, edge_row = down_ref, place, (tall_row - ROWS) * STRIP, tall_row - ROWS
            else:
                source, at, low, edge_row = ref, frame, tall_row * STRIP, tall_row
            line = source[at, pl.ds(low, STRIP), :]
            edge_low = TILE if source is ref else RIM
            edge = source[at, pl.ds(edge_low, EDGES), :].astype(f32)
            places = []
            for row_tap in range(3):
                row = tall_row + 1 - row_tap
                if 0 <= row < ROWS:
                    places.append((row_tap, place * TILE + row * STRIP))
                elif row == -1:
                    places.append((row_tap, FRAMES * TILE + place * RIM))
                elif row == ROWS:
                    places.append((row_tap, FRAMES * TILE + place * RIM + STRIP))
            place_line(
                col_ref,
                line,
                edge[edge_row : edge_row + 1],
                edge[ROWS + edge_row : ROWS + edge_row + 1],
                places,
            )

    @pl.loop(0, 2)
    def _(frame):
        spread(early_ref, frame, frame)

    @pl.loop(0, GROUP)
    def _(frame):
        spread(held_ref, frame, frame + 2)

    for low, step in ((0, TILE), (FRAMES * TILE, RIM)):
        total = None
        for tap in range(3):
            rows = col_ref[low + tap * step : low + (tap + GROUP) * step, :]
            part = jnp.dot(rows, w_ref[tap], preferred_element_type=f32)
            total = part if total is None else total + part
        place = 0 if step == TILE else GROUP * TILE
        lin_ref[place : place + GROUP * step, :] = total

    @pl.loop(0, ROWS)
    def _(row):
        low = pl.multiple_of(row * STRIP, STRIP)
        linear = [lin_ref[pl.ds(frame * TILE + low, STRIP), :] for frame in range(GROUP)]
        gate = [jax.nn.sigmoid(value) for value in linear]
        band = [(value * part).astype(bf16).astype(f32) for value, part in zip(linear, gate)]
        detail = [None] * GROUP
        for level in range(LEVELS):
            step = 1 << level
            following = [None] * GROUP
            for frame in range(0, GROUP, 2 * step):
                lower, upper = band[frame], band[frame + step]
                smooth = (lower + upper) * root_half
                if level < LEVELS - 1:
                    smooth = smooth.astype(bf16).astype(f32)
                change = (upper - lower) * root_half
                following[frame] = smooth
                for member in range(frame, frame + 2 * step, 2):
                    detail[member] = change if level == 0 else detail[member] + change
            band = following
        for member in range(0, GROUP, 2):
            code = (band[0] + band_weight * detail[member]).astype(bf16)
            code_ref[member, pl.ds(low, STRIP), :] = code
            code_ref[member + 1, pl.ds(low, STRIP), :] = code
        place = pl.multiple_of(HELD + lax.rem(row + 1, ROWS) * STRIP, STRIP)
        cot = [held_ref[frame, pl.ds(place, STRIP), :].astype(f32) for frame in range(GROUP)]
        back = adjoint_bands(cot)
        for frame in range(GROUP):
            g_ref[frame, pl.ds(low, STRIP), :] = (
                back[frame] * slope_of(linear[frame], gate[frame])
            ).astype(bf16)

    for offset, source, rim_ref in ((0, up_ref, g_up_ref), (STRIP, down_ref, g_down_ref)):
        cot = [
            source[frame + 2, pl.ds(RIM + EDGES, STRIP), :].astype(f32) for frame in range(GROUP)
        ]
        back = adjoint_bands(cot)
        for frame in range(GROUP):
            linear = lin_ref[pl.ds(GROUP * TILE + frame * RIM + offset, STRIP), :]
            slope = slope_of(linear, jax.nn.sigmoid(linear))
            rim_ref[frame] = (back[frame] * slope).astype(bf16)

    gt_ref[...] = jnp.zeros_like(gt_ref)
    for frame in range(GROUP):
        turned = g_ref[frame].astype(f32).T.astype(bf16)
        for tap in range(3):
            gt_ref[pl.ds(tap * CH, CH), pl.ds((frame + tap) * TILE, TILE)] = turned
    _, peers, _, _ = terms_ref.shape
    wide = CHIPS[0]
    deep = peers // wide
    part = 27 * CH // (2 * peers)
    terms_ref[...] = jnp.zeros_like(terms_ref)
    for low in range(0, 9, 2):
        high = min(low + 2, 9)
        product = jnp.dot(
            gt_ref[...],
            col_ref[0 : FRAMES * TILE, low * CH : high * CH],
            preferred_element_type=f32,
        )
        for tap in range(low, high):
            for frame_tap in range(3):
                block = product[
                    frame_tap * CH : (frame_tap + 1) * CH, (tap - low) * CH : (tap - low + 1) * CH
                ].T
                first = (frame_tap * 9 + tap) * CH
                at = first
                while at < first + CH:
                    place, row = divmod(at, part)
                    count = min(part - row, first + CH - at)
                    line, column = divmod(place, wide)
                    depth, core = divmod(line, 2)
                    terms_ref[core, column * deep + depth, pl.ds(row, count), :] = block[
                        at - first : at - first + count
                    ]
                    at += count
    for core in range(2):

        @pl.when(core_ref[0] == core)
        def _():
            for peer in range(peers):
                keep_ref[peer] = terms_ref[core, peer].astype(bf16)
                send_ref[peer] = terms_ref[1 - core, peer].astype(bf16)


def backward_body(g_ref, up_ref, down_ref, late_ref, code_ref, w_ref, out_ref, col_ref, side_ref):
    nothing = jnp.zeros((1, CH), f32)

    def spread(lines, place):
        for tall_row, line in enumerate(lines):
            places = [
                (row_tap, place * TILE + (tall_row - row_tap) * STRIP)
                for row_tap in range(3)
                if 0 <= tall_row - row_tap < ROWS
            ]
            place_line(col_ref, line, nothing, nothing, places)

    @pl.loop(0, GROUP)
    def _(frame):
        rows = [g_ref[frame, pl.ds(row * STRIP, STRIP), :] for row in range(ROWS)]
        spread([up_ref[frame]] + rows + [down_ref[frame]], frame)

    @pl.loop(0, 2)
    def _(frame):
        lines = [late_ref[frame, pl.ds(row * STRIP, STRIP), :] for row in range(TALL)]
        spread(lines, frame + GROUP)

    total = (
        jnp.dot(col_ref[0 : GROUP * TILE, :], w_ref[0], preferred_element_type=f32)
        + jnp.dot(col_ref[TILE : (GROUP + 1) * TILE, :], w_ref[1], preferred_element_type=f32)
        + jnp.dot(col_ref[2 * TILE : (GROUP + 2) * TILE, :], w_ref[2], preferred_element_type=f32)
    )
    for frame in range(GROUP):
        out_ref[frame, 0:TILE, :] = code_ref[frame]
        out_ref[frame, TILE : 2 * TILE, :] = total[frame * TILE : (frame + 1) * TILE].astype(bf16)
    for side, (offset, col_tap) in enumerate(((0, 2), (STRIP - 1, 0))):
        for frame in range(FRAMES):
            for row in range(ROWS):
                at = frame * TILE + row * STRIP + (0 if side == 0 else STRIP - 8)
                for row_tap in range(3):
                    mid = (row_tap * 3 + 1) * CH
                    piece = col_ref[pl.ds(frame * TILE + row * STRIP, STRIP), pl.ds(mid, CH)]
                    one = piece.astype(f32)[offset : offset + 1]
                    side_ref[pl.ds(frame * ROWS + row, 1), pl.ds(row_tap * CH, CH)] = one
        summed = None
        for frame_tap in range(3):
            rows = side_ref[pl.ds(frame_tap * ROWS, GROUP * ROWS), :].astype(bf16)
            for row_tap in range(3):
                tap = row_tap * 3 + col_tap
                part = jnp.dot(
                    rows[:, row_tap * CH : (row_tap + 1) * CH],
                    w_ref[frame_tap, pl.ds(tap * CH, CH), :],
                    preferred_element_type=f32,
                )
                summed = part if summed is None else summed + part
        if side == 0:
            first = summed
    for frame in range(GROUP):
        pair = [value[frame * ROWS : (frame + 1) * ROWS] for value in (first, summed)]
        out_ref[frame, 2 * TILE : SENT, :] = jnp.concatenate(pair, axis=0).astype(bf16)


def add_body(one_ref, other_ref, out_ref):
    out_ref[...] = (one_ref[...].astype(f32) + other_ref[...].astype(f32)).astype(bf16)


def part_body(parts_ref, out_ref):
    part = parts_ref[0].astype(f32)
    for peer in range(1, parts_ref.shape[0]):
        part = part + parts_ref[peer].astype(f32)
    part = part.astype(bf16)
    for place in range(out_ref.shape[0]):
        out_ref[place] = part


def share_body(got_ref, out_ref, norm):
    total = got_ref[0].astype(f32)
    for place in range(1, got_ref.shape[0]):
        total = total + got_ref[place].astype(f32)
    copies = (total * norm).astype(bf16)
    for owner in range(out_ref.shape[0]):
        out_ref[owner] = copies


def unpack(got_ref, code_ref, grad_ref):
    at = lax.broadcasted_iota(jnp.int32, (STRIP, CH), 0)
    for strip in range(GROUP):
        columns = pl.ds(strip * STRIP, STRIP)
        if strip > 0:
            before = got_ref[strip - 1, pl.ds(2 * TILE, EDGES), :].astype(f32)
        if strip < GROUP - 1:
            after = got_ref[strip + 1, pl.ds(2 * TILE, EDGES), :].astype(f32)
        for row in range(ROWS):
            code_ref[row, columns, :] = got_ref[strip, pl.ds(row * STRIP, STRIP), :]
            value = got_ref[strip, pl.ds(TILE + row * STRIP, STRIP), :].astype(f32)
            if strip > 0:
                value = value + jnp.where(at == 0, before[ROWS + row : ROWS + row + 1], 0.0)
            if strip < GROUP - 1:
                value = value + jnp.where(at == STRIP - 1, after[row : row + 1], 0.0)
            grad_ref[row, columns, :] = value.astype(bf16)


def finish_body(
    got_ref, terms_ref, code_hbm, grad_hbm, kernel_hbm, code_ref, grad_ref, kernel_ref, sems
):
    copies = []
    chunks = kernel_ref.shape[0]
    part = kernel_ref.shape[1] // CHUNK
    for chunk in range(chunks):
        for place in range(CHUNK):
            rows = terms_ref[chunk * CHUNK + place].astype(f32)
            kernel_ref[chunk, pl.ds(place * part, part), :] = rows[:part]
        copies.append(
            pltpu.make_async_copy(kernel_ref.at[chunk], kernel_hbm.at[chunk], sems.at[chunk])
        )
        copies[-1].start()
    unpack(got_ref, code_ref, grad_ref)
    for at, (ref, hbm) in enumerate(((code_ref, code_hbm), (grad_ref, grad_hbm))):
        copies.append(pltpu.make_async_copy(ref, hbm, sems.at[chunks + at]))
        copies[-1].start()
    for copy in copies:
        copy.wait()


def shifted(value, axes, by):
    count = lax.axis_size(axes)
    route = [(i, i + by) for i in range(count) if 0 <= i + by < count]
    return lax.ppermute(value, axes, route)


def between_chips(value):
    count = lax.axis_size(("z", "core"))
    pairs = [(i, i + 1) for i in range(1, count - 1, 2)]
    return lax.ppermute(value, ("z", "core"), pairs + [(j, i) for i, j in pairs])


def swapped(value):
    return lax.ppermute(value, "core", [(0, 1), (1, 0)])


def shards(frames, kernel, cotangent):
    weights = kernel.reshape(3, WIDE, CH)
    turned = jnp.swapaxes(kernel[::-1, ::-1, ::-1], 3, 4).reshape(3, WIDE, CH)
    lines = ("z", "core")
    packed = pl.pallas_call(
        pack_body,
        out_shape=jax.ShapeDtypeStruct((GROUP, LOAD, CH), bf16),
        in_specs=[pl.BlockSpec(memory_space=pl.ANY)] * 2,
        scratch_shapes=[pltpu.VMEM((GROUP, ROWS, CH), f32)] * 2
        + [pltpu.SemaphoreType.DMA((2, ROWS))],
    )(frames.reshape(ROWS, GROUP, STRIP, CH), cotangent.reshape(ROWS, GROUP, STRIP, CH))
    held = lax.all_to_all(packed, "y", 0, 0)
    early = shifted(held[GROUP - 2 :, : HELD + 2 * STRIP], "x", 1)

    def edge_rows(*places):
        pieces = [
            jnp.concatenate([early[:, low:high], held[:, low:high]], axis=0)
            for low, high in places
        ]
        return pieces[0] if len(pieces) == 1 else jnp.concatenate(pieces, axis=1)

    core = lax.axis_index("core")
    last = edge_rows((TILE - RIM, HELD + STRIP))
    first = edge_rows((0, RIM), (TILE, HELD), (HELD + STRIP, HELD + 2 * STRIP))
    near = swapped(jnp.where(core == 0, last, first))
    far = between_chips(jnp.where(core == 0, first, last))

    devices = lax.axis_size(("x", "y", "z", "core"))
    peers, wide = lax.axis_size(("x", "z")), lax.axis_size("x")
    share = PART * -(-27 * CH // (2 * PART * peers))
    mail = jax.ShapeDtypeStruct((peers, share, CH), bf16)
    flops = 2 * GROUP * TILE * 27 * CH * CH
    code, g, g_up, g_down, keep, send = kernel_call(
        forward_body,
        (
            jax.ShapeDtypeStruct((GROUP, TILE, CH), bf16),
            jax.ShapeDtypeStruct((GROUP, TILE, CH), bf16),
            jax.ShapeDtypeStruct((GROUP, STRIP, CH), bf16),
            jax.ShapeDtypeStruct((GROUP, STRIP, CH), bf16),
            mail,
            mail,
        ),
        [
            pltpu.VMEM((FRAMES * (TILE + RIM), WIDE), bf16),
            pltpu.VMEM((GROUP * (TILE + RIM), CH), f32),
            pltpu.VMEM((3 * CH, FRAMES * TILE), bf16),
            pltpu.VMEM((2, peers, share, CH), f32),
        ]
        + [pltpu.VMEM((FRAMES, RIM + EDGES + STRIP, CH), bf16)] * 2,
        flops=2 * flops,
        in_specs=[pl.BlockSpec(memory_space=pltpu.SMEM)]
        + [pl.BlockSpec(memory_space=pltpu.VMEM)] * 5,
    )(core.astype(jnp.int32).reshape(1), held, early, near, far, weights)

    chip_sum = kernel_call(add_body, mail)(keep, swapped(send))
    parts = lax.all_to_all(chip_sum, ("x", "z"), 0, 0)
    late = shifted(jnp.concatenate([g_up[:2], g[:2], g_down[:2]], axis=1), "x", -1)
    sent = kernel_call(
        backward_body,
        jax.ShapeDtypeStruct((GROUP, SENT, CH), bf16),
        [
            pltpu.VMEM((FRAMES * TILE, WIDE), bf16),
            pltpu.VMEM((FRAMES * ROWS, 3 * CH), f32),
        ],
        flops=flops,
    )(g, g_up, g_down, late, code, turned)
    parts, sent = lax.optimization_barrier((parts, sent))
    part = kernel_call(part_body, jax.ShapeDtypeStruct((GROUP, share, CH), bf16))(parts)
    norm = 1.0 / math.sqrt(devices * GROUP * TILE)
    copies = kernel_call(
        functools.partial(share_body, norm=norm),
        jax.ShapeDtypeStruct((wide, share, CH), bf16),
    )(lax.all_to_all(part, "y", 0, 0))
    line = lax.all_to_all(copies, "x", 0, 0).reshape(wide * share, CH)
    terms = lax.all_gather(line, lines, tiled=True).reshape(-1, share, CH)

    got = lax.all_to_all(sent, "y", 0, 0)
    whole = (ROWS, GROUP * STRIP, CH)
    part = 27 * CH // terms.shape[0]
    code_out, grad_frames, grad_kernel = pl.pallas_call(
        finish_body,
        out_shape=(
            jax.ShapeDtypeStruct(whole, bf16),
            jax.ShapeDtypeStruct(whole, bf16),
            jax.ShapeDtypeStruct((terms.shape[0] // CHUNK, CHUNK * part, CH), f32),
        ),
        in_specs=[pl.BlockSpec(memory_space=pltpu.VMEM)] * 2,
        out_specs=[pl.BlockSpec(memory_space=pl.ANY)] * 3,
        scratch_shapes=[
            pltpu.VMEM(whole, bf16),
            pltpu.VMEM(whole, bf16),
            pltpu.VMEM((terms.shape[0] // CHUNK, CHUNK * part, CH), f32),
            pltpu.SemaphoreType.DMA((2 + terms.shape[0] // CHUNK,)),
        ],
        compiler_params=pltpu.CompilerParams(vmem_limit_bytes=VMEM_LIMIT),
    )(got, terms)
    return (code_out[None], grad_frames[None], grad_kernel.reshape(3, 3, 3, CH, CH))


def solution(mesh):
    split = Mesh(mesh.devices.reshape(CHIPS), ("x", "y", "z", "core"))
    block = P(("x", "y"), ("z", "core"), None, None)
    return jax.shard_map(
        shards,
        mesh=split,
        in_specs=(block, P(), block),
        out_specs=(block, block, P()),
        check_vma=False,
    )
```

```python
import functools
import math

import jax
import jax.numpy as jnp
from jax import lax
from jax.experimental import pallas as pl
from jax.experimental.pallas import tpu as pltpu
from jax.sharding import Mesh
from jax.sharding import PartitionSpec as P

CHIPS = (4, 8, 8, 2)
LEVELS = 3
GROUP = 1 << LEVELS
ROWS = 8
STRIP = 16
TILE = ROWS * STRIP
TALL = ROWS + 2
CH = 128
WIDE = 9 * CH
FRAMES = GROUP + 2
EDGES = 2 * ROWS
HELD = TILE + EDGES
LOAD = HELD + TILE
SENT = 2 * TILE + EDGES
RIM = 2 * STRIP
PART = 8
CHUNK = 8

band_weight = 0.75
root_half = 0.7071067811865476
f32 = jnp.float32
bf16 = jnp.bfloat16
VMEM_LIMIT = 48 * 1024 * 1024


def kernel_call(body, outs, scratch=(), flops=0, **specs):
    return pl.pallas_call(
        body,
        **specs,
        out_shape=outs,
        scratch_shapes=list(scratch),
        compiler_params=pltpu.CompilerParams(vmem_limit_bytes=VMEM_LIMIT),
        cost_estimate=pl.CostEstimate(flops=flops, bytes_accessed=4 << 20, transcendentals=0),
    )


def pack_body(x_hbm, cot_hbm, out_hbm, x_ref, edge_ref, left_ref, right_ref, sems, own_sems):
    own = pltpu.make_async_copy(x_hbm, x_ref, own_sems.at[0])
    own.start()
    copies = [
        pltpu.make_async_copy(
            hbm.at[row], out_hbm.at[:, pl.ds(place(row), STRIP), :], sems.at[side, row]
        )
        for side, (hbm, place) in enumerate(((x_hbm, x_place), (cot_hbm, cot_place)))
        for row in range(ROWS)
    ]
    for copy in copies:
        copy.start()
    left_ref[...] = jnp.zeros_like(left_ref)
    right_ref[...] = jnp.zeros_like(right_ref)
    own.wait()
    for row in range(ROWS):
        for strip in range(GROUP):
            wide = x_ref[row, strip].astype(f32)
            if strip < GROUP - 1:
                left_ref[strip + 1, pl.ds(row, 1), :] = wide[STRIP - 1 : STRIP]
            if strip > 0:
                right_ref[strip - 1, pl.ds(row, 1), :] = wide[0:1]
    for strip in range(GROUP):
        pair = jnp.concatenate([left_ref[strip], right_ref[strip]], axis=0)
        edge_ref[strip] = pair.astype(bf16)
    edges = pltpu.make_async_copy(edge_ref, out_hbm.at[:, pl.ds(TILE, EDGES), :], own_sems.at[1])
    edges.start()
    for copy in copies + [edges]:
        copy.wait()


def x_place(row):
    return row * STRIP


def cot_place(row):
    return HELD + (row + 1) % ROWS * STRIP


def place_line(col_ref, line, left, right, places):
    at = lax.broadcasted_iota(jnp.int32, (STRIP, CH), 0)
    wide = line.astype(f32)
    before = jnp.where(at == 0, left, pltpu.roll(wide, 1, 0)).astype(bf16)
    after = jnp.where(at == STRIP - 1, right, pltpu.roll(wide, STRIP - 1, 0)).astype(bf16)
    for row_tap, place in places:
        start = pl.multiple_of(place, STRIP)
        for col_tap, piece in enumerate((before, line, after)):
            tap = row_tap * 3 + col_tap
            col_ref[pl.ds(start, STRIP), pl.ds(tap * CH, CH)] = piece


def gate_of(linear):
    return 0.5 * jnp.tanh(0.5 * linear) + 0.5


def bands(active):
    sums, code = active, [0.0] * (GROUP // 2)
    scale = 1.0
    for level in range(LEVELS):
        scale = scale * root_half
        changes = [(sums[at + 1] - sums[at]) * (band_weight * scale) for at in range(0, len(sums), 2)]
        sums = [sums[at] + sums[at + 1] for at in range(0, len(sums), 2)]
        if level == LEVELS - 1:
            changes = [changes[0] + sums[0] * scale]
        code = [value + changes[at >> level] for at, value in enumerate(code)]
    return code


def adjoint_bands(cot):
    levels = [cot]
    for level in range(LEVELS):
        last = levels[-1]
        levels.append([last[at] + last[at + 1] for at in range(0, len(last), 2)])
    scale = root_half**LEVELS
    back = [levels[LEVELS][0] * scale]
    for level in range(LEVELS - 1, -1, -1):
        weight = band_weight * root_half ** (level + 1)
        steps = [value * weight for value in levels[level + 1]]
        back = [
            value
            for at, step in enumerate(steps)
            for value in (back[at] - step, back[at] + step)
        ]
    return back


def slope_of(linear, gate):
    return gate * (1.0 + linear * (1.0 - gate))


def forward_body(
    core_ref,
    held_ref,
    early_ref,
    near_ref,
    far_ref,
    w_ref,
    code_ref,
    g_ref,
    g_up_ref,
    g_down_ref,
    keep_ref,
    send_ref,
    col_ref,
    lin_ref,
    gt_ref,
    terms_ref,
    up_ref,
    down_ref,
):
    for core, (above, below) in enumerate(((far_ref, near_ref), (near_ref, far_ref))):

        @pl.when(core_ref[0] == core)
        def _():
            up_ref[...] = above[...]
            down_ref[...] = below[...]

    def spread(ref, frame, place):
        for tall_row in range(-2, ROWS + 2):
            if tall_row < 0:
                source, at, low, edge_row = up_ref, place, (tall_row + 2) * STRIP, ROWS + tall_row
            elif tall_row >= ROWS:
                source, at, low, edge_row = down_ref, place, (tall_row - ROWS) * STRIP, tall_row - ROWS
            else:
                source, at, low, edge_row = ref, frame, tall_row * STRIP, tall_row
            line = source[at, pl.ds(low, STRIP), :]
            edge_low = TILE if source is ref else RIM
            edge = source[at, pl.ds(edge_low, EDGES), :].astype(f32)
            places = []
            for row_tap in range(3):
                row = tall_row + 1 - row_tap
                if 0 <= row < ROWS:
                    places.append((row_tap, place * TILE + row * STRIP))
                elif row == -1:
                    places.append((row_tap, FRAMES * TILE + place * RIM))
                elif row == ROWS:
                    places.append((row_tap, FRAMES * TILE + place * RIM + STRIP))
            place_line(
                col_ref,
                line,
                edge[edge_row : edge_row + 1],
                edge[ROWS + edge_row : ROWS + edge_row + 1],
                places,
            )

    @pl.loop(0, 2)
    def _(frame):
        spread(early_ref, frame, frame)

    @pl.loop(0, GROUP)
    def _(frame):
        spread(held_ref, frame, frame + 2)

    for low, step in ((0, TILE), (FRAMES * TILE, RIM)):
        total = None
        for tap in range(3):
            rows = col_ref[low + tap * step : low + (tap + GROUP) * step, :]
            part = jnp.dot(rows, w_ref[tap], preferred_element_type=f32)
            total = part if total is None else total + part
        place = 0 if step == TILE else GROUP * TILE
        lin_ref[place : place + GROUP * step, :] = total

    @pl.loop(0, ROWS)
    def _(row):
        low = pl.multiple_of(row * STRIP, STRIP)
        linear = [lin_ref[pl.ds(frame * TILE + low, STRIP), :] for frame in range(GROUP)]
        gate = [gate_of(value) for value in linear]
        codes = bands([value * part for value, part in zip(linear, gate)])
        for pair, value in enumerate(codes):
            code = value.astype(bf16)
            code_ref[2 * pair, pl.ds(low, STRIP), :] = code
            code_ref[2 * pair + 1, pl.ds(low, STRIP), :] = code
        place = pl.multiple_of(HELD + lax.rem(row + 1, ROWS) * STRIP, STRIP)
        cot = [held_ref[frame, pl.ds(place, STRIP), :].astype(f32) for frame in range(GROUP)]
        back = adjoint_bands(cot)
        for frame in range(GROUP):
            g_ref[frame, pl.ds(low, STRIP), :] = (
                back[frame] * slope_of(linear[frame], gate[frame])
            ).astype(bf16)

    for offset, source, rim_ref in ((0, up_ref, g_up_ref), (STRIP, down_ref, g_down_ref)):
        cot = [
            source[frame + 2, pl.ds(RIM + EDGES, STRIP), :].astype(f32) for frame in range(GROUP)
        ]
        back = adjoint_bands(cot)
        for frame in range(GROUP):
            linear = lin_ref[pl.ds(GROUP * TILE + frame * RIM + offset, STRIP), :]
            slope = slope_of(linear, gate_of(linear))
            rim_ref[frame] = (back[frame] * slope).astype(bf16)

    gt_ref[...] = jnp.zeros_like(gt_ref)
    for frame in range(GROUP):
        turned = g_ref[frame].astype(f32).T.astype(bf16)
        for tap in range(3):
            gt_ref[pl.ds(tap * CH, CH), pl.ds((frame + tap) * TILE, TILE)] = turned
    _, peers, _, _ = terms_ref.shape
    wide = CHIPS[0]
    deep = peers // wide
    part = 27 * CH // (2 * peers)
    terms_ref[...] = jnp.zeros_like(terms_ref)
    for low in range(0, 9, 2):
        high = min(low + 2, 9)
        product = jnp.dot(
            gt_ref[...],
            col_ref[0 : FRAMES * TILE, low * CH : high * CH],
            preferred_element_type=f32,
        )
        for tap in range(low, high):
            for frame_tap in range(3):
                block = product[
                    frame_tap * CH : (frame_tap + 1) * CH, (tap - low) * CH : (tap - low + 1) * CH
                ].T
                first = (frame_tap * 9 + tap) * CH
                at = first
                while at < first + CH:
                    place, row = divmod(at, part)
                    count = min(part - row, first + CH - at)
                    line, column = divmod(place, wide)
                    depth, core = divmod(line, 2)
                    terms_ref[core, column * deep + depth, pl.ds(row, count), :] = block[
                        at - first : at - first + count
                    ]
                    at += count
    for core in range(2):

        @pl.when(core_ref[0] == core)
        def _():
            for peer in range(peers):
                keep_ref[peer] = terms_ref[core, peer].astype(bf16)
                send_ref[peer] = terms_ref[1 - core, peer].astype(bf16)


def backward_body(g_ref, up_ref, down_ref, late_ref, code_ref, w_ref, out_ref, col_ref, side_ref):
    nothing = jnp.zeros((1, CH), f32)

    def spread(lines, place):
        for tall_row, line in enumerate(lines):
            places = [
                (row_tap, place * TILE + (tall_row - row_tap) * STRIP)
                for row_tap in range(3)
                if 0 <= tall_row - row_tap < ROWS
            ]
            place_line(col_ref, line, nothing, nothing, places)

    @pl.loop(0, GROUP)
    def _(frame):
        rows = [g_ref[frame, pl.ds(row * STRIP, STRIP), :] for row in range(ROWS)]
        spread([up_ref[frame]] + rows + [down_ref[frame]], frame)

    @pl.loop(0, 2)
    def _(frame):
        lines = [late_ref[frame, pl.ds(row * STRIP, STRIP), :] for row in range(TALL)]
        spread(lines, frame + GROUP)

    total = (
        jnp.dot(col_ref[0 : GROUP * TILE, :], w_ref[0], preferred_element_type=f32)
        + jnp.dot(col_ref[TILE : (GROUP + 1) * TILE, :], w_ref[1], preferred_element_type=f32)
        + jnp.dot(col_ref[2 * TILE : (GROUP + 2) * TILE, :], w_ref[2], preferred_element_type=f32)
    )
    for frame in range(GROUP):
        out_ref[frame, 0:TILE, :] = code_ref[frame]
        out_ref[frame, TILE : 2 * TILE, :] = total[frame * TILE : (frame + 1) * TILE].astype(bf16)
    for side, (offset, col_tap) in enumerate(((0, 2), (STRIP - 1, 0))):
        for frame in range(FRAMES):
            for row in range(ROWS):
                at = frame * TILE + row * STRIP + (0 if side == 0 else STRIP - 8)
                for row_tap in range(3):
                    mid = (row_tap * 3 + 1) * CH
                    piece = col_ref[pl.ds(frame * TILE + row * STRIP, STRIP), pl.ds(mid, CH)]
                    one = piece.astype(f32)[offset : offset + 1]
                    side_ref[pl.ds(frame * ROWS + row, 1), pl.ds(row_tap * CH, CH)] = one
        summed = None
        for frame_tap in range(3):
            rows = side_ref[pl.ds(frame_tap * ROWS, GROUP * ROWS), :].astype(bf16)
            for row_tap in range(3):
                tap = row_tap * 3 + col_tap
                part = jnp.dot(
                    rows[:, row_tap * CH : (row_tap + 1) * CH],
                    w_ref[frame_tap, pl.ds(tap * CH, CH), :],
                    preferred_element_type=f32,
                )
                summed = part if summed is None else summed + part
        if side == 0:
            first = summed
    for frame in range(GROUP):
        pair = [value[frame * ROWS : (frame + 1) * ROWS] for value in (first, summed)]
        out_ref[frame, 2 * TILE : SENT, :] = jnp.concatenate(pair, axis=0).astype(bf16)


def add_body(one_ref, other_ref, out_hbm, sum_ref, sems):
    copies = []
    count = out_hbm.shape[0] // sems.shape[0]
    for chunk in range(sems.shape[0]):
        pieces = pl.ds(chunk * count, count)
        sum_ref[pieces] = (one_ref[pieces].astype(f32) + other_ref[pieces].astype(f32)).astype(bf16)
        copies.append(
            pltpu.make_async_copy(sum_ref.at[pieces], out_hbm.at[pieces], sems.at[chunk])
        )
        copies[-1].start()
    for copy in copies:
        copy.wait()


def part_body(parts_ref, out_ref):
    part = parts_ref[0].astype(f32)
    for peer in range(1, parts_ref.shape[0]):
        part = part + parts_ref[peer].astype(f32)
    part = part.astype(bf16)
    for place in range(out_ref.shape[0]):
        out_ref[place] = part


def share_body(got_ref, out_ref, norm):
    total = got_ref[0].astype(f32)
    for place in range(1, got_ref.shape[0]):
        total = total + got_ref[place].astype(f32)
    copies = (total * norm).astype(bf16)
    for owner in range(out_ref.shape[0]):
        out_ref[owner] = copies


def unpack(got_ref, code_ref, grad_ref):
    at = lax.broadcasted_iota(jnp.int32, (STRIP, CH), 0)
    for strip in range(GROUP):
        columns = pl.ds(strip * STRIP, STRIP)
        if strip > 0:
            before = got_ref[strip - 1, pl.ds(2 * TILE, EDGES), :].astype(f32)
        if strip < GROUP - 1:
            after = got_ref[strip + 1, pl.ds(2 * TILE, EDGES), :].astype(f32)
        for row in range(ROWS):
            code_ref[row, columns, :] = got_ref[strip, pl.ds(row * STRIP, STRIP), :]
            value = got_ref[strip, pl.ds(TILE + row * STRIP, STRIP), :].astype(f32)
            if strip > 0:
                value = value + jnp.where(at == 0, before[ROWS + row : ROWS + row + 1], 0.0)
            if strip < GROUP - 1:
                value = value + jnp.where(at == STRIP - 1, after[row : row + 1], 0.0)
            grad_ref[row, columns, :] = value.astype(bf16)


def finish_body(
    got_ref, terms_ref, code_hbm, grad_hbm, kernel_hbm, code_ref, grad_ref, kernel_ref, sems
):
    copies = []
    chunks = kernel_ref.shape[0]
    part = kernel_ref.shape[1] // CHUNK
    for chunk in range(chunks):
        for place in range(CHUNK):
            rows = terms_ref[chunk * CHUNK + place].astype(f32)
            kernel_ref[chunk, pl.ds(place * part, part), :] = rows[:part]
        copies.append(
            pltpu.make_async_copy(kernel_ref.at[chunk], kernel_hbm.at[chunk], sems.at[chunk])
        )
        copies[-1].start()
    unpack(got_ref, code_ref, grad_ref)
    for at, (ref, hbm) in enumerate(((code_ref, code_hbm), (grad_ref, grad_hbm))):
        copies.append(pltpu.make_async_copy(ref, hbm, sems.at[chunks + at]))
        copies[-1].start()
    for copy in copies:
        copy.wait()


def shifted(value, axes, by):
    count = lax.axis_size(axes)
    route = [(i, i + by) for i in range(count) if 0 <= i + by < count]
    return lax.ppermute(value, axes, route)


def between_chips(value):
    count = lax.axis_size(("z", "core"))
    pairs = [(i, i + 1) for i in range(1, count - 1, 2)]
    return lax.ppermute(value, ("z", "core"), pairs + [(j, i) for i, j in pairs])


def swapped(value):
    return lax.ppermute(value, "core", [(0, 1), (1, 0)])


def shards(frames, kernel, cotangent):
    taps = kernel.reshape(3, WIDE, CH)
    weights = taps
    turned = jnp.swapaxes(kernel[::-1, ::-1, ::-1], 3, 4).reshape(3, WIDE, CH)
    lines = ("z", "core")
    packed = pl.pallas_call(
        pack_body,
        out_shape=jax.ShapeDtypeStruct((GROUP, LOAD, CH), bf16),
        in_specs=[pl.BlockSpec(memory_space=pl.ANY)] * 2,
        out_specs=pl.BlockSpec(memory_space=pl.ANY),
        scratch_shapes=[
            pltpu.VMEM((ROWS, GROUP, STRIP, CH), bf16),
            pltpu.VMEM((GROUP, EDGES, CH), bf16),
            pltpu.VMEM((GROUP, ROWS, CH), f32),
            pltpu.VMEM((GROUP, ROWS, CH), f32),
            pltpu.SemaphoreType.DMA((2, ROWS)),
            pltpu.SemaphoreType.DMA((2,)),
        ],
    )(frames.reshape(ROWS, GROUP, STRIP, CH), cotangent.reshape(ROWS, GROUP, STRIP, CH))
    held = lax.all_to_all(packed, "y", 0, 0)
    early = shifted(held[GROUP - 2 :, : HELD + 2 * STRIP], "x", 1)

    def edge_rows(*places):
        pieces = [
            jnp.concatenate([early[:, low:high], held[:, low:high]], axis=0)
            for low, high in places
        ]
        return pieces[0] if len(pieces) == 1 else jnp.concatenate(pieces, axis=1)

    core = lax.axis_index("core")
    last = edge_rows((TILE - RIM, HELD + STRIP))
    first = edge_rows((0, RIM), (TILE, HELD), (HELD + STRIP, HELD + 2 * STRIP))
    near = swapped(jnp.where(core == 0, last, first))
    far = between_chips(jnp.where(core == 0, first, last))

    devices = lax.axis_size(("x", "y", "z", "core"))
    peers, wide = lax.axis_size(("x", "z")), lax.axis_size("x")
    share = PART * -(-27 * CH // (2 * PART * peers))
    mail = jax.ShapeDtypeStruct((peers, share, CH), bf16)
    flops = 2 * GROUP * TILE * 27 * CH * CH
    code, g, g_up, g_down, keep, send = kernel_call(
        forward_body,
        (
            jax.ShapeDtypeStruct((GROUP, TILE, CH), bf16),
            jax.ShapeDtypeStruct((GROUP, TILE, CH), bf16),
            jax.ShapeDtypeStruct((GROUP, STRIP, CH), bf16),
            jax.ShapeDtypeStruct((GROUP, STRIP, CH), bf16),
            mail,
            mail,
        ),
        [
            pltpu.VMEM((FRAMES * (TILE + RIM), WIDE), bf16),
            pltpu.VMEM((GROUP * (TILE + RIM), CH), f32),
            pltpu.VMEM((3 * CH, FRAMES * TILE), bf16),
            pltpu.VMEM((2, peers, share, CH), f32),
        ]
        + [pltpu.VMEM((FRAMES, RIM + EDGES + STRIP, CH), bf16)] * 2,
        flops=2 * flops,
        in_specs=[pl.BlockSpec(memory_space=pltpu.SMEM)]
        + [pl.BlockSpec(memory_space=pltpu.VMEM)] * 5,
    )(core.astype(jnp.int32).reshape(1), held, early, near, far, weights)

    chip_sum = kernel_call(
        add_body,
        mail,
        [pltpu.VMEM(mail.shape, bf16), pltpu.SemaphoreType.DMA((4,))],
        in_specs=[pl.BlockSpec(memory_space=pltpu.VMEM)] * 2,
        out_specs=pl.BlockSpec(memory_space=pl.ANY),
    )(keep, swapped(send))
    parts = lax.all_to_all(chip_sum, ("x", "z"), 0, 0)
    late = shifted(jnp.concatenate([g_up[:2], g[:2], g_down[:2]], axis=1), "x", -1)
    sent = kernel_call(
        backward_body,
        jax.ShapeDtypeStruct((GROUP, SENT, CH), bf16),
        [
            pltpu.VMEM((FRAMES * TILE, WIDE), bf16),
            pltpu.VMEM((FRAMES * ROWS, 3 * CH), f32),
        ],
        flops=flops,
    )(g, g_up, g_down, late, code, turned)
    parts, sent = lax.optimization_barrier((parts, sent))
    part = kernel_call(part_body, jax.ShapeDtypeStruct((GROUP, share, CH), bf16))(parts)
    norm = 1.0 / math.sqrt(devices * GROUP * TILE)
    copies = kernel_call(
        functools.partial(share_body, norm=norm),
        jax.ShapeDtypeStruct((wide, share, CH), bf16),
    )(lax.all_to_all(part, "y", 0, 0))
    line = lax.all_to_all(copies, "x", 0, 0).reshape(wide * share, CH)
    terms = lax.all_gather(line, lines, tiled=True).reshape(-1, share, CH)

    got = lax.all_to_all(sent, "y", 0, 0)
    whole = (ROWS, GROUP * STRIP, CH)
    part = 27 * CH // terms.shape[0]
    code_out, grad_frames, grad_kernel = pl.pallas_call(
        finish_body,
        out_shape=(
            jax.ShapeDtypeStruct(whole, bf16),
            jax.ShapeDtypeStruct(whole, bf16),
            jax.ShapeDtypeStruct((terms.shape[0] // CHUNK, CHUNK * part, CH), f32),
        ),
        in_specs=[pl.BlockSpec(memory_space=pltpu.VMEM)] * 2,
        out_specs=[pl.BlockSpec(memory_space=pl.ANY)] * 3,
        scratch_shapes=[
            pltpu.VMEM(whole, bf16),
            pltpu.VMEM(whole, bf16),
            pltpu.VMEM((terms.shape[0] // CHUNK, CHUNK * part, CH), f32),
            pltpu.SemaphoreType.DMA((2 + terms.shape[0] // CHUNK,)),
        ],
        compiler_params=pltpu.CompilerParams(vmem_limit_bytes=VMEM_LIMIT),
    )(got, terms)
    return (code_out[None], grad_frames[None], grad_kernel.reshape(3, 3, 3, CH, CH))


def solution(mesh):
    split = Mesh(mesh.devices.reshape(CHIPS), ("x", "y", "z", "core"))
    block = P(("x", "y"), ("z", "core"), None, None)
    return jax.shard_map(
        shards,
        mesh=split,
        in_specs=(block, P(), block),
        out_specs=(block, block, P()),
        check_vma=False,
    )
```

```python
import functools
import math

import jax
import jax.numpy as jnp
from jax import lax
from jax.experimental import pallas as pl
from jax.experimental.pallas import tpu as pltpu
from jax.sharding import Mesh
from jax.sharding import PartitionSpec as P

CHIPS = (4, 8, 8, 2)
LEVELS = 3
GROUP = 1 << LEVELS
ROWS = 8
STRIP = 16
TILE = ROWS * STRIP
TALL = ROWS + 2
CH = 128
WIDE = 9 * CH
FRAMES = GROUP + 2
EDGES = 2 * ROWS
HELD = TILE + EDGES
LOAD = HELD + TILE
SENT = 2 * TILE + EDGES
RIM = 2 * STRIP
PART = 8
CHUNK = 8

band_weight = 0.75
root_half = 0.7071067811865476
f32 = jnp.float32
bf16 = jnp.bfloat16
VMEM_LIMIT = 24 * 1024 * 1024


def kernel_call(body, outs, scratch=(), flops=0, **specs):
    return pl.pallas_call(
        body,
        **specs,
        out_shape=outs,
        scratch_shapes=list(scratch),
        compiler_params=pltpu.CompilerParams(vmem_limit_bytes=VMEM_LIMIT),
        cost_estimate=pl.CostEstimate(flops=flops, bytes_accessed=4 << 20, transcendentals=0),
    )


def pack_body(x_hbm, cot_hbm, out_ref, left_ref, right_ref, sems):
    copies = [
        pltpu.make_async_copy(
            hbm.at[row], out_ref.at[:, pl.ds(place(row), STRIP), :], sems.at[side, row]
        )
        for side, (hbm, place) in enumerate(((x_hbm, x_place), (cot_hbm, cot_place)))
        for row in range(ROWS)
    ]
    for copy in copies:
        copy.start()
    left_ref[...] = jnp.zeros_like(left_ref)
    right_ref[...] = jnp.zeros_like(right_ref)
    for row in range(ROWS):
        copies[row].wait()
        for strip in range(GROUP):
            wide = out_ref[strip, pl.ds(x_place(row), STRIP), :].astype(f32)
            if strip < GROUP - 1:
                left_ref[strip + 1, pl.ds(row, 1), :] = wide[STRIP - 1 : STRIP]
            if strip > 0:
                right_ref[strip - 1, pl.ds(row, 1), :] = wide[0:1]
    for strip in range(GROUP):
        pair = jnp.concatenate([left_ref[strip], right_ref[strip]], axis=0)
        out_ref[strip, pl.ds(TILE, EDGES), :] = pair.astype(bf16)
    for copy in copies[ROWS:]:
        copy.wait()


def x_place(row):
    return row * STRIP


def cot_place(row):
    return HELD + (row + 1) % ROWS * STRIP


def place_line(col_ref, line, left, right, places):
    at = lax.broadcasted_iota(jnp.int32, (STRIP, CH), 0)
    wide = line.astype(f32)
    before = jnp.where(at == 0, left, pltpu.roll(wide, 1, 0)).astype(bf16)
    after = jnp.where(at == STRIP - 1, right, pltpu.roll(wide, STRIP - 1, 0)).astype(bf16)
    for row_tap, place in places:
        start = pl.multiple_of(place, STRIP)
        for col_tap, piece in enumerate((before, line, after)):
            tap = row_tap * 3 + col_tap
            col_ref[pl.ds(start, STRIP), pl.ds(tap * CH, CH)] = piece


def gate_of(linear):
    return 0.5 * jnp.tanh(0.5 * linear) + 0.5


def bands(active):
    sums, code = active, [0.0] * (GROUP // 2)
    scale = 1.0
    for level in range(LEVELS):
        scale = scale * root_half
        changes = [(sums[at + 1] - sums[at]) * (band_weight * scale) for at in range(0, len(sums), 2)]
        sums = [sums[at] + sums[at + 1] for at in range(0, len(sums), 2)]
        if level == LEVELS - 1:
            changes = [changes[0] + sums[0] * scale]
        code = [value + changes[at >> level] for at, value in enumerate(code)]
    return code


def adjoint_bands(cot):
    levels = [cot]
    for level in range(LEVELS):
        last = levels[-1]
        levels.append([last[at] + last[at + 1] for at in range(0, len(last), 2)])
    scale = root_half**LEVELS
    back = [levels[LEVELS][0] * scale]
    for level in range(LEVELS - 1, -1, -1):
        weight = band_weight * root_half ** (level + 1)
        steps = [value * weight for value in levels[level + 1]]
        back = [
            value
            for at, step in enumerate(steps)
            for value in (back[at] - step, back[at] + step)
        ]
    return back


def slope_of(linear, gate):
    return gate * (1.0 + linear * (1.0 - gate))


def spread(ref, frame, place, col_ref, tall_rows, wanted, up_ref=None, down_ref=None):
    for tall_row in tall_rows:
        if tall_row < 0:
            source, at, low, edge_row = up_ref, place, (tall_row + 2) * STRIP, ROWS + tall_row
        elif tall_row >= ROWS:
            source, at, low, edge_row = down_ref, place, (tall_row - ROWS) * STRIP, tall_row - ROWS
        else:
            source, at, low, edge_row = ref, frame, tall_row * STRIP, tall_row
        line = source[at, pl.ds(low, STRIP), :]
        edge_low = TILE if source is ref else RIM
        edge = source[at, pl.ds(edge_low, EDGES), :].astype(f32)
        places = []
        for row_tap in range(3):
            row = tall_row + 1 - row_tap
            if row not in wanted:
                continue
            if 0 <= row < ROWS:
                places.append((row_tap, place * TILE + row * STRIP))
            elif row == -1:
                places.append((row_tap, FRAMES * TILE + place * RIM))
            else:
                places.append((row_tap, FRAMES * TILE + place * RIM + STRIP))
        place_line(
            col_ref,
            line,
            edge[edge_row : edge_row + 1],
            edge[ROWS + edge_row : ROWS + edge_row + 1],
            places,
        )


def products(col_ref, w_ref, lin_ref, ranges, first=0):
    total = None
    for tap in range(3):
        rows = [
            col_ref[pl.ds(low + (frame + tap - first) * step, count), :]
            for frame, low, count, step in ranges
        ]
        part = jnp.dot(jnp.concatenate(rows, axis=0), w_ref[tap], preferred_element_type=f32)
        total = part if total is None else total + part
    at = 0
    for frame, low, count, step in ranges:
        out = low if step == TILE else low - (FRAMES - GROUP) * TILE
        lin_ref[out + frame * step : out + frame * step + count, :] = total[at : at + count]
        at += count


INNER = [(frame, STRIP, (ROWS - 2) * STRIP, TILE) for frame in range(GROUP)]
OUTER = [
    piece
    for frame in range(GROUP)
    for piece in (
        (frame, 0, STRIP, TILE),
        (frame, TILE - STRIP, STRIP, TILE),
        (frame, FRAMES * TILE, RIM, RIM),
    )
]


def ahead_body(held_ref, w_ref, col_ref, lin_ref):
    @pl.loop(0, GROUP)
    def _(frame):
        spread(held_ref, frame, frame, col_ref, range(ROWS), range(ROWS))

    products(col_ref, w_ref, lin_ref, INNER[2:], first=2)


def forward_body(
    core_ref,
    held_ref,
    early_ref,
    near_ref,
    far_ref,
    w_ref,
    col_in_ref,
    lin_in_ref,
    code_ref,
    g_ref,
    g_up_ref,
    g_down_ref,
    keep_ref,
    send_ref,
    col_ref,
    lin_ref,
    gt_ref,
    terms_ref,
    up_ref,
    down_ref,
):
    for core, (above, below) in enumerate(((far_ref, near_ref), (near_ref, far_ref))):

        @pl.when(core_ref[0] == core)
        def _():
            up_ref[...] = above[...]
            down_ref[...] = below[...]

    col_ref[2 * TILE : FRAMES * TILE, :] = col_in_ref[...]
    lin_ref[2 * TILE : GROUP * TILE, :] = lin_in_ref[2 * TILE :, :]
    tall = range(-1, ROWS + 1)

    @pl.loop(0, 2)
    def _(frame):
        spread(early_ref, frame, frame, col_ref, range(-2, ROWS + 2), tall, up_ref, down_ref)

    @pl.loop(0, GROUP)
    def _(frame):
        beyond = (-2, -1, ROWS, ROWS + 1)
        spread(held_ref, frame, frame + 2, col_ref, beyond, tall, up_ref, down_ref)
        spread(held_ref, frame, frame + 2, col_ref, (0, ROWS - 1), (-1, ROWS))

    products(col_ref, w_ref, lin_ref, INNER[:2] + OUTER)

    @pl.loop(0, ROWS)
    def _(row):
        low = pl.multiple_of(row * STRIP, STRIP)
        linear = [lin_ref[pl.ds(frame * TILE + low, STRIP), :] for frame in range(GROUP)]
        gate = [gate_of(value) for value in linear]
        codes = bands([value * part for value, part in zip(linear, gate)])
        for pair, value in enumerate(codes):
            code = value.astype(bf16)
            code_ref[2 * pair, pl.ds(low, STRIP), :] = code
            code_ref[2 * pair + 1, pl.ds(low, STRIP), :] = code
        place = pl.multiple_of(HELD + lax.rem(row + 1, ROWS) * STRIP, STRIP)
        cot = [held_ref[frame, pl.ds(place, STRIP), :].astype(f32) for frame in range(GROUP)]
        back = adjoint_bands(cot)
        for frame in range(GROUP):
            g_ref[frame, pl.ds(low, STRIP), :] = (
                back[frame] * slope_of(linear[frame], gate[frame])
            ).astype(bf16)

    for offset, source, rim_ref in ((0, up_ref, g_up_ref), (STRIP, down_ref, g_down_ref)):
        cot = [
            source[frame + 2, pl.ds(RIM + EDGES, STRIP), :].astype(f32) for frame in range(GROUP)
        ]
        back = adjoint_bands(cot)
        for frame in range(GROUP):
            linear = lin_ref[pl.ds(GROUP * TILE + frame * RIM + offset, STRIP), :]
            slope = slope_of(linear, gate_of(linear))
            rim_ref[frame] = (back[frame] * slope).astype(bf16)

    gt_ref[...] = jnp.zeros_like(gt_ref)
    for frame in range(GROUP):
        turned = g_ref[frame].astype(f32).T.astype(bf16)
        for tap in range(3):
            gt_ref[pl.ds(tap * CH, CH), pl.ds((frame + tap) * TILE, TILE)] = turned
    _, peers, _, _ = terms_ref.shape
    wide = CHIPS[0]
    deep = peers // wide
    part = 27 * CH // (2 * peers)
    terms_ref[...] = jnp.zeros_like(terms_ref)
    for low in range(0, 9, 2):
        high = min(low + 2, 9)
        product = jnp.dot(
            gt_ref[...],
            col_ref[0 : FRAMES * TILE, low * CH : high * CH],
            preferred_element_type=f32,
        )
        for tap in range(low, high):
            for frame_tap in range(3):
                block = product[
                    frame_tap * CH : (frame_tap + 1) * CH, (tap - low) * CH : (tap - low + 1) * CH
                ].T
                first = (frame_tap * 9 + tap) * CH
                at = first
                while at < first + CH:
                    place, row = divmod(at, part)
                    count = min(part - row, first + CH - at)
                    line, column = divmod(place, wide)
                    depth, core = divmod(line, 2)
                    terms_ref[core, column * deep + depth, pl.ds(row, count), :] = block[
                        at - first : at - first + count
                    ]
                    at += count
    for core in range(2):

        @pl.when(core_ref[0] == core)
        def _():
            for peer in range(peers):
                keep_ref[peer] = terms_ref[core, peer].astype(bf16)
                send_ref[peer] = terms_ref[1 - core, peer].astype(bf16)


def backward_body(g_ref, up_ref, down_ref, late_ref, code_ref, w_ref, out_ref, col_ref, side_ref):
    nothing = jnp.zeros((1, CH), f32)

    def spread(lines, place):
        for tall_row, line in enumerate(lines):
            places = [
                (row_tap, place * TILE + (tall_row - row_tap) * STRIP)
                for row_tap in range(3)
                if 0 <= tall_row - row_tap < ROWS
            ]
            place_line(col_ref, line, nothing, nothing, places)

    @pl.loop(0, GROUP)
    def _(frame):
        rows = [g_ref[frame, pl.ds(row * STRIP, STRIP), :] for row in range(ROWS)]
        spread([up_ref[frame]] + rows + [down_ref[frame]], frame)

    @pl.loop(0, 2)
    def _(frame):
        lines = [late_ref[frame, pl.ds(row * STRIP, STRIP), :] for row in range(TALL)]
        spread(lines, frame + GROUP)

    total = (
        jnp.dot(col_ref[0 : GROUP * TILE, :], w_ref[0], preferred_element_type=f32)
        + jnp.dot(col_ref[TILE : (GROUP + 1) * TILE, :], w_ref[1], preferred_element_type=f32)
        + jnp.dot(col_ref[2 * TILE : (GROUP + 2) * TILE, :], w_ref[2], preferred_element_type=f32)
    )
    for frame in range(GROUP):
        out_ref[frame, 0:TILE, :] = code_ref[frame]
        out_ref[frame, TILE : 2 * TILE, :] = total[frame * TILE : (frame + 1) * TILE].astype(bf16)
    for side, (offset, col_tap) in enumerate(((0, 2), (STRIP - 1, 0))):
        for frame in range(FRAMES):
            for row in range(ROWS):
                at = frame * TILE + row * STRIP + (0 if side == 0 else STRIP - 8)
                for row_tap in range(3):
                    mid = (row_tap * 3 + 1) * CH
                    piece = col_ref[pl.ds(frame * TILE + row * STRIP, STRIP), pl.ds(mid, CH)]
                    one = piece.astype(f32)[offset : offset + 1]
                    side_ref[pl.ds(frame * ROWS + row, 1), pl.ds(row_tap * CH, CH)] = one
        summed = None
        for frame_tap in range(3):
            rows = side_ref[pl.ds(frame_tap * ROWS, GROUP * ROWS), :].astype(bf16)
            for row_tap in range(3):
                tap = row_tap * 3 + col_tap
                part = jnp.dot(
                    rows[:, row_tap * CH : (row_tap + 1) * CH],
                    w_ref[frame_tap, pl.ds(tap * CH, CH), :],
                    preferred_element_type=f32,
                )
                summed = part if summed is None else summed + part
        if side == 0:
            first = summed
    for frame in range(GROUP):
        pair = [value[frame * ROWS : (frame + 1) * ROWS] for value in (first, summed)]
        out_ref[frame, 2 * TILE : SENT, :] = jnp.concatenate(pair, axis=0).astype(bf16)


def add_body(one_ref, other_ref, out_hbm, sum_ref, sems):
    copies = []
    count = out_hbm.shape[0] // sems.shape[0]
    for chunk in range(sems.shape[0]):
        pieces = pl.ds(chunk * count, count)
        sum_ref[pieces] = (one_ref[pieces].astype(f32) + other_ref[pieces].astype(f32)).astype(bf16)
        copies.append(
            pltpu.make_async_copy(sum_ref.at[pieces], out_hbm.at[pieces], sems.at[chunk])
        )
        copies[-1].start()
    for copy in copies:
        copy.wait()


def part_body(parts_ref, out_ref):
    part = parts_ref[0].astype(f32)
    for peer in range(1, parts_ref.shape[0]):
        part = part + parts_ref[peer].astype(f32)
    part = part.astype(bf16)
    for place in range(out_ref.shape[0]):
        out_ref[place] = part


def share_body(got_ref, out_ref, norm):
    total = got_ref[0].astype(f32)
    for place in range(1, got_ref.shape[0]):
        total = total + got_ref[place].astype(f32)
    copies = (total * norm).astype(bf16)
    for owner in range(out_ref.shape[0]):
        out_ref[owner] = copies


def unpack(got_ref, code_ref, grad_ref):
    at = lax.broadcasted_iota(jnp.int32, (STRIP, CH), 0)
    for strip in range(GROUP):
        columns = pl.ds(strip * STRIP, STRIP)
        if strip > 0:
            before = got_ref[strip - 1, pl.ds(2 * TILE, EDGES), :].astype(f32)
        if strip < GROUP - 1:
            after = got_ref[strip + 1, pl.ds(2 * TILE, EDGES), :].astype(f32)
        for row in range(ROWS):
            code_ref[row, columns, :] = got_ref[strip, pl.ds(row * STRIP, STRIP), :]
            value = got_ref[strip, pl.ds(TILE + row * STRIP, STRIP), :].astype(f32)
            if strip > 0:
                value = value + jnp.where(at == 0, before[ROWS + row : ROWS + row + 1], 0.0)
            if strip < GROUP - 1:
                value = value + jnp.where(at == STRIP - 1, after[row : row + 1], 0.0)
            grad_ref[row, columns, :] = value.astype(bf16)


def finish_body(
    got_ref, terms_ref, code_hbm, grad_hbm, kernel_hbm, code_ref, grad_ref, kernel_ref, sems
):
    copies = []
    chunks = kernel_ref.shape[0]
    part = kernel_ref.shape[1] // CHUNK
    for chunk in range(chunks):
        for place in range(CHUNK):
            rows = terms_ref[chunk * CHUNK + place].astype(f32)
            kernel_ref[chunk, pl.ds(place * part, part), :] = rows[:part]
        copies.append(
            pltpu.make_async_copy(kernel_ref.at[chunk], kernel_hbm.at[chunk], sems.at[chunk])
        )
        copies[-1].start()
    unpack(got_ref, code_ref, grad_ref)
    for at, (ref, hbm) in enumerate(((code_ref, code_hbm), (grad_ref, grad_hbm))):
        copies.append(pltpu.make_async_copy(ref, hbm, sems.at[chunks + at]))
        copies[-1].start()
    for copy in copies:
        copy.wait()


def shifted(value, axes, by):
    count = lax.axis_size(axes)
    route = [(i, i + by) for i in range(count) if 0 <= i + by < count]
    return lax.ppermute(value, axes, route)


def between_chips(value):
    count = lax.axis_size(("z", "core"))
    pairs = [(i, i + 1) for i in range(1, count - 1, 2)]
    return lax.ppermute(value, ("z", "core"), pairs + [(j, i) for i, j in pairs])


def swapped(value):
    return lax.ppermute(value, "core", [(0, 1), (1, 0)])


def shards(frames, kernel, cotangent):
    taps = kernel.reshape(3, WIDE, CH)
    weights = taps
    turned = jnp.swapaxes(kernel[::-1, ::-1, ::-1], 3, 4).reshape(3, WIDE, CH)
    lines = ("z", "core")
    packed = pl.pallas_call(
        pack_body,
        out_shape=jax.ShapeDtypeStruct((GROUP, LOAD, CH), bf16),
        in_specs=[pl.BlockSpec(memory_space=pl.ANY)] * 2,
        scratch_shapes=[pltpu.VMEM((GROUP, ROWS, CH), f32)] * 2
        + [pltpu.SemaphoreType.DMA((2, ROWS))],
    )(frames.reshape(ROWS, GROUP, STRIP, CH), cotangent.reshape(ROWS, GROUP, STRIP, CH))
    held = lax.all_to_all(packed, "y", 0, 0)
    early = shifted(held[GROUP - 2 :, : HELD + 2 * STRIP], "x", 1)

    def edge_rows(*places):
        pieces = [
            jnp.concatenate([early[:, low:high], held[:, low:high]], axis=0)
            for low, high in places
        ]
        return pieces[0] if len(pieces) == 1 else jnp.concatenate(pieces, axis=1)

    core = lax.axis_index("core")
    last = edge_rows((TILE - RIM, HELD + STRIP))
    first = edge_rows((0, RIM), (TILE, HELD), (HELD + STRIP, HELD + 2 * STRIP))
    near = swapped(jnp.where(core == 0, last, first))
    far = between_chips(jnp.where(core == 0, first, last))

    devices = lax.axis_size(("x", "y", "z", "core"))
    peers, wide = lax.axis_size(("x", "z")), lax.axis_size("x")
    share = PART * -(-27 * CH // (2 * PART * peers))
    mail = jax.ShapeDtypeStruct((peers, share, CH), bf16)
    flops = 2 * GROUP * TILE * 27 * CH * CH
    ahead = kernel_call(
        ahead_body,
        (
            jax.ShapeDtypeStruct((GROUP * TILE, WIDE), bf16),
            jax.ShapeDtypeStruct((GROUP * TILE, CH), f32),
        ),
        flops=flops // 2,
    )(held, weights)
    code, g, g_up, g_down, keep, send = kernel_call(
        forward_body,
        (
            jax.ShapeDtypeStruct((GROUP, TILE, CH), bf16),
            jax.ShapeDtypeStruct((GROUP, TILE, CH), bf16),
            jax.ShapeDtypeStruct((GROUP, STRIP, CH), bf16),
            jax.ShapeDtypeStruct((GROUP, STRIP, CH), bf16),
            mail,
            mail,
        ),
        [
            pltpu.VMEM((FRAMES * (TILE + RIM), WIDE), bf16),
            pltpu.VMEM((GROUP * (TILE + RIM), CH), f32),
            pltpu.VMEM((3 * CH, FRAMES * TILE), bf16),
            pltpu.VMEM((2, peers, share, CH), f32),
        ]
        + [pltpu.VMEM((FRAMES, RIM + EDGES + STRIP, CH), bf16)] * 2,
        flops=2 * flops,
        in_specs=[pl.BlockSpec(memory_space=pltpu.SMEM)]
        + [pl.BlockSpec(memory_space=pltpu.VMEM)] * 7,
    )(core.astype(jnp.int32).reshape(1), held, early, near, far, weights, *ahead)

    chip_sum = kernel_call(
        add_body,
        mail,
        [pltpu.VMEM(mail.shape, bf16), pltpu.SemaphoreType.DMA((4,))],
        in_specs=[pl.BlockSpec(memory_space=pltpu.VMEM)] * 2,
        out_specs=pl.BlockSpec(memory_space=pl.ANY),
    )(keep, swapped(send))
    parts = lax.all_to_all(chip_sum, ("x", "z"), 0, 0)
    late = shifted(jnp.concatenate([g_up[:2], g[:2], g_down[:2]], axis=1), "x", -1)
    sent = kernel_call(
        backward_body,
        jax.ShapeDtypeStruct((GROUP, SENT, CH), bf16),
        [
            pltpu.VMEM((FRAMES * TILE, WIDE), bf16),
            pltpu.VMEM((FRAMES * ROWS, 3 * CH), f32),
        ],
        flops=flops,
    )(g, g_up, g_down, late, code, turned)
    parts, sent = lax.optimization_barrier((parts, sent))
    part = kernel_call(part_body, jax.ShapeDtypeStruct((GROUP, share, CH), bf16))(parts)
    norm = 1.0 / math.sqrt(devices * GROUP * TILE)
    copies = kernel_call(
        functools.partial(share_body, norm=norm),
        jax.ShapeDtypeStruct((wide, share, CH), bf16),
    )(lax.all_to_all(part, "y", 0, 0))
    line = lax.all_to_all(copies, "x", 0, 0).reshape(wide * share, CH)
    terms = lax.all_gather(line, lines, tiled=True).reshape(-1, share, CH)

    got = lax.all_to_all(sent, "y", 0, 0)
    whole = (ROWS, GROUP * STRIP, CH)
    part = 27 * CH // terms.shape[0]
    code_out, grad_frames, grad_kernel = pl.pallas_call(
        finish_body,
        out_shape=(
            jax.ShapeDtypeStruct(whole, bf16),
            jax.ShapeDtypeStruct(whole, bf16),
            jax.ShapeDtypeStruct((terms.shape[0] // CHUNK, CHUNK * part, CH), f32),
        ),
        in_specs=[pl.BlockSpec(memory_space=pltpu.VMEM)] * 2,
        out_specs=[pl.BlockSpec(memory_space=pl.ANY)] * 3,
        scratch_shapes=[
            pltpu.VMEM(whole, bf16),
            pltpu.VMEM(whole, bf16),
            pltpu.VMEM((terms.shape[0] // CHUNK, CHUNK * part, CH), f32),
            pltpu.SemaphoreType.DMA((2 + terms.shape[0] // CHUNK,)),
        ],
        compiler_params=pltpu.CompilerParams(vmem_limit_bytes=VMEM_LIMIT),
    )(got, terms)
    return (code_out[None], grad_frames[None], grad_kernel.reshape(3, 3, 3, CH, CH))


def solution(mesh):
    split = Mesh(mesh.devices.reshape(CHIPS), ("x", "y", "z", "core"))
    block = P(("x", "y"), ("z", "core"), None, None)
    return jax.shard_map(
        shards,
        mesh=split,
        in_specs=(block, P(), block),
        out_specs=(block, block, P()),
        check_vma=False,
    )
```

```python
import functools
import math

import jax
import jax.numpy as jnp
from jax import lax
from jax.experimental import pallas as pl
from jax.experimental.pallas import tpu as pltpu
from jax.sharding import Mesh
from jax.sharding import PartitionSpec as P

CHIPS = (4, 8, 8, 2)
LEVELS = 3
GROUP = 1 << LEVELS
ROWS = 8
STRIP = 16
TILE = ROWS * STRIP
TALL = ROWS + 2
CH = 128
WIDE = 9 * CH
FRAMES = GROUP + 2
EDGES = 2 * ROWS
HELD = TILE + EDGES
LOAD = HELD + TILE
SENT = 2 * TILE + EDGES
RIM = 2 * STRIP
PART = 8
CHUNK = 8

band_weight = 0.75
root_half = 0.7071067811865476
f32 = jnp.float32
bf16 = jnp.bfloat16
VMEM_LIMIT = 24 * 1024 * 1024


def kernel_call(body, outs, scratch=(), flops=0, **specs):
    return pl.pallas_call(
        body,
        **specs,
        out_shape=outs,
        scratch_shapes=list(scratch),
        compiler_params=pltpu.CompilerParams(vmem_limit_bytes=VMEM_LIMIT),
        cost_estimate=pl.CostEstimate(flops=flops, bytes_accessed=4 << 20, transcendentals=0),
    )


def pack_body(x_hbm, cot_hbm, out_ref, left_ref, right_ref, sems):
    copies = [
        pltpu.make_async_copy(
            hbm.at[row], out_ref.at[:, pl.ds(place(row), STRIP), :], sems.at[side, row]
        )
        for side, (hbm, place) in enumerate(((x_hbm, x_place), (cot_hbm, cot_place)))
        for row in range(ROWS)
    ]
    for copy in copies:
        copy.start()
    left_ref[...] = jnp.zeros_like(left_ref)
    right_ref[...] = jnp.zeros_like(right_ref)
    for row in range(ROWS):
        copies[row].wait()
        for strip in range(GROUP):
            wide = out_ref[strip, pl.ds(x_place(row), STRIP), :].astype(f32)
            if strip < GROUP - 1:
                left_ref[strip + 1, pl.ds(row, 1), :] = wide[STRIP - 1 : STRIP]
            if strip > 0:
                right_ref[strip - 1, pl.ds(row, 1), :] = wide[0:1]
    for strip in range(GROUP):
        pair = jnp.concatenate([left_ref[strip], right_ref[strip]], axis=0)
        out_ref[strip, pl.ds(TILE, EDGES), :] = pair.astype(bf16)
    for copy in copies[ROWS:]:
        copy.wait()


def x_place(row):
    return row * STRIP


def cot_place(row):
    return HELD + (row + 1) % ROWS * STRIP


def place_line(col_ref, line, left, right, places):
    at = lax.broadcasted_iota(jnp.int32, (STRIP, CH), 0)
    wide = line.astype(f32)
    before = jnp.where(at == 0, left, pltpu.roll(wide, 1, 0)).astype(bf16)
    after = jnp.where(at == STRIP - 1, right, pltpu.roll(wide, STRIP - 1, 0)).astype(bf16)
    for row_tap, place in places:
        start = pl.multiple_of(place, STRIP)
        for col_tap, piece in enumerate((before, line, after)):
            tap = row_tap * 3 + col_tap
            col_ref[pl.ds(start, STRIP), pl.ds(tap * CH, CH)] = piece


def gate_of(linear):
    return 0.5 * jnp.tanh(0.5 * linear) + 0.5


def bands(active):
    sums, code = active, [0.0] * (GROUP // 2)
    scale = 1.0
    for level in range(LEVELS):
        scale = scale * root_half
        changes = [(sums[at + 1] - sums[at]) * (band_weight * scale) for at in range(0, len(sums), 2)]
        sums = [sums[at] + sums[at + 1] for at in range(0, len(sums), 2)]
        if level == LEVELS - 1:
            changes = [changes[0] + sums[0] * scale]
        code = [value + changes[at >> level] for at, value in enumerate(code)]
    return code


def adjoint_bands(cot):
    levels = [cot]
    for level in range(LEVELS):
        last = levels[-1]
        levels.append([last[at] + last[at + 1] for at in range(0, len(last), 2)])
    scale = root_half**LEVELS
    back = [levels[LEVELS][0] * scale]
    for level in range(LEVELS - 1, -1, -1):
        weight = band_weight * root_half ** (level + 1)
        steps = [value * weight for value in levels[level + 1]]
        back = [
            value
            for at, step in enumerate(steps)
            for value in (back[at] - step, back[at] + step)
        ]
    return back


def slope_of(linear, gate):
    return gate * (1.0 + linear * (1.0 - gate))


def spread(ref, frame, place, col_ref, tall_rows, wanted, up_ref=None, down_ref=None):
    for tall_row in tall_rows:
        if tall_row < 0:
            source, at, low, edge_row = up_ref, place, (tall_row + 2) * STRIP, ROWS + tall_row
        elif tall_row >= ROWS:
            source, at, low, edge_row = down_ref, place, (tall_row - ROWS) * STRIP, tall_row - ROWS
        else:
            source, at, low, edge_row = ref, frame, tall_row * STRIP, tall_row
        line = source[at, pl.ds(low, STRIP), :]
        edge_low = TILE if source is ref else RIM
        edge = source[at, pl.ds(edge_low, EDGES), :].astype(f32)
        places = []
        for row_tap in range(3):
            row = tall_row + 1 - row_tap
            if row not in wanted:
                continue
            if 0 <= row < ROWS:
                places.append((row_tap, place * TILE + row * STRIP))
            elif row == -1:
                places.append((row_tap, FRAMES * TILE + place * RIM))
            else:
                places.append((row_tap, FRAMES * TILE + place * RIM + STRIP))
        place_line(
            col_ref,
            line,
            edge[edge_row : edge_row + 1],
            edge[ROWS + edge_row : ROWS + edge_row + 1],
            places,
        )


def products(col_ref, w_ref, lin_ref, ranges, first=0):
    total = None
    for tap in range(3):
        rows = [
            col_ref[pl.ds(low + (frame + tap - first) * step, count), :]
            for frame, low, count, step in ranges
        ]
        part = jnp.dot(jnp.concatenate(rows, axis=0), w_ref[tap], preferred_element_type=f32)
        total = part if total is None else total + part
    at = 0
    for frame, low, count, step in ranges:
        out = low if step == TILE else low - (FRAMES - GROUP) * TILE
        lin_ref[out + frame * step : out + frame * step + count, :] = total[at : at + count]
        at += count


INNER = [(frame, STRIP, (ROWS - 2) * STRIP, TILE) for frame in range(GROUP)]
OUTER = [
    piece
    for frame in range(GROUP)
    for piece in (
        (frame, 0, STRIP, TILE),
        (frame, TILE - STRIP, STRIP, TILE),
        (frame, FRAMES * TILE, RIM, RIM),
    )
]


def ahead_body(held_ref, w_ref, col_ref, lin_ref):
    @pl.loop(0, GROUP)
    def _(frame):
        spread(held_ref, frame, frame, col_ref, range(ROWS), range(ROWS))

    products(col_ref, w_ref, lin_ref, INNER[2:], first=2)


def forward_body(
    core_ref,
    held_ref,
    early_ref,
    near_ref,
    far_ref,
    w_ref,
    col_in_ref,
    lin_in_ref,
    code_ref,
    g_ref,
    g_up_ref,
    g_down_ref,
    keep_ref,
    send_ref,
    col_ref,
    lin_ref,
    gt_ref,
    terms_ref,
    up_ref,
    down_ref,
):
    for core, (above, below) in enumerate(((far_ref, near_ref), (near_ref, far_ref))):

        @pl.when(core_ref[0] == core)
        def _():
            up_ref[...] = above[...]
            down_ref[...] = below[...]

    col_ref[2 * TILE : FRAMES * TILE, :] = col_in_ref[...]
    lin_ref[2 * TILE : GROUP * TILE, :] = lin_in_ref[2 * TILE :, :]
    tall = range(-1, ROWS + 1)

    @pl.loop(0, 2)
    def _(frame):
        spread(early_ref, frame, frame, col_ref, range(-2, ROWS + 2), tall, up_ref, down_ref)

    @pl.loop(0, GROUP)
    def _(frame):
        beyond = (-2, -1, ROWS, ROWS + 1)
        spread(held_ref, frame, frame + 2, col_ref, beyond, tall, up_ref, down_ref)
        spread(held_ref, frame, frame + 2, col_ref, (0, ROWS - 1), (-1, ROWS))

    products(col_ref, w_ref, lin_ref, INNER[:2] + OUTER)

    @pl.loop(0, ROWS)
    def _(row):
        low = pl.multiple_of(row * STRIP, STRIP)
        linear = [lin_ref[pl.ds(frame * TILE + low, STRIP), :] for frame in range(GROUP)]
        gate = [gate_of(value) for value in linear]
        codes = bands([value * part for value, part in zip(linear, gate)])
        for pair, value in enumerate(codes):
            code = value.astype(bf16)
            code_ref[2 * pair, pl.ds(low, STRIP), :] = code
            code_ref[2 * pair + 1, pl.ds(low, STRIP), :] = code
        place = pl.multiple_of(HELD + lax.rem(row + 1, ROWS) * STRIP, STRIP)
        cot = [held_ref[frame, pl.ds(place, STRIP), :].astype(f32) for frame in range(GROUP)]
        back = adjoint_bands(cot)
        for frame in range(GROUP):
            g_ref[frame, pl.ds(low, STRIP), :] = (
                back[frame] * slope_of(linear[frame], gate[frame])
            ).astype(bf16)

    for offset, source, rim_ref in ((0, up_ref, g_up_ref), (STRIP, down_ref, g_down_ref)):
        cot = [
            source[frame + 2, pl.ds(RIM + EDGES, STRIP), :].astype(f32) for frame in range(GROUP)
        ]
        back = adjoint_bands(cot)
        for frame in range(GROUP):
            linear = lin_ref[pl.ds(GROUP * TILE + frame * RIM + offset, STRIP), :]
            slope = slope_of(linear, gate_of(linear))
            rim_ref[frame] = (back[frame] * slope).astype(bf16)

    gt_ref[...] = jnp.zeros_like(gt_ref)
    for frame in range(GROUP):
        turned = g_ref[frame].astype(f32).T.astype(bf16)
        for tap in range(3):
            gt_ref[pl.ds(tap * CH, CH), pl.ds((frame + tap) * TILE, TILE)] = turned
    _, peers, _, _ = terms_ref.shape
    wide = CHIPS[0]
    deep = peers // wide
    part = 27 * CH // (2 * peers)
    terms_ref[...] = jnp.zeros_like(terms_ref)
    for low in range(0, 9, 2):
        high = min(low + 2, 9)
        product = jnp.dot(
            gt_ref[...],
            col_ref[0 : FRAMES * TILE, low * CH : high * CH],
            preferred_element_type=f32,
        )
        for tap in range(low, high):
            for frame_tap in range(3):
                block = product[
                    frame_tap * CH : (frame_tap + 1) * CH, (tap - low) * CH : (tap - low + 1) * CH
                ].T
                first = (frame_tap * 9 + tap) * CH
                at = first
                while at < first + CH:
                    place, row = divmod(at, part)
                    count = min(part - row, first + CH - at)
                    line, column = divmod(place, wide)
                    depth, core = divmod(line, 2)
                    terms_ref[core, column * deep + depth, pl.ds(row, count), :] = block[
                        at - first : at - first + count
                    ]
                    at += count
    for core in range(2):

        @pl.when(core_ref[0] == core)
        def _():
            for peer in range(peers):
                keep_ref[peer] = terms_ref[core, peer].astype(bf16)
                send_ref[peer] = terms_ref[1 - core, peer].astype(bf16)


def backward_body(g_ref, up_ref, down_ref, late_ref, code_ref, w_ref, out_ref, col_ref, side_ref):
    nothing = jnp.zeros((1, CH), f32)

    def spread(lines, place):
        for tall_row, line in enumerate(lines):
            places = [
                (row_tap, place * TILE + (tall_row - row_tap) * STRIP)
                for row_tap in range(3)
                if 0 <= tall_row - row_tap < ROWS
            ]
            place_line(col_ref, line, nothing, nothing, places)

    @pl.loop(0, GROUP)
    def _(frame):
        rows = [g_ref[frame, pl.ds(row * STRIP, STRIP), :] for row in range(ROWS)]
        spread([up_ref[frame]] + rows + [down_ref[frame]], frame)

    @pl.loop(0, 2)
    def _(frame):
        lines = [late_ref[frame, pl.ds(row * STRIP, STRIP), :] for row in range(TALL)]
        spread(lines, frame + GROUP)

    total = (
        jnp.dot(col_ref[0 : GROUP * TILE, :], w_ref[0], preferred_element_type=f32)
        + jnp.dot(col_ref[TILE : (GROUP + 1) * TILE, :], w_ref[1], preferred_element_type=f32)
        + jnp.dot(col_ref[2 * TILE : (GROUP + 2) * TILE, :], w_ref[2], preferred_element_type=f32)
    )
    for frame in range(GROUP):
        out_ref[frame, 0:TILE, :] = code_ref[frame]
        out_ref[frame, TILE : 2 * TILE, :] = total[frame * TILE : (frame + 1) * TILE].astype(bf16)
    for side, (offset, col_tap) in enumerate(((0, 2), (STRIP - 1, 0))):
        for frame in range(FRAMES):
            for row in range(ROWS):
                at = frame * TILE + row * STRIP + (0 if side == 0 else STRIP - 8)
                for row_tap in range(3):
                    mid = (row_tap * 3 + 1) * CH
                    piece = col_ref[pl.ds(frame * TILE + row * STRIP, STRIP), pl.ds(mid, CH)]
                    one = piece.astype(f32)[offset : offset + 1]
                    side_ref[pl.ds(frame * ROWS + row, 1), pl.ds(row_tap * CH, CH)] = one
        summed = None
        for frame_tap in range(3):
            rows = side_ref[pl.ds(frame_tap * ROWS, GROUP * ROWS), :].astype(bf16)
            for row_tap in range(3):
                tap = row_tap * 3 + col_tap
                part = jnp.dot(
                    rows[:, row_tap * CH : (row_tap + 1) * CH],
                    w_ref[frame_tap, pl.ds(tap * CH, CH), :],
                    preferred_element_type=f32,
                )
                summed = part if summed is None else summed + part
        if side == 0:
            first = summed
    for frame in range(GROUP):
        pair = [value[frame * ROWS : (frame + 1) * ROWS] for value in (first, summed)]
        out_ref[frame, 2 * TILE : SENT, :] = jnp.concatenate(pair, axis=0).astype(bf16)


def add_body(one_ref, other_ref, out_hbm, sum_ref, sems):
    copies = []
    count = out_hbm.shape[0] // sems.shape[0]
    for chunk in range(sems.shape[0]):
        pieces = pl.ds(chunk * count, count)
        sum_ref[pieces] = (one_ref[pieces].astype(f32) + other_ref[pieces].astype(f32)).astype(bf16)
        copies.append(
            pltpu.make_async_copy(sum_ref.at[pieces], out_hbm.at[pieces], sems.at[chunk])
        )
        copies[-1].start()
    for copy in copies:
        copy.wait()


def part_body(parts_ref, out_ref):
    part = parts_ref[0].astype(f32)
    for peer in range(1, parts_ref.shape[0]):
        part = part + parts_ref[peer].astype(f32)
    part = part.astype(bf16)
    for place in range(out_ref.shape[0]):
        out_ref[place] = part


def share_body(got_ref, out_ref, norm):
    total = got_ref[0].astype(f32)
    for place in range(1, got_ref.shape[0]):
        total = total + got_ref[place].astype(f32)
    copies = (total * norm).astype(bf16)
    for owner in range(out_ref.shape[0]):
        out_ref[owner] = copies


def unpack(got_ref, code_ref, grad_ref):
    at = lax.broadcasted_iota(jnp.int32, (STRIP, CH), 0)
    for strip in range(GROUP):
        columns = pl.ds(strip * STRIP, STRIP)
        if strip > 0:
            before = got_ref[strip - 1, pl.ds(2 * TILE, EDGES), :].astype(f32)
        if strip < GROUP - 1:
            after = got_ref[strip + 1, pl.ds(2 * TILE, EDGES), :].astype(f32)
        for row in range(ROWS):
            code_ref[row, columns, :] = got_ref[strip, pl.ds(row * STRIP, STRIP), :]
            value = got_ref[strip, pl.ds(TILE + row * STRIP, STRIP), :].astype(f32)
            if strip > 0:
                value = value + jnp.where(at == 0, before[ROWS + row : ROWS + row + 1], 0.0)
            if strip < GROUP - 1:
                value = value + jnp.where(at == STRIP - 1, after[row : row + 1], 0.0)
            grad_ref[row, columns, :] = value.astype(bf16)


def finish_body(
    got_ref, terms_ref, code_hbm, grad_hbm, kernel_hbm, code_ref, grad_ref, kernel_ref, sems
):
    copies = []
    chunks = kernel_ref.shape[0]
    part = kernel_ref.shape[1] // CHUNK
    for chunk in range(chunks):
        for place in range(CHUNK):
            rows = terms_ref[chunk * CHUNK + place].astype(f32)
            kernel_ref[chunk, pl.ds(place * part, part), :] = rows[:part]
        copies.append(
            pltpu.make_async_copy(kernel_ref.at[chunk], kernel_hbm.at[chunk], sems.at[chunk])
        )
        copies[-1].start()
    unpack(got_ref, code_ref, grad_ref)
    for at, (ref, hbm) in enumerate(((code_ref, code_hbm), (grad_ref, grad_hbm))):
        copies.append(pltpu.make_async_copy(ref, hbm, sems.at[chunks + at]))
        copies[-1].start()
    for copy in copies:
        copy.wait()


def shifted(value, axes, by):
    count = lax.axis_size(axes)
    route = [(i, i + by) for i in range(count) if 0 <= i + by < count]
    return lax.ppermute(value, axes, route)


def between_chips(value):
    count = lax.axis_size(("z", "core"))
    pairs = [(i, i + 1) for i in range(1, count - 1, 2)]
    return lax.ppermute(value, ("z", "core"), pairs + [(j, i) for i, j in pairs])


def swapped(value):
    return lax.ppermute(value, "core", [(0, 1), (1, 0)])


def shards(frames, kernel, cotangent):
    taps = kernel.reshape(3, WIDE, CH)
    weights = taps
    turned = jnp.swapaxes(kernel[::-1, ::-1, ::-1], 3, 4).reshape(3, WIDE, CH)
    lines = ("z", "core")
    packed = pl.pallas_call(
        pack_body,
        out_shape=jax.ShapeDtypeStruct((GROUP, LOAD, CH), bf16),
        in_specs=[pl.BlockSpec(memory_space=pl.ANY)] * 2,
        scratch_shapes=[pltpu.VMEM((GROUP, ROWS, CH), f32)] * 2
        + [pltpu.SemaphoreType.DMA((2, ROWS))],
    )(frames.reshape(ROWS, GROUP, STRIP, CH), cotangent.reshape(ROWS, GROUP, STRIP, CH))
    held = lax.all_to_all(packed, "y", 0, 0)
    early = shifted(held[GROUP - 2 :, : HELD + 2 * STRIP], "x", 1)

    flops = 2 * GROUP * TILE * 27 * CH * CH
    ahead = kernel_call(
        ahead_body,
        (
            jax.ShapeDtypeStruct((GROUP * TILE, WIDE), bf16),
            jax.ShapeDtypeStruct((GROUP * TILE, CH), f32),
        ),
        flops=flops // 2,
    )(held, weights)
    early, ahead = lax.optimization_barrier((early, tuple(ahead)))

    def edge_rows(*places):
        pieces = [
            jnp.concatenate([early[:, low:high], held[:, low:high]], axis=0)
            for low, high in places
        ]
        return pieces[0] if len(pieces) == 1 else jnp.concatenate(pieces, axis=1)

    core = lax.axis_index("core")
    last = edge_rows((TILE - RIM, HELD + STRIP))
    first = edge_rows((0, RIM), (TILE, HELD), (HELD + STRIP, HELD + 2 * STRIP))
    near = swapped(jnp.where(core == 0, last, first))
    far = between_chips(jnp.where(core == 0, first, last))

    devices = lax.axis_size(("x", "y", "z", "core"))
    peers, wide = lax.axis_size(("x", "z")), lax.axis_size("x")
    share = PART * -(-27 * CH // (2 * PART * peers))
    mail = jax.ShapeDtypeStruct((peers, share, CH), bf16)
    code, g, g_up, g_down, keep, send = kernel_call(
        forward_body,
        (
            jax.ShapeDtypeStruct((GROUP, TILE, CH), bf16),
            jax.ShapeDtypeStruct((GROUP, TILE, CH), bf16),
            jax.ShapeDtypeStruct((GROUP, STRIP, CH), bf16),
            jax.ShapeDtypeStruct((GROUP, STRIP, CH), bf16),
            mail,
            mail,
        ),
        [
            pltpu.VMEM((FRAMES * (TILE + RIM), WIDE), bf16),
            pltpu.VMEM((GROUP * (TILE + RIM), CH), f32),
            pltpu.VMEM((3 * CH, FRAMES * TILE), bf16),
            pltpu.VMEM((2, peers, share, CH), f32),
        ]
        + [pltpu.VMEM((FRAMES, RIM + EDGES + STRIP, CH), bf16)] * 2,
        flops=2 * flops,
        in_specs=[pl.BlockSpec(memory_space=pltpu.SMEM)]
        + [pl.BlockSpec(memory_space=pltpu.VMEM)] * 7,
    )(core.astype(jnp.int32).reshape(1), held, early, near, far, weights, *ahead)

    chip_sum = kernel_call(
        add_body,
        mail,
        [pltpu.VMEM(mail.shape, bf16), pltpu.SemaphoreType.DMA((4,))],
        in_specs=[pl.BlockSpec(memory_space=pltpu.VMEM)] * 2,
        out_specs=pl.BlockSpec(memory_space=pl.ANY),
    )(keep, swapped(send))
    parts = lax.all_to_all(chip_sum, ("x", "z"), 0, 0)
    late = shifted(jnp.concatenate([g_up[:2], g[:2], g_down[:2]], axis=1), "x", -1)
    sent = kernel_call(
        backward_body,
        jax.ShapeDtypeStruct((GROUP, SENT, CH), bf16),
        [
            pltpu.VMEM((FRAMES * TILE, WIDE), bf16),
            pltpu.VMEM((FRAMES * ROWS, 3 * CH), f32),
        ],
        flops=flops,
    )(g, g_up, g_down, late, code, turned)
    parts, sent = lax.optimization_barrier((parts, sent))
    part = kernel_call(part_body, jax.ShapeDtypeStruct((GROUP, share, CH), bf16))(parts)
    norm = 1.0 / math.sqrt(devices * GROUP * TILE)
    copies = kernel_call(
        functools.partial(share_body, norm=norm),
        jax.ShapeDtypeStruct((wide, share, CH), bf16),
    )(lax.all_to_all(part, "y", 0, 0))
    line = lax.all_to_all(copies, "x", 0, 0).reshape(wide * share, CH)
    terms = lax.all_gather(line, lines, tiled=True).reshape(-1, share, CH)

    got = lax.all_to_all(sent, "y", 0, 0)
    whole = (ROWS, GROUP * STRIP, CH)
    part = 27 * CH // terms.shape[0]
    code_out, grad_frames, grad_kernel = pl.pallas_call(
        finish_body,
        out_shape=(
            jax.ShapeDtypeStruct(whole, bf16),
            jax.ShapeDtypeStruct(whole, bf16),
            jax.ShapeDtypeStruct((terms.shape[0] // CHUNK, CHUNK * part, CH), f32),
        ),
        in_specs=[pl.BlockSpec(memory_space=pltpu.VMEM)] * 2,
        out_specs=[pl.BlockSpec(memory_space=pl.ANY)] * 3,
        scratch_shapes=[
            pltpu.VMEM(whole, bf16),
            pltpu.VMEM(whole, bf16),
            pltpu.VMEM((terms.shape[0] // CHUNK, CHUNK * part, CH), f32),
            pltpu.SemaphoreType.DMA((2 + terms.shape[0] // CHUNK,)),
        ],
        compiler_params=pltpu.CompilerParams(vmem_limit_bytes=VMEM_LIMIT),
    )(got, terms)
    return (code_out[None], grad_frames[None], grad_kernel.reshape(3, 3, 3, CH, CH))


def solution(mesh):
    split = Mesh(mesh.devices.reshape(CHIPS), ("x", "y", "z", "core"))
    block = P(("x", "y"), ("z", "core"), None, None)
    return jax.shard_map(
        shards,
        mesh=split,
        in_specs=(block, P(), block),
        out_specs=(block, block, P()),
        check_vma=False,
    )
```
